128 devices in a mesh: dp: 64 (over y, x_hi, z, core), tensor: 2 (over x_lo).
Axes of the slice: x: 4 (x_hi: 2, x_lo: 2; x = x_hi * 2 + x_lo), y: 4, z: 4, core: 2. Of those that a mesh axis runs over, the one named last changes fastest.
Arguments:
- tokens: bfloat16 [32768, 1024], P(('dp', 'tensor')), may hold values from -6 to 6
- gain_attn: float32 [1024], replicated, may hold values from 0.5 to 1.5
- w_query: bfloat16 [1024, 1024], P('dp', 'tensor'), may hold values from -0.25 to 0.25
- w_key: bfloat16 [1024, 1024], P('dp', 'tensor'), may hold values from -0.25 to 0.25
- w_value: bfloat16 [1024, 1024], P('dp', 'tensor'), may hold values from -0.1875 to 0.1875
- w_out: bfloat16 [1024, 1024], P('tensor', 'dp'), may hold values from -1.5 to 1.5
- gain_moe: float32 [1024], replicated, may hold values from 0.5 to 1.5
- w_gate: bfloat16 [32, 1024, 512], P(None, 'dp', 'tensor'), may hold values from -0.1875 to 0.1875
- w_up: bfloat16 [32, 1024, 512], P(None, 'dp', 'tensor'), may hold values from -0.1875 to 0.1875
- w_down: bfloat16 [32, 512, 1024], P(None, 'tensor', 'dp'), may hold values from -1 to 1
- routes: int32 [32768, 8], P('dp'), may hold values from 0 to 31, all different within a row; in each aligned block of 512 rows (0 to 511, 512 to 1023, ...) at most 160 rows name the same one
- route_weights: float32 [32768, 8], P('dp'), may hold values from 0.06 to 0.25
- cotangent: bfloat16 [32768, 1024], P(('dp', 'tensor')), may hold values from -6 to 6
Outputs:
- output: bfloat16 [32768, 1024], P(('dp', 'tensor'))
- grad_tokens: bfloat16 [32768, 1024], P(('dp', 'tensor'))
- grad_gain_attn: float32 [1024], replicated
- grad_query: float32 [1024, 1024], P('dp', 'tensor')
- grad_key: float32 [1024, 1024], P('dp', 'tensor')
- grad_value: float32 [1024, 1024], P('dp', 'tensor')
- grad_out: float32 [1024, 1024], P('tensor', 'dp')
- grad_gain_moe: float32 [1024], replicated
- grad_gate: float32 [32, 1024, 512], P(None, 'dp', 'tensor')
- grad_up: float32 [32, 1024, 512], P(None, 'dp', 'tensor')
- grad_down: float32 [32, 512, 1024], P(None, 'tensor', 'dp')
The draws below stay inside these ranges and needn't reach their ends.
Inputs may be any that keep to these rules, and one draw needn't show every extreme that they name: `routes`: each token names 8 different experts. Among the 512 tokens of one sequence no expert is named by more than 160 tokens, and in every draw some expert is named by exactly 160.
All inputs are finite; a program needn't handle non-finite values.
Results may differ from the reference program's by a relative error of at most 0.02.
Values may be sent and summed in bfloat16 or wider, within the bound.
No kernel may reach another device: no remote copies, remote signals or barrier semaphores. Data moves between devices by JAX's collectives and lax.ppermute only.
A program may use at most 320 MiB of HBM per device.

```python
import math
import jax
import jax.numpy as jnp
import numpy as np
from jax import lax

D = 1024
HQ = 16
HD = 64
FF = 512
TOP = 8
E = 32
SEQ = 512
CAP = 160
TOKENS = 32768
N_DP = 64


def block_scale(own_key, extent, split, least, high):
    level = 1.0
    for position, parts in split:
        heights = jax.random.uniform(jax.random.fold_in(jax.random.fold_in(own_key, 6), position), (parts,), jnp.float32, least / len(split), high / len(split))
        level = level * jnp.repeat(jnp.exp(heights), extent[position] // parts).reshape((-1,) + (1,) * (len(extent) - 1 - position))
    return level


def routed_block(rng, own, number, rows, number_of, top, limit, slope):
    sequence = jax.random.permutation(rng, number_of)
    packed, usual = portions_of(number_of, rows * top, limit, slope, True), portions_of(number_of, rows * top, limit, slope, False)
    places = jnp.arange(number_of)

    def named(lengths, offset_by):
        used = int((lengths > 0).sum())
        fixed = max(1, used // 4)
        passed = fixed + (places - fixed + offset_by * (used - fixed)) % max(1, number_of - fixed)
        return jnp.zeros((number_of,), jnp.int32).at[sequence[jnp.where(places < fixed, places, passed)]].set(jnp.asarray(lengths, jnp.int32))

    lengths = jnp.where(number % 4 == 0, named(packed, number // 4), named(usual, number - number // 4 - 1))
    mixed = jax.random.permutation(jax.random.fold_in(own, 3), number_of)
    donor, receiver = mixed[0:number_of // 2 * 2:2], mixed[1:number_of // 2 * 2:2]
    room = jnp.minimum(lengths[donor] - 1, limit - lengths[receiver]) // 2
    room = jnp.where((donor == sequence[0]) | (receiver == sequence[0]) | (lengths[receiver] == 0), 0, jnp.maximum(room, 0))
    passed = jax.random.randint(jax.random.fold_in(own, 4), (number_of // 2,), 0, 1 << 20) % (room + 1)
    lengths = lengths.at[donor].add(-passed).at[receiver].add(passed)
    members = jnp.searchsorted(jnp.cumsum(lengths), jnp.arange(rows * top), side="right").astype(jnp.int32)
    table = members.reshape(top, rows).T
    table = table[jax.random.permutation(jax.random.fold_in(own, 1), rows)]
    offset_by = jax.random.randint(jax.random.fold_in(own, 2), (rows, 1), 0, top)
    return jnp.take_along_axis(table, (jnp.arange(top)[None, :] + offset_by) % top, axis=1)


def portions_of(number_of, total, reach, slope, full):
    loads = [(1 << 20) // math.isqrt(rank ** slope) + 1 for rank in range(1, number_of + 1)]
    largest = reach if full else min(reach, max(-(-total // number_of), total * loads[0] // sum(loads)))
    least = 1 if total - largest >= number_of - 1 else 0
    counts, spare = [largest] + [least] * (number_of - 1), total - largest - least * (number_of - 1)
    while spare > 0:
        candidates = [i for i in range(1, number_of) if counts[i] < largest] or [i for i in range(1, number_of) if counts[i] < reach]
        pool, left = sum([loads[i] for i in candidates]), spare
        for i in candidates:
            more = min(reach - counts[i], max(1, left * loads[i] // pool), spare)
            counts[i] = counts[i] + more
            spare = spare - more
    return np.array(counts)


def gaussian(stream_key, extent, spread, limit, cuts=(), kind=jnp.bfloat16):
    array = spread * jax.random.normal(stream_key, extent, jnp.float32)
    if cuts:
        array = array * block_scale(stream_key, extent, cuts, -0.22, 0.18)
    return jnp.clip(array, -limit, limit).astype(kind)


def setup_inputs(seed: int = 0) -> dict:
    key_of = jax.random.split(jax.random.key(seed), 14)
    tokens = gaussian(key_of[0], (TOKENS, D), 1.0, 6.0, ((0, 128),))
    gain_attn = jnp.clip(1.0 + 0.1 * jax.random.normal(key_of[1], (D,), jnp.float32), 0.5, 1.5)
    w_query = gaussian(key_of[2], (D, HQ * HD), (D // 2) ** -0.5, 0.25, ((0, 64), (1, 2)))
    w_key = gaussian(key_of[3], (D, HQ * HD), (D // 2) ** -0.5, 0.25, ((0, 64), (1, 2)))
    w_value = gaussian(key_of[4], (D, HQ * HD), D ** -0.5, 0.1875, ((0, 64), (1, 2)))
    w_out = gaussian(key_of[5], (HQ * HD, D), (HQ * HD // 64) ** -0.5, 1.5, ((0, 2), (1, 64)))
    gain_moe = jnp.clip(1.0 + 0.1 * jax.random.normal(key_of[6], (D,), jnp.float32), 0.5, 1.5)
    w_gate = gaussian(key_of[7], (E, D, FF), D ** -0.5, 0.1875, ((1, 64), (2, 2)))
    w_up = gaussian(key_of[8], (E, D, FF), D ** -0.5, 0.1875, ((1, 64), (2, 2)))
    w_down = gaussian(key_of[9], (E, FF, D), (FF // 16) ** -0.5, 1.0, ((1, 2), (2, 64)))
    routes_keys = jax.random.split(jax.random.fold_in(key_of[10], 1), TOKENS // SEQ)
    routes_turns = jax.random.permutation(jax.random.fold_in(key_of[10], 3), TOKENS // SEQ)
    routes = jax.vmap(lambda own, number: routed_block(jax.random.fold_in(key_of[10], 2), own, number, SEQ, E, TOP, CAP, 1))(routes_keys, routes_turns).reshape((TOKENS, TOP))
    route_weights = jnp.clip(jnp.exp(math.log(0.25) - 1.4271164 * jax.random.uniform(key_of[11], (TOKENS, TOP), jnp.float32) ** block_scale(key_of[11], (TOKENS, TOP), ((0, 64),), -0.2, 0.2)), 0.06, 0.25)
    cotangent = gaussian(key_of[12], (TOKENS, D), 1.0, 6.0, ((0, 128),))
    return {"tokens": tokens, "gain_attn": gain_attn, "w_query": w_query, "w_key": w_key, "w_value": w_value, "w_out": w_out, "gain_moe": gain_moe, "w_gate": w_gate, "w_up": w_up, "w_down": w_down, "routes": routes, "route_weights": route_weights, "cotangent": cotangent}


@jax.custom_vjp
def low(v):
    return lax.optimization_barrier(v.astype(jnp.bfloat16)).astype(jnp.float32)

@jax.custom_vjp
def low_back(v):
    return v

def low_keep(v):
    return (low(v), None)

def low_pass(kept, grad):
    return (grad,)

def back_keep(v):
    return (v, None)

def back_low(kept, grad):
    return (low(grad),)
low.defvjp(low_keep, low_pass)
low_back.defvjp(back_keep, back_low)
EPSILON = 1e-06
THETA = 10000.0
HIGHEST = lax.Precision.HIGHEST

def rotary_tables(length, head_size):
    half_size = head_size // 2
    frequency = THETA ** (-2.0 * jnp.arange(half_size, dtype=jnp.float32) / head_size)
    angles = jnp.arange(length, dtype=jnp.float32)[:, None] * frequency[None, :]
    return (jnp.cos(angles)[:, None, :], jnp.sin(angles)[:, None, :])

def rotate(heads, cosine_table, sine_table):
    half_size = heads.shape[-1] // 2
    first_half = heads[..., :half_size]
    second_half = heads[..., half_size:]
    return jnp.concatenate([first_half * cosine_table - second_half * sine_table, second_half * cosine_table + first_half * sine_table], -1)

def rms_scale(rows):
    return lax.rsqrt(lax.optimization_barrier(jnp.mean(rows * rows, -1, keepdims=True)) + EPSILON)

def layer(resid_in, params, route_ids, route_share):
    gain_attn, w_query, w_key, w_value, w_out, gain_moe, w_gate, w_up, w_down = params
    length = resid_in.shape[0]
    cosine_table, sine_table = rotary_tables(length, HD)
    normed = low(resid_in * rms_scale(resid_in) * gain_attn)
    query_proj = low_back(jnp.dot(normed, w_query, precision=HIGHEST)).reshape(length, HQ, HD)
    queries = low(rotate(query_proj, cosine_table, sine_table))
    key_proj = low_back(jnp.dot(normed, w_key, precision=HIGHEST)).reshape(length, HQ, HD)
    key_heads = low(rotate(key_proj, cosine_table, sine_table))
    value_heads = low(low_back(jnp.dot(normed, w_value, precision=HIGHEST))).reshape(length, HQ, HD)
    scores = low_back(jnp.einsum('qhd,khd->hqk', queries, key_heads, precision=HIGHEST) * HD ** (-0.5))
    row_max = lax.optimization_barrier(jnp.max(scores, -1, keepdims=True))
    exponent = jnp.exp(scores - row_max)
    softmax_w = low(exponent / lax.optimization_barrier(jnp.sum(exponent, -1, keepdims=True)))
    mixed = jnp.einsum('hqk,khd->qhd', softmax_w, value_heads, precision=HIGHEST).reshape(length, HQ * HD)
    mixed = low(low_back(mixed))
    hidden = resid_in + low_back(jnp.dot(mixed, w_out, precision=HIGHEST))
    normed_moe = low(hidden * rms_scale(hidden) * gain_moe)
    gate_act = low_back(jnp.einsum('ld,edf->elf', normed_moe, w_gate, precision=HIGHEST))
    up_act = low_back(jnp.einsum('ld,edf->elf', normed_moe, w_up, precision=HIGHEST))
    hidden_units = low(jax.nn.silu(gate_act) * up_act)
    expert_out = low_back(jnp.einsum('elf,efd->eld', hidden_units, w_down, precision=HIGHEST))
    chosen = (route_ids[:, :, None] == jnp.arange(E, dtype=jnp.int32)[None, None, :]).astype(jnp.float32)
    combine = lax.optimization_barrier(jnp.sum(chosen * route_share[:, :, None], 1))
    return hidden + jnp.einsum('le,eld->ld', combine, expert_out, precision=HIGHEST)

def reference(tokens, gain_attn, w_query, w_key, w_value, w_out, gain_moe, w_gate, w_up, w_down, routes, route_weights, cotangent):
    params = tuple((weight.astype(jnp.float32) for weight in (gain_attn, w_query, w_key, w_value, w_out, gain_moe, w_gate, w_up, w_down)))
    sequences = tokens.astype(jnp.float32).reshape(N_DP, SEQ, D)
    gradients_in = cotangent.astype(jnp.float32).reshape(N_DP, SEQ, D)
    routes_seq = routes.reshape(N_DP, SEQ, TOP)
    shares_seq = route_weights.reshape(N_DP, SEQ, TOP)

    def advance(totals, pieces):
        resid_in, route_ids, route_share, grad_result = pieces

        def forward(inputs, weights):
            return layer(inputs, weights, route_ids, route_share)
        result, pullback = jax.vjp(forward, resid_in, params)
        grad_in, grad_params = pullback(grad_result)
        return (jax.tree.map(jnp.add, totals, grad_params), (result, grad_in))
    zero_grads = tuple((jnp.zeros_like(weight) for weight in params))
    totals, outputs = lax.scan(advance, zero_grads, (sequences, routes_seq, shares_seq, gradients_in))
    results, grads_in = outputs
    return (results.reshape(N_DP * SEQ, D).astype(jnp.bfloat16), grads_in.reshape(N_DP * SEQ, D).astype(jnp.bfloat16), totals[0], totals[1], totals[2], totals[3], totals[4], totals[5], totals[6], totals[7], totals[8])
```

```python
import jax
import jax.numpy as jnp
from jax import lax
from jax.experimental import pallas as pl
from jax.experimental.pallas import tpu as pltpu
from jax.sharding import Mesh
from jax.sharding import PartitionSpec as P

HD = 64
CAP = 160
EPSILON = 1e-06
THETA = 10000.0
LOCAL_E = 4
F32 = jnp.float32
BF16 = jnp.bfloat16
VMEM_BYTES = 60 * 1024 * 1024


def swap_x(value, bits):
    return lax.ppermute(value, ("xh", "xl"), [(i, i ^ bits) for i in range(4)])


def swap_c(value):
    return lax.ppermute(value, "c", [(0, 1), (1, 0)])


def swap_4(value, axis, bits):
    return lax.ppermute(value, axis, [(i, i ^ bits) for i in range(4)])


def flip(value, axis, bit):
    return jnp.where(bit == 1, jnp.flip(value, axis), value)


def gather_group(value, order=(2, 3, 1)):
    pieces = {(0, 0): value, (1, 0): swap_c(value)}
    for x in order:
        pieces[0, x] = swap_x(value, x)
        pieces[1, x] = swap_c(pieces[0, x])
    return pieces


def exchange_group(near, far):
    other = swap_c(far)
    both = [jnp.stack([near[x], other[x]]) for x in range(4)]
    return [both[0]] + [swap_x(both[x], x) for x in (1, 2, 3)]


def scatter_group(near, far):
    other = swap_c(far)
    sums = [(near[x].astype(F32) + other[x].astype(F32)).astype(BF16) for x in range(4)]
    return [sums[0]] + [swap_x(sums[x], x) for x in (2, 3, 1)]


def dot(a, b, ca, cb):
    return lax.dot_general(a, b, (((ca,), (cb,)), ((), ())), preferred_element_type=F32)


def whole(n):
    return [pl.BlockSpec(memory_space=pltpu.VMEM)] * n


def kernel_call(body, ins, outs, name, scratch=(), smem=0):
    specs = [pl.BlockSpec(memory_space=pltpu.SMEM)] * smem + whole(len(ins) - smem)
    return pl.pallas_call(
        body,
        out_shape=outs,
        in_specs=specs,
        out_specs=whole(len(outs)),
        scratch_shapes=list(scratch),
        compiler_params=pltpu.CompilerParams(vmem_limit_bytes=VMEM_BYTES),
        name=name,
    )(*ins)


def shape(*dims, dtype=BF16):
    return jax.ShapeDtypeStruct(dims, dtype)


def assemble_body(ids, p0, p1, p2, p3, qkv_ref, out_ref):
    for y, piece in enumerate((p0, p1, p2, p3)):
        for z in range(4):
            for xh in range(2):
                row = ((y ^ ids[0]) * 8 + xh * 4 + (z ^ ids[1])) * 32
                rows = pl.ds(pl.multiple_of(row, 32), 32)
                part = piece[z, xh * 32 : xh * 32 + 32, :]
                qkv_ref[rows, :] = part[:, :384]
                out_ref[rows, :] = part[:, 384:]


def rotated(v, cos, sin):
    lane = lax.broadcasted_iota(jnp.int32, v.shape, 1)
    other = jnp.where(lane % HD < HD // 2, pltpu.roll(v, 96, 1), pltpu.roll(v, 32, 1))
    return v * cos + other * sin


def attend_body(*refs):
    token_refs = refs[:8]
    gain, w_qkv, cos_ref, sin_ref = refs[8:12]
    n1_ref, qkv_ref, near_ref, far_ref = refs[12:]
    cos, sin = cos_ref[...], sin_ref[...]
    for s in range(4):
        for half in range(2):
            x = token_refs[2 * s + half][...].astype(F32)
            r1 = lax.rsqrt(jnp.mean(x * x, -1, keepdims=True) + EPSILON)
            n1_ref[s, half * 256 : half * 256 + 256, :] = (x * r1 * gain[...]).astype(BF16)
        proj = jnp.dot(n1_ref[s], w_qkv[...], preferred_element_type=F32)
        q = rotated(proj[:, :128], cos, sin).astype(BF16)
        k = rotated(proj[:, 128:256], cos, sin).astype(BF16)
        v = proj[:, 256:].astype(BF16)
        qkv_ref[s, :, :128] = q
        qkv_ref[s, :, 128:256] = k
        qkv_ref[s, :, 256:] = v
        mixed = []
        for h in range(2):
            cols = slice(h * HD, h * HD + HD)
            scores = dot(q[:, cols], k[:, cols], 1, 1) * (HD**-0.5)
            e = jnp.exp(scores - jnp.max(scores, -1, keepdims=True))
            p = (e / jnp.sum(e, -1, keepdims=True)).astype(BF16)
            mixed.append(dot(p, v[:, cols], 1, 0).astype(BF16))
        out = jnp.concatenate(mixed, 1)
        dst = near_ref if s < 2 else far_ref
        dst[2 * (s % 2)] = out[:256]
        dst[2 * (s % 2) + 1] = out[256:]


def project_body(*refs):
    tokens, gain = refs[:2]
    mixed = refs[2:6]
    weights = refs[6:14]
    hidden_ref, n2_ref, mixed_ref, wo_ref = refs[14:]
    for c in range(2):
        for x in range(4):
            k = c * 4 + x
            mixed_ref[:, k * 128 : k * 128 + 128] = mixed[x][c]
            wo_ref[:, k * 128 : k * 128 + 128] = weights[k][...]
    hidden = tokens[...].astype(F32) + dot(mixed_ref[...], wo_ref[...], 1, 1)
    hidden_ref[...] = hidden
    r2 = lax.rsqrt(jnp.mean(hidden * hidden, -1, keepdims=True) + EPSILON)
    n2_ref[...] = (hidden * r2 * gain[...]).astype(BF16)


def expert_pieces():
    for y in range(4):
        for z in range(4):
            for c in range(2):
                for xh in range(2):
                    for xl in range(2):
                        row = y * 256 + xh * 128 + z * 32 + c * 16
                        yield y * 4 + z, c * 4 + xh * 2 + xl, slice(row, row + 16), slice(
                            xl * 256, xl * 256 + 256
                        )


def expert_body(*refs):
    n2 = refs[:8]
    ct = refs[8:16]
    rank_ref, share_ref, w_ref = refs[16:19]
    z_near, z_far, g_near, g_far, dw_ref = refs[19:24]
    wg, wu, wd, x_s, gz_s, p_s, z_s, gx_s = refs[24:]
    e = pl.program_id(0)
    rows = 4 * CAP
    for piece, source, d, f in expert_pieces():
        wg[d, f] = w_ref[piece, source, 0, 0]
        wu[d, f] = w_ref[piece, source, 1, 0]
        wd[d, f] = w_ref[piece, source, 2, 0]
    shares = []
    slot = lax.broadcasted_iota(jnp.int32, (CAP, 512), 0)
    for s in range(4):
        hit = slot == rank_ref[0, s : s + 1, :]
        share = jnp.sum(jnp.where(hit, share_ref[0, s : s + 1, :], 0.0), 1, keepdims=True)
        shares.append(share)
        p = hit.astype(F32).astype(BF16)
        p_s[s, pl.ds(pl.multiple_of(e * CAP, 32), CAP), :] = p
        here = slice(s * CAP, s * CAP + CAP)
        x_s[here, :] = (
            dot(p[:, :256], n2[2 * s][...], 1, 0) + dot(p[:, 256:], n2[2 * s + 1][...], 1, 0)
        ).astype(BF16)
        gz_s[here, :] = (
            (dot(p[:, :256], ct[2 * s][...], 1, 0) + dot(p[:, 256:], ct[2 * s + 1][...], 1, 0))
            * share
        ).astype(BF16)
    share = jnp.concatenate(shares, 0)
    a = dot(x_s[...], wg[...], 1, 0)
    b = dot(x_s[...], wu[...], 1, 0)
    sig = 1.0 / (1.0 + jnp.exp(-a))
    sa = a * sig
    u = (sa * b).astype(BF16)
    gu = dot(gz_s[...], wd[...], 1, 0)
    ga = (gu * b * sig * (1.0 + a * (1.0 - sig))).astype(BF16)
    gb = (gu * sa).astype(BF16)
    z = (dot(u, wd[...], 1, 1) * share).astype(BF16)
    gx = (dot(ga, wg[...], 1, 1) + dot(gb, wu[...], 1, 1)).astype(BF16)
    for s in range(4):
        here = slice(s * CAP, s * CAP + CAP)
        there = pl.ds(pl.multiple_of(e * CAP, 32), CAP)
        z_s[s, there, :] = z[here]
        gx_s[s, there, :] = gx[here]
    for m, term in enumerate((dot(x_s[...], ga, 0, 0), dot(x_s[...], gb, 0, 0), dot(gz_s[...], u, 0, 0))):
        term = term.astype(BF16)
        for piece, source, d, f in expert_pieces():
            dw_ref[piece, source, m, 0] = term[d, f]

    @pl.when(e == LOCAL_E - 1)
    def _():
        for s in range(4):
            for src, near, far in ((z_s, z_near, z_far), (gx_s, g_near, g_far)):
                total = dot(p_s[s], src[s], 0, 0).astype(BF16)
                dst = near if s < 2 else far
                dst[2 * (s % 2)] = total[:256]
                dst[2 * (s % 2) + 1] = total[256:]


def run_experts(n2, ct, rank, share, weights):
    block = (16, 8, 3, 1, 16, 256)
    w_spec = pl.BlockSpec(block, lambda e: (0, 0, 0, e, 0, 0))
    table = pl.BlockSpec((1, 4, 512), lambda e: (e, 0, 0))
    blocks = shape(4, 256, 1024)
    return pl.pallas_call(
        expert_body,
        grid=(LOCAL_E,),
        out_shape=(blocks,) * 4 + (shape(16, 8, 3, LOCAL_E, 16, 256),),
        in_specs=whole(16) + [table, table, w_spec],
        out_specs=whole(4) + [w_spec],
        scratch_shapes=[
            pltpu.VMEM((1024, 512), BF16),
            pltpu.VMEM((1024, 512), BF16),
            pltpu.VMEM((1024, 512), BF16),
            pltpu.VMEM((4 * CAP, 1024), BF16),
            pltpu.VMEM((4 * CAP, 1024), BF16),
            pltpu.VMEM((4, LOCAL_E * CAP, 512), BF16),
            pltpu.VMEM((4, LOCAL_E * CAP, 1024), BF16),
            pltpu.VMEM((4, LOCAL_E * CAP, 1024), BF16),
        ],
        compiler_params=pltpu.CompilerParams(vmem_limit_bytes=VMEM_BYTES),
        name="experts",
    )(*n2, *ct, rank, share, weights)


def hidden_back_body(g0, g1, g2, g3, hidden_ref, ct, gain, wo, gh_ref, ghb_ref, near_ref, far_ref, dgain_ref):
    gn2 = g0[...].astype(F32) + g1[...].astype(F32) + g2[...].astype(F32) + g3[...].astype(F32)
    hidden = hidden_ref[...]
    r2 = lax.rsqrt(jnp.mean(hidden * hidden, -1, keepdims=True) + EPSILON)
    w2 = gn2 * gain[...]
    gh = ct[...].astype(F32) + r2 * w2 - hidden * (r2 * r2 * r2) * jnp.mean(w2 * hidden, -1, keepdims=True)
    gh_ref[...] = gh
    ghb = gh.astype(BF16)
    ghb_ref[...] = ghb
    gm = dot(ghb, wo[...], 1, 0).astype(BF16)
    for x in range(4):
        near_ref[x] = gm[:, x * 128 : x * 128 + 128]
        far_ref[x] = gm[:, 512 + x * 128 : 512 + x * 128 + 128]
    dgain_ref[...] = jnp.sum(gn2 * hidden * r2, 0, keepdims=True)


def out_grad_body(ghb, mixed, near_ref, far_ref):
    term = dot(ghb[...], mixed[...], 0, 0).astype(BF16)
    for x in range(4):
        near_ref[x] = term[:, x * 128 : x * 128 + 128]
        far_ref[x] = term[:, 512 + x * 128 : 512 + x * 128 + 128]


def attend_back_body(qkv, m0, m1, m2, m3, cos_ref, sin_ref, near_ref, far_ref):
    gm_refs = (m0, m1, m2, m3)
    cos, sin = cos_ref[...], -sin_ref[...]
    for s in range(4):
        c, x = s // 2, 2 * (s % 2)
        gm = jnp.concatenate([gm_refs[x][c], gm_refs[x + 1][c]], 0)
        gqs, gks, gvs = [], [], []
        for h in range(2):
            q = qkv[s, :, h * HD : h * HD + HD]
            k = qkv[s, :, 128 + h * HD : 128 + h * HD + HD]
            v = qkv[s, :, 256 + h * HD : 256 + h * HD + HD]
            gmh = gm[:, h * HD : h * HD + HD]
            scores = dot(q, k, 1, 1) * (HD**-0.5)
            e = jnp.exp(scores - jnp.max(scores, -1, keepdims=True))
            p = e / jnp.sum(e, -1, keepdims=True)
            gp = dot(gmh, v, 1, 1)
            gs = (p * (gp - jnp.sum(gp * p, -1, keepdims=True))).astype(BF16)
            gqs.append(dot(gs, k, 1, 0) * (HD**-0.5))
            gks.append(dot(gs, q, 0, 0) * (HD**-0.5))
            gvs.append(dot(p.astype(BF16), gmh, 0, 0))
        gq = rotated(jnp.concatenate(gqs, 1), cos, sin).astype(BF16)
        gk = rotated(jnp.concatenate(gks, 1), cos, sin).astype(BF16)
        gv = jnp.concatenate(gvs, 1).astype(BF16)
        dst = near_ref if s < 2 else far_ref
        for j, g in enumerate((gq, gk, gv)):
            dst[x, :, j * 128 : j * 128 + 128] = g[:256]
            dst[x + 1, :, j * 128 : j * 128 + 128] = g[256:]


def attend_grad_body(ids, n1, near, far, w_qkv, gain, pieces_ref, dgain_ref, total):
    for s in range(4):
        src = near if s < 2 else far
        x = 2 * (s % 2)
        term = dot(n1[s, :256], src[x], 0, 0) + dot(n1[s, 256:], src[x + 1], 0, 0)
        total[...] = term if s == 0 else total[...] + term
    weighted = total[...] * w_qkv[...].astype(F32)
    ones = jnp.ones((8, 384), F32)
    sums = lax.dot_general(
        ones,
        weighted,
        (((1,), (1,)), ((), ())),
        precision=lax.Precision.HIGHEST,
        preferred_element_type=F32,
    )
    dgain_ref[...] = sums[:1] / gain[...]
    for y in range(4):
        for z in range(4):
            for xh in range(2):
                row = ((y ^ ids[0]) * 8 + xh * 4 + (z ^ ids[1])) * 32
                part = total[pl.ds(pl.multiple_of(row, 32), 32), :]
                pieces_ref[y, z, xh * 32 : xh * 32 + 32, :] = part.astype(BF16)


def arrange_body(ids, w0, w1, w2, w3, pieces_ref, total):
    total[...] = sum(w[...].astype(F32) for w in (w0, w1, w2, w3))
    for y in range(4):
        for z in range(4):
            for xh in range(2):
                row = ((y ^ ids[0]) * 8 + xh * 4 + (z ^ ids[1])) * 32
                part = total[pl.ds(pl.multiple_of(row, 32), 32), :]
                pieces_ref[y, z, xh * 32 : xh * 32 + 32, :] = part.astype(BF16)


def tokens_back_body(*refs):
    g = refs[:4]
    weights = refs[4:12]
    tokens, gain, gh, out_ref = refs[12:]
    gn1 = jnp.zeros((256, 1024), F32)
    for c in range(2):
        for x in range(4):
            gn1 = gn1 + dot(g[x][c], weights[c * 4 + x][...], 1, 1)
    x = tokens[...].astype(F32)
    r1 = lax.rsqrt(jnp.mean(x * x, -1, keepdims=True) + EPSILON)
    w1 = gn1 * gain[...]
    out_ref[...] = (
        gh[...] + r1 * w1 - x * (r1 * r1 * r1) * jnp.mean(w1 * x, -1, keepdims=True)
    ).astype(BF16)


def pieces_in_order(pieces):
    return [pieces[c, x] for c in range(2) for x in range(4)]


def route_tables(routes, route_weights, c, xh, xl):
    table = jnp.concatenate([routes.T.astype(F32), route_weights.T], 0)
    other = swap_c(table)
    tables = jnp.stack([table, swap_x(table, 2), other, swap_x(other, 2)])
    tables = flip(tables.reshape(4, 16, 2, 256), 2, xl).reshape(4, 16, 512)
    first = ((c * 4 + xh * 2 + xl) * LOCAL_E).astype(F32)
    names = first + jnp.arange(LOCAL_E, dtype=F32)
    match = tables[None, :, :8, :] == names[:, None, None, None]
    share = jnp.sum(jnp.where(match, tables[None, :, 8:, :], 0.0), 2)
    named = jnp.any(match, 2)
    before = (jnp.arange(512)[:, None] <= jnp.arange(512)[None, :]).astype(BF16)
    count = jnp.dot(named.astype(BF16), before, preferred_element_type=F32)
    rank = jnp.where(named, count.astype(jnp.int32) - 1, -1)
    return rank, share


def all_sum(value):
    value = value.reshape(8, 128)
    value = value + swap_c(value)
    value = value + (swap_x(value, 1) + swap_x(value, 2) + swap_x(value, 3))
    for axis in ("y", "z"):
        value = value + (swap_4(value, axis, 1) + swap_4(value, axis, 2) + swap_4(value, axis, 3))
    return value.reshape(1024)


def on_device(
    tokens,
    gain_attn,
    w_query,
    w_key,
    w_value,
    w_out,
    gain_moe,
    w_gate,
    w_up,
    w_down,
    routes,
    route_weights,
    cotangent,
):
    y, xh, z, c, xl = (lax.axis_index(a) for a in ("y", "xh", "z", "c", "xl"))
    ids = jnp.stack([y, z]).astype(jnp.int32)
    gain_attn = gain_attn.reshape(1, 1024)
    gain_moe = gain_moe.reshape(1, 1024)

    mine = jnp.stack([w_query, w_key, w_value, w_out.T], 1)
    mine = mine.reshape(16, 4, 2, 2, 128).transpose(2, 3, 0, 1, 4)
    mine = flip(flip(mine, 0, xh), 1, c).reshape(2, 2, 16, 512)
    got = jnp.stack([mine[0, 0], swap_c(mine[0, 1]), swap_x(mine[1, 0], 2), swap_x(swap_c(mine[1, 1]), 2)])
    got = flip(flip(got.reshape(2, 2, 16, 512), 0, xh), 1, c).reshape(64, 512)
    zs = jnp.stack([got] + [swap_4(got, "z", k) for k in (1, 2, 3)])
    ys = [zs] + [swap_4(zs, "y", k) for k in (1, 2, 3)]
    w_qkv, w_o = kernel_call(
        assemble_body, [ids, *ys], (shape(1024, 384), shape(1024, 128)), "assemble", smem=1
    )

    blocks = gather_group(tokens)

    local = jnp.stack([w_gate, w_up, jnp.swapaxes(w_down, 1, 2)])
    local = local.reshape(3, 8, LOCAL_E, 16, 256).swapaxes(0, 1)
    owned = lax.all_to_all(local, ("c", "xh", "xl"), 0, 0, tiled=True)
    experts = lax.all_gather(owned, ("y", "z"), axis=0)

    rank, share = route_tables(routes, route_weights, c, xh, xl)

    half = HD // 2
    frequency = THETA ** (-2.0 * jnp.arange(half, dtype=F32) / HD)
    place = jnp.arange(512)
    place = ((place // 256) ^ xl) * 256 + place % 256
    angles = place.astype(F32)[:, None] * frequency[None, :]
    cos, sin = jnp.cos(angles), jnp.sin(angles)
    cos = jnp.concatenate([cos] * 4, 1)
    sin = jnp.concatenate([-sin, sin, -sin, sin], 1)

    n1, qkv, near, far = kernel_call(
        attend_body,
        [*pieces_in_order(blocks), gain_attn, w_qkv, cos, sin],
        (shape(4, 512, 1024), shape(4, 512, 384), shape(4, 256, 128), shape(4, 256, 128)),
        "attend",
    )
    w_o_all = pieces_in_order(gather_group(w_o))
    mixed = exchange_group(near, far)
    hidden, n2, mixed, w_o_full = kernel_call(
        project_body,
        [tokens, gain_moe, *mixed, *w_o_all],
        (shape(256, 1024, dtype=F32), shape(256, 1024), shape(256, 1024), shape(1024, 1024)),
        "project",
    )
    n2_all = gather_group(n2)
    cot_all = gather_group(cotangent)
    z_near, z_far, g_near, g_far, grads = run_experts(
        pieces_in_order(n2_all), pieces_in_order(cot_all), rank, share, experts
    )
    reduced = lax.psum_scatter(grads, ("y", "z"), scatter_dimension=0)
    gn2 = scatter_group(g_near, g_far)
    gh, ghb, near, far, dgain_moe = kernel_call(
        hidden_back_body,
        [*gn2, hidden, cotangent, gain_moe, w_o_full],
        (
            shape(256, 1024, dtype=F32),
            shape(256, 1024),
            shape(4, 256, 128),
            shape(4, 256, 128),
            shape(1, 1024, dtype=F32),
        ),
        "hidden_back",
    )
    gm = exchange_group(near, far)
    near, far = kernel_call(
        attend_back_body,
        [qkv, *gm, cos, sin],
        (shape(4, 256, 384), shape(4, 256, 384)),
        "attend_back",
    )
    w_qkv_all = pieces_in_order(gather_group(w_qkv))
    g = exchange_group(near, far)
    grad_tokens = kernel_call(
        tokens_back_body,
        [*g, *w_qkv_all, tokens, gain_attn, gh],
        (shape(256, 1024),),
        "tokens_back",
    )[0]
    qkv_pieces, dgain_attn = kernel_call(
        attend_grad_body,
        [ids, n1, near, far, w_qkv, gain_attn],
        (shape(4, 4, 64, 384), shape(1, 1024, dtype=F32)),
        "attend_grad",
        scratch=[pltpu.VMEM((1024, 384), F32)],
        smem=1,
    )
    near, far = kernel_call(
        out_grad_body, [ghb, mixed], (shape(4, 1024, 128), shape(4, 1024, 128)), "out_grad"
    )
    out_pieces = kernel_call(
        arrange_body,
        [ids, *scatter_group(near, far)],
        (shape(4, 4, 64, 128),),
        "arrange",
        scratch=[pltpu.VMEM((1024, 128), F32)],
        smem=1,
    )[0]
    pieces = jnp.concatenate([qkv_pieces, out_pieces], 3)
    sums = sum([pieces[0].astype(F32)] + [swap_4(pieces[k], "y", k).astype(F32) for k in (1, 2, 3)])
    sums = sums.astype(BF16)
    sums = sum([sums[0].astype(F32)] + [swap_4(sums[k], "z", k).astype(F32) for k in (1, 2, 3)])
    back = flip(flip(sums.reshape(2, 2, 16, 512), 0, xh), 1, c)
    got = jnp.stack([back[0, 0], swap_c(back[0, 1]), swap_x(back[1, 0], 2), swap_x(swap_c(back[1, 1]), 2)])
    got = flip(flip(got.reshape(2, 2, 16, 4, 128), 0, xh), 1, c)
    got = got.transpose(3, 2, 0, 1, 4).reshape(4, 16, 512)

    back = lax.all_to_all(reduced, ("c", "xh", "xl"), 0, 0, tiled=True)
    back = back.swapaxes(0, 1).reshape(3, 32, 16, 256).astype(F32)

    z_terms = scatter_group(z_near, z_far)
    output = (hidden + sum(t.astype(F32) for t in z_terms)).astype(BF16)
    return (
        output,
        grad_tokens,
        all_sum(dgain_attn),
        got[0],
        got[1],
        got[2],
        got[3].T,
        all_sum(dgain_moe),
        back[0],
        back[1],
        jnp.swapaxes(back[2], 1, 2),
    )


def solution(mesh):
    split = Mesh(mesh.devices.reshape(4, 2, 4, 2, 2), ("y", "xh", "z", "c", "xl"))
    dp = ("y", "xh", "z", "c")
    rows = P((*dp, "xl"), None)
    outs = (
        rows,
        rows,
        P(),
        P(dp, "xl"),
        P(dp, "xl"),
        P(dp, "xl"),
        P("xl", dp),
        P(),
        P(None, dp, "xl"),
        P(None, dp, "xl"),
        P(None, "xl", dp),
    )
    ins = (
        rows,
        P(),
        P(dp, "xl"),
        P(dp, "xl"),
        P(dp, "xl"),
        P("xl", dp),
        P(),
        P(None, dp, "xl"),
        P(None, dp, "xl"),
        P(None, "xl", dp),
        P(dp, None),
        P(dp, None),
        rows,
    )
    return jax.shard_map(on_device, mesh=split, in_specs=ins, out_specs=outs, check_vma=False)
```

```python
import jax
import jax.numpy as jnp
from jax import lax
from jax.experimental import pallas as pl
from jax.experimental.pallas import tpu as pltpu
from jax.sharding import Mesh
from jax.sharding import PartitionSpec as P

HD = 64
CAP = 160
EPSILON = 1e-06
THETA = 10000.0
LOCAL_E = 4
F32 = jnp.float32
BF16 = jnp.bfloat16
VMEM_BYTES = 60 * 1024 * 1024
SMALL_VMEM_BYTES = 32 * 1024 * 1024


def swap_x(value, bits):
    return lax.ppermute(value, ("xh", "xl"), [(i, i ^ bits) for i in range(4)])


def swap_c(value):
    return lax.ppermute(value, "c", [(0, 1), (1, 0)])


def swap_4(value, axis, bits):
    return lax.ppermute(value, axis, [(i, i ^ bits) for i in range(4)])


def after(value, *others):
    return lax.optimization_barrier((value, others))[0]


def together(*values):
    return lax.optimization_barrier(values)


def flip(value, axis, bit):
    return jnp.where(bit == 1, jnp.flip(value, axis), value)


def add(*terms):
    return sum(t.astype(F32) for t in terms)


def dot(a, b, ca, cb):
    return lax.dot_general(a, b, (((ca,), (cb,)), ((), ())), preferred_element_type=F32)


def whole(n):
    return [pl.BlockSpec(memory_space=pltpu.VMEM)] * n


def cost(flops, nbytes):
    return pl.CostEstimate(flops=int(flops), bytes_accessed=int(nbytes), transcendentals=0)


def kernel_call(body, ins, outs, name, scratch=(), smem=0, flops=1e9):
    specs = [pl.BlockSpec(memory_space=pltpu.SMEM)] * smem + whole(len(ins) - smem)
    nbytes = sum(v.size * v.dtype.itemsize for v in (*ins, *outs))
    return pl.pallas_call(
        body,
        out_shape=outs,
        in_specs=specs,
        out_specs=whole(len(outs)),
        scratch_shapes=list(scratch),
        compiler_params=pltpu.CompilerParams(vmem_limit_bytes=SMALL_VMEM_BYTES),
        cost_estimate=cost(flops, nbytes),
        name=name,
    )(*ins)


def shape(*dims, dtype=BF16):
    return jax.ShapeDtypeStruct(dims, dtype)


OUT, QKV, SPARE = 1024, 768, 128
PACKED = OUT + QKV
OWN = 256 + QKV


def d_block(y, xh, z):
    return (y * 2 + xh) * 4 + z


def assemble_body(ids, p0, p1, p2, p3, half_ref):
    for y, piece in enumerate((p0, p1, p2, p3)):
        for z in range(4):
            for xh in range(2):
                row = d_block(y ^ ids[0], xh, z ^ ids[1]) * 16
                rows = pl.ds(pl.multiple_of(row, 16), 16)
                half_ref[rows, :] = piece[z, xh * 16 : xh * 16 + 16, :]


def interleave(ids, own, other, dst):
    for half, c in ((own, ids[2]), (other, 1 - ids[2])):
        for n in range(32):
            rows = pl.ds(pl.multiple_of(n * 32 + c * 16, 16), 16)
            dst[rows, :] = half[n * 16 : n * 16 + 16, :]


def rotated(v, cos, sin):
    lane = lax.broadcasted_iota(jnp.int32, v.shape, 1)
    width = v.shape[1]
    other = jnp.where(lane % HD < HD // 2, pltpu.roll(v, width - 32, 1), pltpu.roll(v, 32, 1))
    return v * cos + other * sin


def attend_body(ids, t0, t1, t2, t3, gain, own, other, cos_ref, sin_ref, n1_ref, qkv_ref, w_ref, m0, m1, m2, m3):
    tokens, outs = (t0, t1, t2, t3), (m0, m1, m2, m3)
    cos, sin = cos_ref[...], sin_ref[...]
    interleave(ids, own, other, w_ref)
    for s in range(2):
        for half in range(2):
            x = tokens[2 * s + half][:256].astype(F32)
            r1 = lax.rsqrt(jnp.mean(x * x, -1, keepdims=True) + EPSILON)
            n1_ref[s, half * 256 : half * 256 + 256, :] = (x * r1 * gain[...]).astype(BF16)
        proj = jnp.dot(n1_ref[s], w_ref[...], preferred_element_type=F32)
        q = rotated(proj[:, :256], cos, sin).astype(BF16)
        k = rotated(proj[:, 256:512], cos, sin).astype(BF16)
        v = proj[:, 512:].astype(BF16)
        qkv_ref[s, :, :256] = q
        qkv_ref[s, :, 256:512] = k
        qkv_ref[s, :, 512:] = v
        mixed = []
        for h in range(4):
            cols = slice(h * HD, h * HD + HD)
            scores = dot(q[:, cols], k[:, cols], 1, 1) * (HD**-0.5)
            e = jnp.exp(scores - jnp.max(scores, -1, keepdims=True))
            p = (e / jnp.sum(e, -1, keepdims=True)).astype(BF16)
            mixed.append(dot(p, v[:, cols], 1, 0).astype(BF16))
        out = jnp.concatenate(mixed, 1)
        outs[2 * s][...] = out[:256]
        outs[2 * s + 1][...] = out[256:]


def out_columns(x):
    block = (x % 2) * 2 + x // 2
    return slice(block * 256, block * 256 + 256)


def project_body(ids, tokens, gain, m0, m1, m2, m3, own, other, hidden_ref, n2_ref, wo_ref, mixed_ref):
    interleave(ids, own, other, wo_ref)
    for x, m in enumerate((m0, m1, m2, m3)):
        mixed_ref[:, out_columns(x)] = m[...]
    hidden = tokens[...].astype(F32) + dot(mixed_ref[...], wo_ref[...], 1, 1)
    hidden_ref[...] = hidden
    r2 = lax.rsqrt(jnp.mean(hidden * hidden, -1, keepdims=True) + EPSILON)
    n2_ref[...] = (hidden * r2 * gain[...]).astype(BF16)


def expert_pieces():
    for y in range(4):
        for z in range(4):
            for xh in range(2):
                row = d_block(y, xh, z) * 32
                yield (y * 4 + z, xh), slice(row, row + 32)


def relative_pieces(ids):
    for y in range(4):
        for z in range(4):
            for c in range(2):
                for x in range(4):
                    row = d_block(y, (x // 2) ^ ids[3], z) * 32 + (c ^ ids[2]) * 16
                    rows = pl.ds(pl.multiple_of(row, 16), 16)
                    yield (y * 4 + z, c, x), rows, slice((x % 2) * 256, (x % 2) * 256 + 256)


def expert_body(*refs):
    ids, n2, ct = refs[0], refs[1:9], list(refs[9:15])
    ct[5:] = [ct[5].at[0], ct[5].at[1], ct[5].at[2]]
    rank_ref, share_ref, w_ref = refs[15:18]
    z_near, z_far, g_near, g_far, dw_ref = refs[18:23]
    wg, wu, wd, x_s, gz_s, p_s, z_s, gx_s, dw_s = refs[23:]
    e = pl.program_id(0)
    there = pl.ds(pl.multiple_of(e * CAP, 32), CAP)
    for piece, d in expert_pieces():
        wg[d, :] = w_ref[*piece, 0, 0]
        wu[d, :] = w_ref[*piece, 1, 0]
        wd[d, :] = w_ref[*piece, 2, 0]
    shares = []
    slot = lax.broadcasted_iota(jnp.int32, (CAP, 512), 0)
    for s in range(4):
        hit = slot == rank_ref[0, s : s + 1, :]
        share = jnp.sum(jnp.where(hit, share_ref[0, s : s + 1, :], 0.0), 1, keepdims=True)
        shares.append(share)
        p = hit.astype(F32).astype(BF16)
        p_s[s, there, :] = p
        here = slice(s * CAP, s * CAP + CAP)
        x_s[here, :] = (
            dot(p[:, :256], n2[2 * s][...], 1, 0) + dot(p[:, 256:], n2[2 * s + 1][...], 1, 0)
        ).astype(BF16)
        gz_s[here, :] = (
            (dot(p[:, :256], ct[2 * s][...], 1, 0) + dot(p[:, 256:], ct[2 * s + 1][...], 1, 0))
            * share
        ).astype(BF16)
    share = jnp.concatenate(shares, 0)
    a = dot(x_s[...], wg[...], 1, 0)
    b = dot(x_s[...], wu[...], 1, 0)
    sig = 1.0 / (1.0 + jnp.exp(-a))
    sa = a * sig
    u = (sa * b).astype(BF16)
    gu = dot(gz_s[...], wd[...], 1, 0)
    ga = (gu * b * sig * (1.0 + a * (1.0 - sig))).astype(BF16)
    gb = (gu * sa).astype(BF16)
    z = (dot(u, wd[...], 1, 1) * share).astype(BF16)
    gx = (dot(ga, wg[...], 1, 1) + dot(gb, wu[...], 1, 1)).astype(BF16)
    for s in range(4):
        here = slice(s * CAP, s * CAP + CAP)
        z_s[s, there, :] = z[here]
        gx_s[s, there, :] = gx[here]
    for m, (left, right) in enumerate(((x_s, ga), (x_s, gb), (gz_s, u))):
        dw_s[...] = dot(left[...], right, 0, 0).astype(BF16)
        for piece, rows, cols in relative_pieces(ids):
            dw_ref[*piece, m, 0] = dw_s[rows, cols]

    @pl.when(e == LOCAL_E - 1)
    def _():
        for s in range(4):
            for src, near, far in ((z_s, z_near, z_far), (gx_s, g_near, g_far)):
                total = dot(p_s[s], src[s], 0, 0).astype(BF16)
                dst = near if s < 2 else far
                dst[2 * (s % 2)] = total[:256]
                dst[2 * (s % 2) + 1] = total[256:]


W_BLOCK = (16, 2, 3, 1, 32, 512)


def run_experts(ids, n2, ct, rank, share, weights):
    table = pl.BlockSpec((1, 4, 512), lambda e: (e, 0, 0))
    w_spec = pl.BlockSpec(W_BLOCK, lambda e: (0, 0, 0, e, 0, 0))
    dw_spec = pl.BlockSpec((16, 2, 4, 3, 1, 16, 256), lambda e: (0, 0, 0, 0, e, 0, 0))
    blocks = shape(4, 256, 1024)
    return pl.pallas_call(
        expert_body,
        grid=(LOCAL_E,),
        out_shape=(blocks,) * 4 + (shape(16, 2, 4, 3, LOCAL_E, 16, 256),),
        in_specs=[pl.BlockSpec(memory_space=pltpu.SMEM)] + whole(14) + [table, table, w_spec],
        out_specs=whole(4) + [dw_spec],
        scratch_shapes=[
            pltpu.VMEM((1024, 512), BF16),
            pltpu.VMEM((1024, 512), BF16),
            pltpu.VMEM((1024, 512), BF16),
            pltpu.VMEM((4 * CAP, 1024), BF16),
            pltpu.VMEM((4 * CAP, 1024), BF16),
            pltpu.VMEM((4, LOCAL_E * CAP, 512), BF16),
            pltpu.VMEM((4, LOCAL_E * CAP, 1024), BF16),
            pltpu.VMEM((4, LOCAL_E * CAP, 1024), BF16),
            pltpu.VMEM((1024, 512), BF16),
        ],
        compiler_params=pltpu.CompilerParams(vmem_limit_bytes=VMEM_BYTES),
        cost_estimate=cost(36e9, 60e6),
        name="experts",
    )(ids, *n2, *ct, rank, share, weights)


def hidden_back_body(g0, g1, g2, g3, hidden_ref, ct, gain, wo, gh_ref, ghb_ref, m0, m1, m2, m3, dgain_ref):
    gn2 = g0[...].astype(F32) + g1[...].astype(F32) + g2[...].astype(F32) + g3[...].astype(F32)
    hidden = hidden_ref[...]
    r2 = lax.rsqrt(jnp.mean(hidden * hidden, -1, keepdims=True) + EPSILON)
    w2 = gn2 * gain[...]
    gh = ct[...].astype(F32) + r2 * w2 - hidden * (r2 * r2 * r2) * jnp.mean(w2 * hidden, -1, keepdims=True)
    gh_ref[...] = gh
    ghb = gh.astype(BF16)
    ghb_ref[...] = ghb
    gm = dot(ghb, wo[...], 1, 0).astype(BF16)
    for x, m in enumerate((m0, m1, m2, m3)):
        m[...] = gm[:, out_columns(x)]
    dgain_ref[...] = jnp.sum(gn2 * hidden * r2, 0, keepdims=True)


def attend_back_body(qkv, m0, m1, m2, m3, cos_ref, sin_ref, w_ref, g_ref, p0, p1, p2, p3):
    gm_refs, outs = (m0, m1, m2, m3), (p0, p1, p2, p3)
    cos, sin = cos_ref[...], -sin_ref[...]
    for s in range(2):
        gm = jnp.concatenate([gm_refs[2 * s][...], gm_refs[2 * s + 1][...]], 0)
        gqs, gks, gvs = [], [], []
        for h in range(4):
            q = qkv[s, :, h * HD : h * HD + HD]
            k = qkv[s, :, 256 + h * HD : 256 + h * HD + HD]
            v = qkv[s, :, 512 + h * HD : 512 + h * HD + HD]
            gmh = gm[:, h * HD : h * HD + HD]
            scores = dot(q, k, 1, 1) * (HD**-0.5)
            e = jnp.exp(scores - jnp.max(scores, -1, keepdims=True))
            p = e / jnp.sum(e, -1, keepdims=True)
            gp = dot(gmh, v, 1, 1)
            gs = (p * (gp - jnp.sum(gp * p, -1, keepdims=True))).astype(BF16)
            gqs.append(dot(gs, k, 1, 0) * (HD**-0.5))
            gks.append(dot(gs, q, 0, 0) * (HD**-0.5))
            gvs.append(dot(p.astype(BF16), gmh, 0, 0))
        g_ref[s, :, :256] = rotated(jnp.concatenate(gqs, 1), cos, sin).astype(BF16)
        g_ref[s, :, 256:512] = rotated(jnp.concatenate(gks, 1), cos, sin).astype(BF16)
        g_ref[s, :, 512:] = jnp.concatenate(gvs, 1).astype(BF16)
        part = dot(g_ref[s], w_ref[...], 1, 1).astype(BF16)
        outs[2 * s][...] = part[:256]
        outs[2 * s + 1][...] = part[256:]


def attend_grad_body(n1, g, w_qkv, gain, grad_ref, dgain_ref):
    qkv = dot(n1[0], g[0], 0, 0) + dot(n1[1], g[1], 0, 0)
    grad_ref[...] = qkv.astype(BF16)
    weighted = qkv * w_qkv[...].astype(F32)
    ones = jnp.ones((8, QKV), F32)
    sums = lax.dot_general(
        ones,
        weighted,
        (((1,), (1,)), ((), ())),
        precision=lax.Precision.HIGHEST,
        preferred_element_type=F32,
    )
    dgain_ref[...] = sums[:1] / gain[...]


def arrange_body(ids, qkv, dgain, dgain_moe, *refs):
    ghb, mixed = refs[:4], refs[4:8]
    near_ref, far_ref, out = refs[8:]
    out[...] = sum(dot(ghb[x][...], mixed[x][...], 0, 0) for x in range(4)).astype(BF16)
    rows = [v[:, i * 128 : i * 128 + 128] for v in (dgain[...], dgain_moe[...]) for i in range(8)]
    gains = jnp.concatenate(rows + [jnp.zeros((16, 128), F32)], 0).astype(BF16)
    for y in range(4):
        for z in range(4):
            near_ref[z, y, :, OWN:] = gains
            far_ref[z, y, :, OWN:] = gains
            for xh in range(2):
                row = d_block(y ^ ids[0], xh, z ^ ids[1]) * 32
                for dst, c in ((near_ref, ids[2]), (far_ref, 1 - ids[2])):
                    rows = pl.ds(pl.multiple_of(row + c * 16, 16), 16)
                    dst[z, y, xh * 16 : xh * 16 + 16, :256] = out[rows, :]
                    dst[z, y, xh * 16 : xh * 16 + 16, 256:OWN] = qkv[rows, :]


def tokens_back_body(g0, g1, g2, g3, tokens, gain, gh, out_ref):
    gn1 = g0[...].astype(F32) + g1[...].astype(F32) + g2[...].astype(F32) + g3[...].astype(F32)
    x = tokens[...].astype(F32)
    r1 = lax.rsqrt(jnp.mean(x * x, -1, keepdims=True) + EPSILON)
    w1 = gn1 * gain[...]
    out_ref[...] = (
        gh[...] + r1 * w1 - x * (r1 * r1 * r1) * jnp.mean(w1 * x, -1, keepdims=True)
    ).astype(BF16)


def rotary_tables(xl):
    frequency = THETA ** (-2.0 * jnp.arange(HD // 2, dtype=F32) / HD)
    place = jnp.arange(512)
    place = ((place // 256) ^ xl) * 256 + place % 256
    angles = place.astype(F32)[:, None] * frequency[None, :]
    cos, sin = jnp.cos(angles), jnp.sin(angles)
    return jnp.concatenate([cos] * 8, 1), jnp.concatenate([-sin, sin] * 4, 1)


def last_send_body(ids, s0, s1, s2, s3, near, far, own_ref, gain_ref, p1, p2, p3, total):
    total[...] = s0[...].astype(F32) + s1[...].astype(F32) + s2[...].astype(F32) + s3[...].astype(F32)
    own = pl.ds(pl.multiple_of(ids[3] * 16, 16), 16)
    other = pl.ds(pl.multiple_of((1 - ids[3]) * 16, 16), 16)
    gains = total[:16, OWN:]
    gain_ref[...] = gains
    own_ref[...] = total[own, :OWN]
    base = 2 * 3 * LOCAL_E * 16
    for x, p in ((1, p1), (2, p2), (3, p3)):
        for m in range(3):
            for e in range(LOCAL_E):
                row = (m * LOCAL_E + e) * 16
                p[row : row + 16, :] = near[0, x, m, e]
                p[base // 2 + row : base // 2 + row + 16, :] = far[x, m, e]
        p[base : base + 16, :] = jnp.concatenate([gains, gains], 1).astype(BF16)
    for j in range(4):
        part = total[other, j * 256 : j * 256 + 256]
        p2[base + 16 + j * 16 : base + 32 + j * 16, :] = part.astype(BF16)


def last_body(ids, own, own_gains, g1, g2, g3, near, far, do, dq, dk, dv, gain_ref, *experts):
    c, xh, xl = ids[2], ids[3], ids[4]
    base = 2 * 3 * LOCAL_E * 16
    mine = pl.ds(pl.multiple_of(xh * 256, 256), 256)
    theirs = pl.ds(pl.multiple_of((1 - xh) * 256, 256), 256)
    for j, d in enumerate((do, dq, dk, dv)):
        d[:, mine] = own[:, j * 256 : j * 256 + 256]
        d[:, theirs] = g2[base + 16 + j * 16 : base + 32 + j * 16, :].astype(F32)
    gain_ref[...] = own_gains[...] + sum(g[base : base + 16, :128].astype(F32) for g in (g1, g2, g3))
    for x in range(4):
        for b in range(2):
            owner = (c ^ b) * 4 + (xh ^ (x // 2)) * 2 + (xl ^ (x % 2))
            for m, d in enumerate(experts):
                for e in range(LOCAL_E):
                    row = ((b * 3 + m) * LOCAL_E + e) * 16
                    if x == 0:
                        block = near[0, 0, m, e] if b == 0 else far[0, m, e]
                    else:
                        block = (g1, g2, g3)[x - 1][row : row + 16, :]
                    d[owner * LOCAL_E + e] = block.astype(F32)


def route_rows(routes, route_weights, xl):
    high = lax.reduce_precision(route_weights, 8, 7)
    low = lax.reduce_precision(route_weights - high, 8, 7)
    table = jnp.concatenate([routes.T.astype(F32), high.T, low.T], 0).reshape(24, 2, 256)
    table = jnp.where(xl == 1, table[:, 1], table[:, 0])
    return jnp.pad(table.astype(BF16), ((0, 40), (0, 0))).reshape(16, 1024)


def route_tables(near, far, c, xh, xl):
    tables = jnp.concatenate([near, far], 0).reshape(8, 64, 256)[:, :24].astype(F32)
    tables = tables.reshape(4, 2, 24, 256).transpose(0, 2, 1, 3).reshape(4, 24, 512)
    first = ((c * 4 + xh * 2 + xl) * LOCAL_E).astype(F32)
    names = first + jnp.arange(LOCAL_E, dtype=F32)
    match = tables[None, :, :8, :] == names[:, None, None, None]
    shares = tables[:, 8:16] + tables[:, 16:]
    share = jnp.sum(jnp.where(match, shares[None], 0.0), 2)
    named = jnp.any(match, 2)
    before = (jnp.arange(512)[:, None] <= jnp.arange(512)[None, :]).astype(BF16)
    count = jnp.dot(named.astype(BF16), before, preferred_element_type=F32)
    rank = jnp.where(named, count.astype(jnp.int32) - 1, -1)
    return rank, share


def on_device(
    tokens,
    gain_attn,
    w_query,
    w_key,
    w_value,
    w_out,
    gain_moe,
    w_gate,
    w_up,
    w_down,
    routes,
    route_weights,
    cotangent,
):
    y, xh, z, c, xl = (lax.axis_index(a) for a in ("y", "xh", "z", "c", "xl"))
    ids = jnp.stack([y, z, c, xh, xl]).astype(jnp.int32)
    gain_attn = gain_attn.reshape(1, 1024)
    gain_moe = gain_moe.reshape(1, 1024)

    heads = jnp.stack([w_query, w_key, w_value], 1).reshape(16, 3, 2, 256)
    heads = flip(heads, 2, xh)
    w_o = w_out.T.reshape(16, 2, 256)
    for_same, for_other = flip(w_o, 1, xh).reshape(16, 512), flip(w_o, 1, 1 - xh).reshape(16, 512)
    for_2 = jnp.concatenate([for_other, heads[:, :, 1].reshape(16, 768)], 1)
    local = jnp.stack([w_gate, w_up, jnp.swapaxes(w_down, 1, 2)])
    local = local.reshape(3, 2, 2, 2, LOCAL_E, 16, 256)
    local = flip(flip(flip(local, 1, c), 2, xh), 3, xl).transpose(1, 2, 3, 0, 4, 5, 6)
    local = local.reshape(2, 4, 3, LOCAL_E, 16, 256)
    near, far = local[0], local[1]

    got_2, got_1, got_3 = together(swap_x(for_2, 2), swap_x(for_same, 1), swap_x(for_other, 3))
    far = swap_c(far)
    here = jnp.concatenate([for_same, got_1, heads[:, :, 0].reshape(16, 768)], 1)
    there = jnp.concatenate([got_2[:, :512], got_3, got_2[:, 512:]], 1)
    rows = flip(jnp.stack([here, there]), 0, xh).reshape(32, PACKED)
    both = [flip(jnp.stack([near[x], far[x]], 2), 2, c) for x in range(4)]
    sent = jnp.concatenate([tokens, route_rows(routes, route_weights, xl)], 0)
    rows, sent = together(rows, sent)

    moved = together(
        *[swap_4(rows, "z", k) for k in (1, 2, 3)], *[swap_x(both[x], x) for x in (1, 2, 3)]
    )
    owned = [both[0], *moved[3:]]
    owned = jnp.stack([jnp.concatenate(owned[:2], -1), jnp.concatenate(owned[2:], -1)])
    owned = flip(owned, 0, xh).reshape(2, 3, LOCAL_E, 32, 512)
    experts = lax.all_gather(owned, ("y", "z"), axis=0)
    zs_o = jnp.stack([rows[:, :OUT], *[m[:, :OUT] for m in moved[:3]]])
    zs = jnp.stack([rows[:, OUT:], *[m[:, OUT:] for m in moved[:3]]])
    zs, zs_o, sent, owned = together(zs, zs_o, sent, owned)

    *moved, t1, t3, cos, sin = together(
        *[swap_4(zs, "y", k) for k in (1, 2, 3)],
        swap_x(sent, 1),
        swap_x(sent, 3),
        *rotary_tables(xl),
    )
    half = kernel_call(assemble_body, [ids, zs, *moved], (shape(512, QKV),), "assemble", smem=1)
    half, zs_o, sent, t1, t3 = together(half[0], zs_o, sent, t1, t3)
    moved_o = [swap_4(zs_o, "y", k) for k in (1, 2, 3)]
    other_half, t2 = together(swap_c(half), swap_x(sent, 2))
    blocks = [sent, t1, t2, t3]
    near = jnp.stack([t[256:] for t in blocks])
    other_half, near, cot = together(other_half, near, cotangent)
    ct_1, ct_3 = swap_x(cot, 1), swap_x(cot, 3)

    n1, qkv, w_qkv, *mixed = kernel_call(
        attend_body,
        [ids, *blocks, gain_attn, half, other_half, cos, sin],
        (shape(2, 512, 1024), shape(2, 512, QKV), shape(1024, QKV)) + (shape(256, 256),) * 4,
        "attend",
        smem=1,
        flops=8e9,
    )
    *mixed, ct_1, ct_3, near, cot, moved_o[0], moved_o[1], moved_o[2] = together(
        *mixed, ct_1, ct_3, near, cot, *moved_o
    )
    half = kernel_call(assemble_body, [ids, zs_o, *moved_o], (shape(512, OUT),), "assemble", smem=1)
    other_half, cot, *moved = together(
        swap_c(half[0]), cot, *[swap_x(mixed[x], x) for x in (1, 2, 3)]
    )
    ct_2 = swap_x(cot, 2)
    hidden, n2, w_o_full = kernel_call(
        project_body,
        [ids, tokens, gain_moe, mixed[0], *moved, half[0], other_half],
        (shape(256, 1024, dtype=F32), shape(256, 1024), shape(1024, OUT)),
        "project",
        scratch=[pltpu.VMEM((256, OUT), BF16)],
        smem=1,
    )
    n2_1, n2_3, n2_far, far, ct_2 = together(
        swap_x(n2, 1), swap_x(n2, 3), swap_c(n2), swap_c(near), ct_2
    )
    ct_three = jnp.stack([ct_1, ct_2, ct_3])
    ct_three, n2, n2_1, n2_3 = together(ct_three, n2, n2_1, n2_3)
    rank, share = route_tables(near, far, c, xh, xl)
    n2_2, ct_far, n2_far_1, n2_far_3, rank, share = together(
        swap_x(n2, 2), swap_c(ct_three), swap_c(n2_1), swap_c(n2_3), rank, share
    )
    n2_all = [n2, n2_1, n2_2, n2_3, n2_far, n2_far_1, swap_c(n2_2), n2_far_3]
    ct_all = [cot, ct_1, ct_2, ct_3, swap_c(cot), ct_far]
    z_near, z_far, g_near, g_far, grads = run_experts(ids, n2_all, ct_all, rank, share, experts)
    reduced = lax.psum_scatter(grads, ("y", "z"), scatter_dimension=0)
    g_far, z_far = together(swap_c(g_far), z_far)
    g_sums = [add(g_near[x], g_far[x]).astype(BF16) for x in range(4)]
    *g_sums, z_far = together(*g_sums, z_far)
    z_far = swap_c(z_far)
    gn2_1, gn2_3, z_far, z_near = together(swap_x(g_sums[1], 1), swap_x(g_sums[3], 3), z_far, z_near)
    z_sums = [add(z_near[x], z_far[x]).astype(BF16) for x in range(4)]
    gn2_2, *z_sums = together(swap_x(g_sums[2], 2), *z_sums)
    gn2 = [g_sums[0], gn2_1, gn2_2, gn2_3]
    gh, ghb, *gm, dgain_moe = kernel_call(
        hidden_back_body,
        [*gn2, hidden, cotangent, gain_moe, w_o_full],
        (shape(256, 1024, dtype=F32), shape(256, 1024))
        + (shape(256, 256),) * 4
        + (shape(1, 1024, dtype=F32),),
        "hidden_back",
    )
    moved = together(*[swap_x(gm[x], x) for x in (1, 2, 3)])
    gm = [gm[0], *moved]
    ghb, *gm = together(ghb, *gm)
    ghb = [ghb, swap_x(ghb, 1), swap_x(ghb, 2), swap_x(ghb, 3)]
    g, *gn1 = kernel_call(
        attend_back_body,
        [qkv, *gm, cos, sin, w_qkv],
        (shape(2, 512, QKV),) + (shape(256, 1024),) * 4,
        "attend_back",
        flops=10e9,
    )
    g, ghb[1], ghb[3], *gn1 = together(g, ghb[1], ghb[3], *gn1)
    qkv_grad, dgain_attn = kernel_call(
        attend_grad_body,
        [n1, g, w_qkv, gain_attn],
        (shape(1024, QKV), shape(1, 1024, dtype=F32)),
        "attend_grad",
        flops=4e9,
    )
    qkv_grad, ghb[2], gn1[1], gn1[2], gn1[3] = together(qkv_grad, ghb[2], *gn1[1:])
    gn1 = [gn1[0]] + [swap_x(gn1[x], x) for x in (1, 2, 3)]
    near, far = kernel_call(
        arrange_body,
        [ids, qkv_grad, dgain_attn, dgain_moe, *ghb, *mixed],
        (shape(4, 4, 32, OWN + SPARE),) * 2,
        "arrange",
        scratch=[pltpu.VMEM((1024, 256), BF16)],
        smem=1,
    )
    sums = add(near, swap_c(far)).astype(BF16)
    sums, *z_sums[1:] = together(sums, *z_sums[1:])
    *moved, gn1[1], gn1[3], z_1, z_3 = together(
        *[swap_4(sums[k], "z", k) for k in (1, 2, 3)],
        gn1[1],
        gn1[3],
        swap_x(z_sums[1], 1),
        swap_x(z_sums[3], 3),
    )
    z_2 = swap_x(z_sums[2], 2)
    sums = add(sums[0], *moved).astype(BF16)
    sums, reduced = together(sums, reduced)
    back_far = swap_c(reduced[1])
    *moved, back_far, gn1[2] = together(
        *[swap_4(sums[k], "y", k) for k in (1, 2, 3)], back_far, gn1[2]
    )
    grad_tokens = kernel_call(
        tokens_back_body, [*gn1, tokens, gain_attn, gh], (shape(256, 1024),), "tokens_back"
    )[0]
    sent_rows = 2 * 3 * LOCAL_E * 16
    own, own_gains, *sent = kernel_call(
        last_send_body,
        [ids, sums[0], *moved, reduced, back_far],
        (
            shape(16, OWN, dtype=F32),
            shape(16, 128, dtype=F32),
            shape(sent_rows + 16, 256),
            shape(sent_rows + 80, 256),
            shape(sent_rows + 16, 256),
        ),
        "last_send",
        scratch=[pltpu.VMEM((32, OWN + SPARE), F32)],
        smem=1,
    )
    *sent, z_2 = together(*sent, z_2)
    got = together(*[swap_x(sent[x - 1], x) for x in (1, 2, 3)])
    d_out, d_query, d_key, d_value, gains, d_gate, d_up, d_down = kernel_call(
        last_body,
        [ids, own, own_gains, *got, reduced, back_far],
        (shape(16, 512, dtype=F32),) * 4
        + (shape(16, 128, dtype=F32),)
        + (shape(8 * LOCAL_E, 16, 256, dtype=F32),) * 3,
        "last",
        smem=1,
    )
    gains = gains.reshape(2, 1024)
    output = (hidden + add(z_sums[0], z_1, z_2, z_3)).astype(BF16)
    return (
        output,
        grad_tokens,
        gains[0],
        d_query,
        d_key,
        d_value,
        d_out.T,
        gains[1],
        d_gate,
        d_up,
        jnp.swapaxes(d_down, 1, 2),
    )


def solution(mesh):
    split = Mesh(mesh.devices.reshape(4, 2, 4, 2, 2), ("y", "xh", "z", "c", "xl"))
    dp = ("y", "xh", "z", "c")
    rows = P((*dp, "xl"), None)
    outs = (
        rows,
        rows,
        P(),
        P(dp, "xl"),
        P(dp, "xl"),
        P(dp, "xl"),
        P("xl", dp),
        P(),
        P(None, dp, "xl"),
        P(None, dp, "xl"),
        P(None, "xl", dp),
    )
    ins = (
        rows,
        P(),
        P(dp, "xl"),
        P(dp, "xl"),
        P(dp, "xl"),
        P("xl", dp),
        P(),
        P(None, dp, "xl"),
        P(None, dp, "xl"),
        P(None, "xl", dp),
        P(dp, None),
        P(dp, None),
        rows,
    )
    return jax.shard_map(on_device, mesh=split, in_specs=ins, out_specs=outs, check_vma=False)
```

```python
import jax
import jax.numpy as jnp
from jax import lax
from jax.experimental import pallas as pl
from jax.experimental.pallas import tpu as pltpu
from jax.sharding import Mesh
from jax.sharding import PartitionSpec as P

HD = 64
CAP = 160
EPSILON = 1e-06
THETA = 10000.0
LOCAL_E = 4
F32 = jnp.float32
BF16 = jnp.bfloat16
VMEM_BYTES = 60 * 1024 * 1024
SMALL_VMEM_BYTES = 32 * 1024 * 1024


def swap_x(value, bits):
    return lax.ppermute(value, ("xh", "xl"), [(i, i ^ bits) for i in range(4)])


def swap_c(value):
    return lax.ppermute(value, "c", [(0, 1), (1, 0)])


def swap_4(value, axis, bits):
    return lax.ppermute(value, axis, [(i, i ^ bits) for i in range(4)])


def after(value, *others):
    return lax.optimization_barrier((value, others))[0]


def together(*values):
    return lax.optimization_barrier(values)


def flip(value, axis, bit):
    return jnp.where(bit == 1, jnp.flip(value, axis), value)


def add(*terms):
    return sum(t.astype(F32) for t in terms)


def dot(a, b, ca, cb):
    return lax.dot_general(a, b, (((ca,), (cb,)), ((), ())), preferred_element_type=F32)


def whole(n):
    return [pl.BlockSpec(memory_space=pltpu.VMEM)] * n


def cost(flops, nbytes):
    return pl.CostEstimate(flops=int(flops), bytes_accessed=int(nbytes), transcendentals=0)


def kernel_call(body, ins, outs, name, scratch=(), smem=0, flops=1e9):
    specs = [pl.BlockSpec(memory_space=pltpu.SMEM)] * smem + whole(len(ins) - smem)
    nbytes = sum(v.size * v.dtype.itemsize for v in (*ins, *outs))
    return pl.pallas_call(
        body,
        out_shape=outs,
        in_specs=specs,
        out_specs=whole(len(outs)),
        scratch_shapes=list(scratch),
        compiler_params=pltpu.CompilerParams(vmem_limit_bytes=SMALL_VMEM_BYTES),
        cost_estimate=cost(flops, nbytes),
        name=name,
    )(*ins)


def shape(*dims, dtype=BF16):
    return jax.ShapeDtypeStruct(dims, dtype)


OUT, QKV, SPARE = 1024, 768, 128
PACKED = OUT + QKV
OWN = 256 + QKV


def d_block(y, xh, z):
    return (y * 2 + xh) * 4 + z


def assemble_body(ids, p0, p1, p2, p3, half_ref):
    for y, piece in enumerate((p0, p1, p2, p3)):
        for z in range(4):
            for xh in range(2):
                row = d_block(y ^ ids[0], xh, z ^ ids[1]) * 16
                rows = pl.ds(pl.multiple_of(row, 16), 16)
                half_ref[rows, :] = piece[z, xh * 16 : xh * 16 + 16, :]


def interleave(ids, own, other, dst):
    for half, c in ((own, ids[2]), (other, 1 - ids[2])):
        for n in range(32):
            rows = pl.ds(pl.multiple_of(n * 32 + c * 16, 16), 16)
            dst[rows, :] = half[n * 16 : n * 16 + 16, :]


def rotated(v, cos, sin):
    lane = lax.broadcasted_iota(jnp.int32, v.shape, 1)
    width = v.shape[1]
    other = jnp.where(lane % HD < HD // 2, pltpu.roll(v, width - 32, 1), pltpu.roll(v, 32, 1))
    return v * cos + other * sin


def attend_body(ids, t0, t1, t2, t3, gain, own, other, cos_ref, sin_ref, n1_ref, qkv_ref, w_ref, m0, m1, m2, m3):
    tokens, outs = (t0, t1, t2, t3), (m0, m1, m2, m3)
    cos, sin = cos_ref[...], sin_ref[...]
    interleave(ids, own, other, w_ref)
    for s in range(2):
        for half in range(2):
            x = tokens[2 * s + half][:256].astype(F32)
            r1 = lax.rsqrt(jnp.mean(x * x, -1, keepdims=True) + EPSILON)
            n1_ref[s, half * 256 : half * 256 + 256, :] = (x * r1 * gain[...]).astype(BF16)
        proj = jnp.dot(n1_ref[s], w_ref[...], preferred_element_type=F32)
        q = rotated(proj[:, :256], cos, sin).astype(BF16)
        k = rotated(proj[:, 256:512], cos, sin).astype(BF16)
        v = proj[:, 512:].astype(BF16)
        qkv_ref[s, :, :256] = q
        qkv_ref[s, :, 256:512] = k
        qkv_ref[s, :, 512:] = v
        mixed = []
        for h in range(4):
            cols = slice(h * HD, h * HD + HD)
            scores = dot(q[:, cols], k[:, cols], 1, 1) * (HD**-0.5)
            e = jnp.exp(scores - jnp.max(scores, -1, keepdims=True))
            p = (e / jnp.sum(e, -1, keepdims=True)).astype(BF16)
            mixed.append(dot(p, v[:, cols], 1, 0).astype(BF16))
        out = jnp.concatenate(mixed, 1)
        outs[2 * s][...] = out[:256]
        outs[2 * s + 1][...] = out[256:]


def out_columns(x):
    block = (x % 2) * 2 + x // 2
    return slice(block * 256, block * 256 + 256)


def project_body(ids, tokens, gain, m0, m1, m2, m3, own, other, hidden_ref, n2_ref, wo_ref, mixed_ref):
    interleave(ids, own, other, wo_ref)
    for x, m in enumerate((m0, m1, m2, m3)):
        mixed_ref[:, out_columns(x)] = m[...]
    hidden = tokens[...].astype(F32) + dot(mixed_ref[...], wo_ref[...], 1, 1)
    hidden_ref[...] = hidden
    r2 = lax.rsqrt(jnp.mean(hidden * hidden, -1, keepdims=True) + EPSILON)
    n2_ref[...] = (hidden * r2 * gain[...]).astype(BF16)


def expert_pieces():
    for y in range(4):
        for z in range(4):
            for xh in range(2):
                row = d_block(y, xh, z) * 32
                yield (y * 4 + z, xh), slice(row, row + 32)


def relative_pieces(ids):
    for y in range(4):
        for z in range(4):
            for c in range(2):
                for x in range(4):
                    row = d_block(y, (x // 2) ^ ids[3], z) * 32 + (c ^ ids[2]) * 16
                    rows = pl.ds(pl.multiple_of(row, 16), 16)
                    yield (y * 4 + z, c, x), rows, slice((x % 2) * 256, (x % 2) * 256 + 256)


def expert_body(*refs):
    ids, n2, (own, ring, far_own, far) = refs[0], refs[1:9], refs[9:13]
    ct = [own, *[ring.at[x] for x in range(3)], far_own, *[far.at[x] for x in range(3)]]
    rank_ref, share_ref, w_ref = refs[13:16]
    z_near, z_far, g_near, g_far, dw_ref = refs[16:21]
    wg, wu, wd, x_s, gz_s, p_s, z_s, gx_s = refs[21:]
    e = pl.program_id(0)
    there = pl.ds(pl.multiple_of(e * CAP, 32), CAP)
    for piece, d in expert_pieces():
        wg[d, :] = w_ref[*piece, 0, 0]
        wu[d, :] = w_ref[*piece, 1, 0]
        wd[d, :] = w_ref[*piece, 2, 0]
    shares = []
    slot = lax.broadcasted_iota(jnp.int32, (CAP, 512), 0)
    for s in range(4):
        hit = slot == rank_ref[0, s : s + 1, :]
        share = jnp.sum(jnp.where(hit, share_ref[0, s : s + 1, :], 0.0), 1, keepdims=True)
        shares.append(share)
        p = hit.astype(F32).astype(BF16)
        p_s[s, there, :] = p
        here = slice(s * CAP, s * CAP + CAP)
        x_s[here, :] = (
            dot(p[:, :256], n2[2 * s][...], 1, 0) + dot(p[:, 256:], n2[2 * s + 1][...], 1, 0)
        ).astype(BF16)
        gz_s[here, :] = (
            (dot(p[:, :256], ct[2 * s][...], 1, 0) + dot(p[:, 256:], ct[2 * s + 1][...], 1, 0))
            * share
        ).astype(BF16)
    share = jnp.concatenate(shares, 0)
    a = dot(x_s[...], wg[...], 1, 0)
    b = dot(x_s[...], wu[...], 1, 0)
    sig = 1.0 / (1.0 + jnp.exp(-a))
    sa = a * sig
    u = (sa * b).astype(BF16)
    gu = dot(gz_s[...], wd[...], 1, 0)
    ga = (gu * b * sig * (1.0 + a * (1.0 - sig))).astype(BF16)
    gb = (gu * sa).astype(BF16)
    z = (dot(u, wd[...], 1, 1) * share).astype(BF16)
    gx = (dot(ga, wg[...], 1, 1) + dot(gb, wu[...], 1, 1)).astype(BF16)
    for s in range(4):
        here = slice(s * CAP, s * CAP + CAP)
        z_s[s, there, :] = z[here]
        gx_s[s, there, :] = gx[here]
    for m, (left, right) in enumerate(((x_s, ga), (x_s, gb), (gz_s, u))):
        wg[...] = dot(left[...], right, 0, 0).astype(BF16)
        for piece, rows, cols in relative_pieces(ids):
            dw_ref[*piece, m, 0] = wg[rows, cols]

    @pl.when(e == LOCAL_E - 1)
    def _():
        for s in range(4):
            for src, near, far in ((z_s, z_near, z_far), (gx_s, g_near, g_far)):
                total = dot(p_s[s], src[s], 0, 0).astype(BF16)
                dst = near if s < 2 else far
                dst[2 * (s % 2)] = total[:256]
                dst[2 * (s % 2) + 1] = total[256:]


W_BLOCK = (16, 2, 3, 1, 32, 512)


def run_experts(ids, n2, ct, rank, share, weights):
    table = pl.BlockSpec((1, 4, 512), lambda e: (e, 0, 0))
    w_spec = pl.BlockSpec(W_BLOCK, lambda e: (0, 0, 0, e, 0, 0))
    dw_spec = pl.BlockSpec((16, 2, 4, 3, 1, 16, 256), lambda e: (0, 0, 0, 0, e, 0, 0))
    blocks = shape(4, 256, 1024)
    return pl.pallas_call(
        expert_body,
        grid=(LOCAL_E,),
        out_shape=(blocks,) * 4 + (shape(16, 2, 4, 3, LOCAL_E, 16, 256),),
        in_specs=[pl.BlockSpec(memory_space=pltpu.SMEM)] + whole(12) + [table, table, w_spec],
        out_specs=whole(4) + [dw_spec],
        scratch_shapes=[
            pltpu.VMEM((1024, 512), BF16),
            pltpu.VMEM((1024, 512), BF16),
            pltpu.VMEM((1024, 512), BF16),
            pltpu.VMEM((4 * CAP, 1024), BF16),
            pltpu.VMEM((4 * CAP, 1024), BF16),
            pltpu.VMEM((4, LOCAL_E * CAP, 512), BF16),
            pltpu.VMEM((4, LOCAL_E * CAP, 1024), BF16),
            pltpu.VMEM((4, LOCAL_E * CAP, 1024), BF16),
        ],
        compiler_params=pltpu.CompilerParams(vmem_limit_bytes=VMEM_BYTES),
        cost_estimate=cost(36e9, 60e6),
        name="experts",
    )(ids, *n2, *ct, rank, share, weights)


def hidden_back_body(g0, g1, g2, g3, hidden_ref, ct, gain, wo, gh_ref, ghb_ref, m0, m1, m2, m3, dgain_ref):
    gn2 = g0[...].astype(F32) + g1[...].astype(F32) + g2[...].astype(F32) + g3[...].astype(F32)
    hidden = hidden_ref[...]
    r2 = lax.rsqrt(jnp.mean(hidden * hidden, -1, keepdims=True) + EPSILON)
    w2 = gn2 * gain[...]
    gh = ct[...].astype(F32) + r2 * w2 - hidden * (r2 * r2 * r2) * jnp.mean(w2 * hidden, -1, keepdims=True)
    gh_ref[...] = gh
    ghb = gh.astype(BF16)
    ghb_ref[...] = ghb
    gm = dot(ghb, wo[...], 1, 0).astype(BF16)
    for x, m in enumerate((m0, m1, m2, m3)):
        m[...] = gm[:, out_columns(x)]
    dgain_ref[...] = jnp.sum(gn2 * hidden * r2, 0, keepdims=True)


def attend_back_body(qkv, m0, m1, m2, m3, cos_ref, sin_ref, w_ref, z_near, z_far, g_ref, *outs):
    gm_refs = (m0, m1, m2, m3)
    cos, sin = cos_ref[...], -sin_ref[...]
    for s in range(2):
        gm = jnp.concatenate([gm_refs[2 * s][...], gm_refs[2 * s + 1][...]], 0)
        gqs, gks, gvs = [], [], []
        for h in range(4):
            q = qkv[s, :, h * HD : h * HD + HD]
            k = qkv[s, :, 256 + h * HD : 256 + h * HD + HD]
            v = qkv[s, :, 512 + h * HD : 512 + h * HD + HD]
            gmh = gm[:, h * HD : h * HD + HD]
            scores = dot(q, k, 1, 1) * (HD**-0.5)
            e = jnp.exp(scores - jnp.max(scores, -1, keepdims=True))
            p = e / jnp.sum(e, -1, keepdims=True)
            gp = dot(gmh, v, 1, 1)
            gs = (p * (gp - jnp.sum(gp * p, -1, keepdims=True))).astype(BF16)
            gqs.append(dot(gs, k, 1, 0) * (HD**-0.5))
            gks.append(dot(gs, q, 0, 0) * (HD**-0.5))
            gvs.append(dot(p.astype(BF16), gmh, 0, 0))
        g_ref[s, :, :256] = rotated(jnp.concatenate(gqs, 1), cos, sin).astype(BF16)
        g_ref[s, :, 256:512] = rotated(jnp.concatenate(gks, 1), cos, sin).astype(BF16)
        g_ref[s, :, 512:] = jnp.concatenate(gvs, 1).astype(BF16)
        part = dot(g_ref[s], w_ref[...], 1, 1).astype(BF16)
        for half in range(2):
            x = 2 * s + half
            outs[x][...] = part[half * 256 : half * 256 + 256]
            outs[4 + x][...] = (z_near[x].astype(F32) + z_far[x].astype(F32)).astype(BF16)


def attend_grad_body(n1, g, w_qkv, gain, grad_ref, dgain_ref):
    qkv = dot(n1[0], g[0], 0, 0) + dot(n1[1], g[1], 0, 0)
    grad_ref[...] = qkv.astype(BF16)
    weighted = qkv * w_qkv[...].astype(F32)
    ones = jnp.ones((8, QKV), F32)
    sums = lax.dot_general(
        ones,
        weighted,
        (((1,), (1,)), ((), ())),
        precision=lax.Precision.HIGHEST,
        preferred_element_type=F32,
    )
    dgain_ref[...] = sums[:1] / gain[...]


def arrange_body(ids, qkv, dgain, dgain_moe, *refs):
    ghb, mixed = refs[:4], refs[4:8]
    near_ref, far_ref, out = refs[8:]
    out[...] = sum(dot(ghb[x][...], mixed[x][...], 0, 0) for x in range(4)).astype(BF16)
    rows = [v[:, i * 128 : i * 128 + 128] for v in (dgain[...], dgain_moe[...]) for i in range(8)]
    gains = jnp.concatenate(rows + [jnp.zeros((16, 128), F32)], 0).astype(BF16)
    for y in range(4):
        for z in range(4):
            near_ref[z, y, :, OWN:] = gains
            far_ref[z, y, :, OWN:] = gains
            for xh in range(2):
                row = d_block(y ^ ids[0], xh, z ^ ids[1]) * 32
                for dst, c in ((near_ref, ids[2]), (far_ref, 1 - ids[2])):
                    rows = pl.ds(pl.multiple_of(row + c * 16, 16), 16)
                    dst[z, y, xh * 16 : xh * 16 + 16, :256] = out[rows, :]
                    dst[z, y, xh * 16 : xh * 16 + 16, 256:OWN] = qkv[rows, :]


def tokens_back_body(gn1, z, p1, p3, tokens, gain, gh, hidden, out_ref, grad_ref):
    total = p1[...].astype(F32) + p3[...].astype(F32)
    out_ref[...] = (hidden[...] + z[...].astype(F32) + total[256:]).astype(BF16)
    x = tokens[...].astype(F32)
    r1 = lax.rsqrt(jnp.mean(x * x, -1, keepdims=True) + EPSILON)
    w1 = (gn1[...].astype(F32) + total[:256]) * gain[...]
    grad_ref[...] = (
        gh[...] + r1 * w1 - x * (r1 * r1 * r1) * jnp.mean(w1 * x, -1, keepdims=True)
    ).astype(BF16)


def rotary_tables(xl):
    frequency = THETA ** (-2.0 * jnp.arange(HD // 2, dtype=F32) / HD)
    place = jnp.arange(512)
    place = ((place // 256) ^ xl) * 256 + place % 256
    angles = place.astype(F32)[:, None] * frequency[None, :]
    cos, sin = jnp.cos(angles), jnp.sin(angles)
    return jnp.concatenate([cos] * 8, 1), jnp.concatenate([-sin, sin] * 4, 1)


def last_send_body(ids, s0, s1, s2, s3, near, far, own_ref, gain_ref, p1, p2, p3, total):
    total[...] = s0[...].astype(F32) + s1[...].astype(F32) + s2[...].astype(F32) + s3[...].astype(F32)
    own = pl.ds(pl.multiple_of(ids[3] * 16, 16), 16)
    other = pl.ds(pl.multiple_of((1 - ids[3]) * 16, 16), 16)
    gains = total[:16, OWN:]
    gain_ref[...] = gains
    own_ref[...] = total[own, :OWN]
    base = 2 * 3 * LOCAL_E * 16
    for x, p in ((1, p1), (2, p2), (3, p3)):
        for m in range(3):
            for e in range(LOCAL_E):
                row = (m * LOCAL_E + e) * 16
                p[row : row + 16, :] = near[0, x, m, e]
                p[base // 2 + row : base // 2 + row + 16, :] = far[1, x, m, e]
        p[base : base + 16, :] = jnp.concatenate([gains, gains], 1).astype(BF16)
    for j in range(4):
        part = total[other, j * 256 : j * 256 + 256]
        p2[base + 16 + j * 16 : base + 32 + j * 16, :] = part.astype(BF16)


def last_body(ids, own, own_gains, g1, g2, g3, near, far, do, dq, dk, dv, gain_ref, *experts):
    c, xh, xl = ids[2], ids[3], ids[4]
    base = 2 * 3 * LOCAL_E * 16
    mine = pl.ds(pl.multiple_of(xh * 256, 256), 256)
    theirs = pl.ds(pl.multiple_of((1 - xh) * 256, 256), 256)
    for j, d in enumerate((do, dq, dk, dv)):
        d[:, mine] = own[:, j * 256 : j * 256 + 256]
        d[:, theirs] = g2[base + 16 + j * 16 : base + 32 + j * 16, :].astype(F32)
    gain_ref[...] = own_gains[...] + sum(g[base : base + 16, :128].astype(F32) for g in (g1, g2, g3))
    for x in range(4):
        for b in range(2):
            owner = (c ^ b) * 4 + (xh ^ (x // 2)) * 2 + (xl ^ (x % 2))
            for m, d in enumerate(experts):
                for e in range(LOCAL_E):
                    row = ((b * 3 + m) * LOCAL_E + e) * 16
                    if x == 0:
                        block = near[0, 0, m, e] if b == 0 else far[1, 0, m, e]
                    else:
                        block = (g1, g2, g3)[x - 1][row : row + 16, :]
                    d[owner * LOCAL_E + e] = block.astype(F32)


def route_rows(routes, route_weights, xl):
    high = lax.reduce_precision(route_weights, 8, 7)
    low = lax.reduce_precision(route_weights - high, 8, 7)
    table = jnp.concatenate([routes.T.astype(F32), high.T, low.T], 0).reshape(24, 2, 256)
    table = jnp.where(xl == 1, table[:, 1], table[:, 0])
    return jnp.pad(table.astype(BF16), ((0, 40), (0, 0))).reshape(16, 1024)


def route_tables(near, far, c, xh, xl):
    tables = jnp.concatenate([near, far], 0).reshape(8, 64, 256)[:, :24].astype(F32)
    tables = tables.reshape(4, 2, 24, 256).transpose(0, 2, 1, 3).reshape(4, 24, 512)
    first = ((c * 4 + xh * 2 + xl) * LOCAL_E).astype(F32)
    names = first + jnp.arange(LOCAL_E, dtype=F32)
    match = tables[None, :, :8, :] == names[:, None, None, None]
    shares = tables[:, 8:16] + tables[:, 16:]
    share = jnp.sum(jnp.where(match, shares[None], 0.0), 2)
    named = jnp.any(match, 2)
    before = (jnp.arange(512)[:, None] <= jnp.arange(512)[None, :]).astype(BF16)
    count = jnp.dot(named.astype(BF16), before, preferred_element_type=F32)
    rank = jnp.where(named, count.astype(jnp.int32) - 1, -1)
    return rank, share


def on_device(
    tokens,
    gain_attn,
    w_query,
    w_key,
    w_value,
    w_out,
    gain_moe,
    w_gate,
    w_up,
    w_down,
    routes,
    route_weights,
    cotangent,
):
    y, xh, z, c, xl = (lax.axis_index(a) for a in ("y", "xh", "z", "c", "xl"))
    ids = jnp.stack([y, z, c, xh, xl]).astype(jnp.int32)
    gain_attn = gain_attn.reshape(1, 1024)
    gain_moe = gain_moe.reshape(1, 1024)

    heads = jnp.stack([w_query, w_key, w_value], 1).reshape(16, 3, 2, 256)
    heads = flip(heads, 2, xh)
    w_o = w_out.T.reshape(16, 2, 256)
    for_same, for_other = flip(w_o, 1, xh).reshape(16, 512), flip(w_o, 1, 1 - xh).reshape(16, 512)
    for_2 = jnp.concatenate([for_other, heads[:, :, 1].reshape(16, 768)], 1)
    local = jnp.stack([w_gate, w_up, jnp.swapaxes(w_down, 1, 2)])
    local = local.reshape(3, 2, 2, 2, LOCAL_E, 16, 256)
    local = flip(flip(flip(local, 1, c), 2, xh), 3, xl).transpose(1, 2, 3, 0, 4, 5, 6)
    local = local.reshape(2, 4, 3, LOCAL_E, 16, 256)
    near, far = local[0], local[1]

    got_2, got_1, got_3 = together(swap_x(for_2, 2), swap_x(for_same, 1), swap_x(for_other, 3))
    far = swap_c(far)
    here = jnp.concatenate([for_same, got_1, heads[:, :, 0].reshape(16, 768)], 1)
    there = jnp.concatenate([got_2[:, :512], got_3, got_2[:, 512:]], 1)
    rows = flip(jnp.stack([here, there]), 0, xh).reshape(32, PACKED)
    both = [flip(jnp.stack([near[x], far[x]], 2), 2, c) for x in range(4)]
    sent = jnp.concatenate([tokens, route_rows(routes, route_weights, xl)], 0)
    rows, sent = together(rows, sent)

    moved = together(
        *[swap_4(rows, "z", k) for k in (1, 2, 3)], *[swap_x(both[x], x) for x in (1, 2, 3)]
    )
    owned = [both[0], *moved[3:]]
    owned = jnp.stack([jnp.concatenate(owned[:2], -1), jnp.concatenate(owned[2:], -1)])
    owned = flip(owned, 0, xh).reshape(2, 3, LOCAL_E, 32, 512)
    experts = lax.all_gather(owned, ("y", "z"), axis=0)
    zs_o = jnp.stack([rows[:, :OUT], *[m[:, :OUT] for m in moved[:3]]])
    zs = jnp.stack([rows[:, OUT:], *[m[:, OUT:] for m in moved[:3]]])
    zs, zs_o, sent, owned = together(zs, zs_o, sent, owned)

    *moved, t1, t3, cos, sin = together(
        *[swap_4(zs, "y", k) for k in (1, 2, 3)],
        swap_x(sent, 1),
        swap_x(sent, 3),
        *rotary_tables(xl),
    )
    half = kernel_call(assemble_body, [ids, zs, *moved], (shape(512, QKV),), "assemble", smem=1)
    half, zs_o, sent, t1, t3 = together(half[0], zs_o, sent, t1, t3)
    moved_o = [swap_4(zs_o, "y", k) for k in (1, 2, 3)]
    other_half, t2 = together(swap_c(half), swap_x(sent, 2))
    blocks = [sent, t1, t2, t3]
    near = jnp.stack([t[256:] for t in blocks])
    other_half, near, cot = together(other_half, near, cotangent)
    ct_1, ct_3 = swap_x(cot, 1), swap_x(cot, 3)

    n1, qkv, w_qkv, *mixed = kernel_call(
        attend_body,
        [ids, *blocks, gain_attn, half, other_half, cos, sin],
        (shape(2, 512, 1024), shape(2, 512, QKV), shape(1024, QKV)) + (shape(256, 256),) * 4,
        "attend",
        smem=1,
        flops=8e9,
    )
    *mixed, ct_1, ct_3, near, cot, moved_o[0], moved_o[1], moved_o[2] = together(
        *mixed, ct_1, ct_3, near, cot, *moved_o
    )
    half = kernel_call(assemble_body, [ids, zs_o, *moved_o], (shape(512, OUT),), "assemble", smem=1)
    other_half, cot, *moved = together(
        swap_c(half[0]), cot, *[swap_x(mixed[x], x) for x in (1, 2, 3)]
    )
    ct_2 = [swap_x(ct_3[:128], 1), swap_x(ct_1[128:], 3)]
    hidden, n2, w_o_full = kernel_call(
        project_body,
        [ids, tokens, gain_moe, mixed[0], *moved, half[0], other_half],
        (shape(256, 1024, dtype=F32), shape(256, 1024), shape(1024, OUT)),
        "project",
        scratch=[pltpu.VMEM((256, OUT), BF16)],
        smem=1,
    )
    n2, *ct_2 = together(n2, *ct_2)
    ct_three = jnp.stack([ct_1, jnp.concatenate(ct_2, 0), ct_3])
    n2_1, n2_3, n2_far, far = together(swap_x(n2, 1), swap_x(n2, 3), swap_c(n2), swap_c(near))
    n2, n2_1, n2_3, ct_three = together(n2, n2_1, n2_3, ct_three)
    rank, share = route_tables(near, far, c, xh, xl)
    n2_2, ct_far, n2_far_1, n2_far_3, rank, share = together(
        swap_x(n2, 2), swap_c(ct_three), swap_c(n2_1), swap_c(n2_3), rank, share
    )
    n2_all = [n2, n2_1, n2_2, n2_3, n2_far, n2_far_1, swap_c(n2_2), n2_far_3]
    ct_all = [cot, ct_three, swap_c(cot), ct_far]
    z_near, z_far, g_near, g_far, grads = run_experts(ids, n2_all, ct_all, rank, share, experts)
    reduced = lax.psum_scatter(grads, ("y", "z"), scatter_dimension=0)
    g_far, z_far = together(swap_c(g_far), z_far)
    g_sums = [add(g_near[x], g_far[x]).astype(BF16) for x in range(4)]
    *g_sums, z_far = together(*g_sums, z_far)
    z_far = swap_c(z_far)
    gn2_1, gn2_3, z_far = together(swap_x(g_sums[1], 1), swap_x(g_sums[3], 3), z_far)
    gn2_2 = swap_x(g_sums[2], 2)
    gn2 = [g_sums[0], gn2_1, gn2_2, gn2_3]
    gh, ghb, *gm, dgain_moe = kernel_call(
        hidden_back_body,
        [*gn2, hidden, cotangent, gain_moe, w_o_full],
        (shape(256, 1024, dtype=F32), shape(256, 1024))
        + (shape(256, 256),) * 4
        + (shape(1, 1024, dtype=F32),),
        "hidden_back",
    )
    moved = together(*[swap_x(gm[x], x) for x in (1, 2, 3)])
    gm = [gm[0], *moved]
    ghb, *gm = together(ghb, *gm)
    ghb = [ghb, swap_x(ghb, 1), swap_x(ghb, 2), swap_x(ghb, 3)]
    g, *parts = kernel_call(
        attend_back_body,
        [qkv, *gm, cos, sin, w_qkv, z_near, z_far],
        (shape(2, 512, QKV),) + (shape(256, 1024),) * 8,
        "attend_back",
        flops=10e9,
    )
    g, *parts = together(g, *parts)
    gn1, z_sums = parts[:4], parts[4:]
    via_1, via_3 = swap_x(gn1[2], 1), swap_x(z_sums[2], 3)
    qkv_grad, dgain_attn = kernel_call(
        attend_grad_body,
        [n1, g, w_qkv, gain_attn],
        (shape(1024, QKV), shape(1, 1024, dtype=F32)),
        "attend_grad",
        flops=4e9,
    )
    qkv_grad, *ghb[1:] = together(qkv_grad, *ghb[1:])
    near, far = kernel_call(
        arrange_body,
        [ids, qkv_grad, dgain_attn, dgain_moe, *ghb, *mixed],
        (shape(4, 4, 32, OWN + SPARE),) * 2,
        "arrange",
        scratch=[pltpu.VMEM((1024, 256), BF16)],
        smem=1,
    )
    sums = add(near, swap_c(far)).astype(BF16)
    moved = [swap_4(sums[k], "z", k) for k in (1, 2, 3)]
    moved[0], via_1, via_3 = together(moved[0], via_1, via_3)
    part_1 = jnp.concatenate([gn1[1], add(z_sums[1], via_3).astype(BF16)], 0)
    part_3 = jnp.concatenate([add(gn1[3], via_1).astype(BF16), z_sums[3]], 0)
    part_1, part_3 = swap_x(part_1, 1), swap_x(part_3, 3)
    sums = add(sums[0], *moved).astype(BF16)
    sums, reduced = together(sums, reduced)
    *moved, back_far = together(*[swap_4(sums[k], "y", k) for k in (1, 2, 3)], swap_c(reduced))
    sent_rows = 2 * 3 * LOCAL_E * 16
    own, own_gains, *sent = kernel_call(
        last_send_body,
        [ids, sums[0], *moved, reduced, back_far],
        (
            shape(16, OWN, dtype=F32),
            shape(16, 128, dtype=F32),
            shape(sent_rows + 16, 256),
            shape(sent_rows + 80, 256),
            shape(sent_rows + 16, 256),
        ),
        "last_send",
        scratch=[pltpu.VMEM((32, OWN + SPARE), F32)],
        smem=1,
    )
    *sent, part_1, part_3 = together(*sent, part_1, part_3)
    output, grad_tokens = kernel_call(
        tokens_back_body,
        [gn1[0], z_sums[0], part_1, part_3, tokens, gain_attn, gh, hidden],
        (shape(256, 1024),) * 2,
        "tokens_back",
    )
    *got, output, grad_tokens = together(
        *[swap_x(sent[x - 1], x) for x in (1, 2, 3)], output, grad_tokens
    )
    d_out, d_query, d_key, d_value, gains, d_gate, d_up, d_down = kernel_call(
        last_body,
        [ids, own, own_gains, *got, reduced, back_far],
        (shape(16, 512, dtype=F32),) * 4
        + (shape(16, 128, dtype=F32),)
        + (shape(8 * LOCAL_E, 16, 256, dtype=F32),) * 3,
        "last",
        smem=1,
    )
    gains = gains.reshape(2, 1024)
    return (
        output,
        grad_tokens,
        gains[0],
        d_query,
        d_key,
        d_value,
        d_out.T,
        gains[1],
        d_gate,
        d_up,
        jnp.swapaxes(d_down, 1, 2),
    )


def solution(mesh):
    split = Mesh(mesh.devices.reshape(4, 2, 4, 2, 2), ("y", "xh", "z", "c", "xl"))
    dp = ("y", "xh", "z", "c")
    rows = P((*dp, "xl"), None)
    outs = (
        rows,
        rows,
        P(),
        P(dp, "xl"),
        P(dp, "xl"),
        P(dp, "xl"),
        P("xl", dp),
        P(),
        P(None, dp, "xl"),
        P(None, dp, "xl"),
        P(None, "xl", dp),
    )
    ins = (
        rows,
        P(),
        P(dp, "xl"),
        P(dp, "xl"),
        P(dp, "xl"),
        P("xl", dp),
        P(),
        P(None, dp, "xl"),
        P(None, dp, "xl"),
        P(None, "xl", dp),
        P(dp, None),
        P(dp, None),
        rows,
    )
    return jax.shard_map(on_device, mesh=split, in_specs=ins, out_specs=outs, check_vma=False)
```

```python
import jax
import jax.numpy as jnp
from jax import lax
from jax.experimental import pallas as pl
from jax.experimental.pallas import tpu as pltpu
from jax.sharding import Mesh
from jax.sharding import PartitionSpec as P

HD = 64
CAP = 160
EPSILON = 1e-06
THETA = 10000.0
LOCAL_E = 4
F32 = jnp.float32
BF16 = jnp.bfloat16
VMEM_BYTES = 60 * 1024 * 1024
SMALL_VMEM_BYTES = 32 * 1024 * 1024


def swap_x(value, bits):
    return lax.ppermute(value, ("xh", "xl"), [(i, i ^ bits) for i in range(4)])


def swap_c(value):
    return lax.ppermute(value, "c", [(0, 1), (1, 0)])


def swap_4(value, axis, bits):
    return lax.ppermute(value, axis, [(i, i ^ bits) for i in range(4)])


def after(value, *others):
    return lax.optimization_barrier((value, others))[0]


def together(*values):
    return lax.optimization_barrier(values)


def flip(value, axis, bit):
    return jnp.where(bit == 1, jnp.flip(value, axis), value)


def add(*terms):
    return sum(t.astype(F32) for t in terms)


def dot(a, b, ca, cb):
    return lax.dot_general(a, b, (((ca,), (cb,)), ((), ())), preferred_element_type=F32)


def whole(n):
    return [pl.BlockSpec(memory_space=pltpu.VMEM)] * n


def cost(flops, nbytes):
    return pl.CostEstimate(flops=int(flops), bytes_accessed=int(nbytes), transcendentals=0)


def kernel_call(body, ins, outs, name, scratch=(), smem=0, flops=1e9):
    specs = [pl.BlockSpec(memory_space=pltpu.SMEM)] * smem + whole(len(ins) - smem)
    nbytes = sum(v.size * v.dtype.itemsize for v in (*ins, *outs))
    return pl.pallas_call(
        body,
        out_shape=outs,
        in_specs=specs,
        out_specs=whole(len(outs)),
        scratch_shapes=list(scratch),
        compiler_params=pltpu.CompilerParams(vmem_limit_bytes=SMALL_VMEM_BYTES),
        cost_estimate=cost(flops, nbytes),
        name=name,
    )(*ins)


def shape(*dims, dtype=BF16):
    return jax.ShapeDtypeStruct(dims, dtype)


OUT, QKV, SPARE = 1024, 768, 128
PACKED = OUT + QKV
OWN = 256 + QKV


def d_block(y, xh, z):
    return (y * 2 + xh) * 4 + z


def assemble_body(ids, p0, p1, p2, p3, half_ref):
    for y, piece in enumerate((p0, p1, p2, p3)):
        for z in range(4):
            for xh in range(2):
                row = d_block(y ^ ids[0], xh, z ^ ids[1]) * 16
                rows = pl.ds(pl.multiple_of(row, 16), 16)
                half_ref[rows, :] = piece[z, xh * 16 : xh * 16 + 16, :]


def interleave(ids, own, other, dst):
    for half, c in ((own, ids[2]), (other, 1 - ids[2])):
        for n in range(32):
            rows = pl.ds(pl.multiple_of(n * 32 + c * 16, 16), 16)
            dst[rows, :] = half[n * 16 : n * 16 + 16, :]


def rotated(v, cos, sin):
    lane = lax.broadcasted_iota(jnp.int32, v.shape, 1)
    width = v.shape[1]
    other = jnp.where(lane % HD < HD // 2, pltpu.roll(v, width - 32, 1), pltpu.roll(v, 32, 1))
    return v * cos + other * sin


def attend_body(ids, t0, t1, t2a, t2b, t3, gain, own, other, cos_ref, sin_ref, *outs):
    n1_ref, qkv_ref, w_ref, p_ref = outs[:4]
    outs = outs[4:]
    tokens = [(t0.at[:256],), (t1.at[:256],), (t2a, t2b.at[:112]), (t3.at[:256],)]
    cos, sin = cos_ref[...], sin_ref[...]
    interleave(ids, own, other, w_ref)
    for s in range(2):
        for half in range(2):
            x = jnp.concatenate([t[...] for t in tokens[2 * s + half]], 0).astype(F32)
            r1 = lax.rsqrt(jnp.mean(x * x, -1, keepdims=True) + EPSILON)
            n1_ref[s, half * 256 : half * 256 + 256, :] = (x * r1 * gain[...]).astype(BF16)
        proj = jnp.dot(n1_ref[s], w_ref[...], preferred_element_type=F32)
        q = rotated(proj[:, :256], cos, sin).astype(BF16)
        k = rotated(proj[:, 256:512], cos, sin).astype(BF16)
        v = proj[:, 512:].astype(BF16)
        qkv_ref[s, :, :256] = q
        qkv_ref[s, :, 256:512] = k
        qkv_ref[s, :, 512:] = v
        mixed = []
        for h in range(4):
            cols = slice(h * HD, h * HD + HD)
            scores = dot(q[:, cols], k[:, cols], 1, 1) * (HD**-0.5)
            e = jnp.exp(scores - jnp.max(scores, -1, keepdims=True))
            p = (e / jnp.sum(e, -1, keepdims=True)).astype(BF16)
            p_ref[s, h] = p
            mixed.append(dot(p, v[:, cols], 1, 0).astype(BF16))
        out = jnp.concatenate(mixed, 1)
        outs[2 * s][...] = out[:256]
        outs[2 * s + 1][...] = out[256:]


def out_columns(x):
    block = (x % 2) * 2 + x // 2
    return slice(block * 256, block * 256 + 256)


def project_body(ids, tokens, gain, m0, m1, m2, m3, own, other, hidden_ref, n2_ref, wo_ref, mixed_ref):
    interleave(ids, own, other, wo_ref)
    for x, m in enumerate((m0, m1, m2, m3)):
        mixed_ref[:, out_columns(x)] = m[...]
    hidden = tokens[...].astype(F32) + dot(mixed_ref[...], wo_ref[...], 1, 1)
    hidden_ref[...] = hidden
    r2 = lax.rsqrt(jnp.mean(hidden * hidden, -1, keepdims=True) + EPSILON)
    n2_ref[...] = (hidden * r2 * gain[...]).astype(BF16)


def expert_pieces():
    for y in range(4):
        for z in range(4):
            for xh in range(2):
                row = d_block(y, xh, z) * 32
                yield (y * 4 + z, xh), slice(row, row + 32)


def relative_pieces(ids):
    for y in range(4):
        for z in range(4):
            for c in range(2):
                for x in range(4):
                    row = d_block(y, (x // 2) ^ ids[3], z) * 32 + (c ^ ids[2]) * 16
                    rows = pl.ds(pl.multiple_of(row, 16), 16)
                    yield (y * 4 + z, c, x), rows, slice((x % 2) * 256, (x % 2) * 256 + 256)


def expert_body(*refs):
    ids, n2 = refs[0], refs[1:9]
    ct = [r.at[x] for r in refs[9:11] for x in range(4)]
    rank_ref, share_ref, w_ref = refs[11:14]
    z_near, z_far, g_near, g_far, dw_ref = refs[14:19]
    wg, wu, wd, x_s, gz_s, p_s, z_s, gx_s = refs[19:]
    e = pl.program_id(0)
    there = pl.ds(pl.multiple_of(e * CAP, 32), CAP)
    for piece, d in expert_pieces():
        wg[d, :] = w_ref[*piece, 0, 0]
        wu[d, :] = w_ref[*piece, 1, 0]
        wd[d, :] = w_ref[*piece, 2, 0]
    shares = []
    slot = lax.broadcasted_iota(jnp.int32, (CAP, 512), 0)
    for s in range(4):
        hit = slot == rank_ref[0, s : s + 1, :]
        share = jnp.sum(jnp.where(hit, share_ref[0, s : s + 1, :], 0.0), 1, keepdims=True)
        shares.append(share)
        p = hit.astype(F32).astype(BF16)
        p_s[s, there, :] = p
        here = slice(s * CAP, s * CAP + CAP)
        x_s[here, :] = (
            dot(p[:, :256], n2[2 * s][...], 1, 0) + dot(p[:, 256:], n2[2 * s + 1][...], 1, 0)
        ).astype(BF16)
        gz_s[here, :] = (
            (dot(p[:, :256], ct[2 * s][...], 1, 0) + dot(p[:, 256:], ct[2 * s + 1][...], 1, 0))
            * share
        ).astype(BF16)
    share = jnp.concatenate(shares, 0)
    a = dot(x_s[...], wg[...], 1, 0)
    b = dot(x_s[...], wu[...], 1, 0)
    sig = 1.0 / (1.0 + jnp.exp(-a))
    sa = a * sig
    u = (sa * b).astype(BF16)
    gu = dot(gz_s[...], wd[...], 1, 0)
    ga = (gu * b * sig * (1.0 + a * (1.0 - sig))).astype(BF16)
    gb = (gu * sa).astype(BF16)
    z = (dot(u, wd[...], 1, 1) * share).astype(BF16)
    gx = (dot(ga, wg[...], 1, 1) + dot(gb, wu[...], 1, 1)).astype(BF16)
    for s in range(4):
        here = slice(s * CAP, s * CAP + CAP)
        z_s[s, there, :] = z[here]
        gx_s[s, there, :] = gx[here]
    for m, (left, right) in enumerate(((x_s, ga), (x_s, gb), (gz_s, u))):
        wg[...] = dot(left[...], right, 0, 0).astype(BF16)
        for piece, rows, cols in relative_pieces(ids):
            dw_ref[*piece, m, 0] = wg[rows, cols]

    @pl.when(e == LOCAL_E - 1)
    def _():
        for s in range(4):
            for src, near, far in ((z_s, z_near, z_far), (gx_s, g_near, g_far)):
                total = dot(p_s[s], src[s], 0, 0).astype(BF16)
                dst = near if s < 2 else far
                dst[2 * (s % 2)] = total[:256]
                dst[2 * (s % 2) + 1] = total[256:]


W_BLOCK = (16, 2, 3, 1, 32, 512)


def run_experts(ids, n2, ct, rank, share, weights):
    table = pl.BlockSpec((1, 4, 512), lambda e: (e, 0, 0))
    w_spec = pl.BlockSpec(W_BLOCK, lambda e: (0, 0, 0, e, 0, 0))
    dw_spec = pl.BlockSpec((16, 2, 4, 3, 1, 16, 256), lambda e: (0, 0, 0, 0, e, 0, 0))
    blocks = shape(4, 256, 1024)
    return pl.pallas_call(
        expert_body,
        grid=(LOCAL_E,),
        out_shape=(blocks,) * 4 + (shape(16, 2, 4, 3, LOCAL_E, 16, 256),),
        in_specs=[pl.BlockSpec(memory_space=pltpu.SMEM)] + whole(10) + [table, table, w_spec],
        out_specs=whole(4) + [dw_spec],
        scratch_shapes=[
            pltpu.VMEM((1024, 512), BF16),
            pltpu.VMEM((1024, 512), BF16),
            pltpu.VMEM((1024, 512), BF16),
            pltpu.VMEM((4 * CAP, 1024), BF16),
            pltpu.VMEM((4 * CAP, 1024), BF16),
            pltpu.VMEM((4, LOCAL_E * CAP, 512), BF16),
            pltpu.VMEM((4, LOCAL_E * CAP, 1024), BF16),
            pltpu.VMEM((4, LOCAL_E * CAP, 1024), BF16),
        ],
        compiler_params=pltpu.CompilerParams(vmem_limit_bytes=VMEM_BYTES),
        cost_estimate=cost(36e9, 60e6),
        name="experts",
    )(ids, *n2, *ct, rank, share, weights)


def hidden_back_body(g0, g1, g2, g3, hidden_ref, ct, gain, wo, gh_ref, ghb_ref, m0, m1, m2, m3, dgain_ref):
    gn2 = g0[...].astype(F32) + g1[...].astype(F32) + g2[...].astype(F32) + g3[...].astype(F32)
    hidden = hidden_ref[...]
    r2 = lax.rsqrt(jnp.mean(hidden * hidden, -1, keepdims=True) + EPSILON)
    w2 = gn2 * gain[...]
    gh = ct[...].astype(F32) + r2 * w2 - hidden * (r2 * r2 * r2) * jnp.mean(w2 * hidden, -1, keepdims=True)
    gh_ref[...] = gh
    ghb = gh.astype(BF16)
    ghb_ref[...] = ghb
    gm = dot(ghb, wo[...], 1, 0).astype(BF16)
    for x, m in enumerate((m0, m1, m2, m3)):
        m[...] = gm[:, out_columns(x)]
    dgain_ref[...] = jnp.sum(gn2 * hidden * r2, 0, keepdims=True)


def attend_back_body(qkv, p_ref, m0, m1, m2, m3, cos_ref, sin_ref, w_ref, z_near, z_far, g_ref, *outs):
    gm_refs = (m0, m1, m2, m3)
    cos, sin = cos_ref[...], -sin_ref[...]
    for s in range(2):
        gm = jnp.concatenate([gm_refs[2 * s][...], gm_refs[2 * s + 1][...]], 0)
        gqs, gks, gvs = [], [], []
        for h in range(4):
            q = qkv[s, :, h * HD : h * HD + HD]
            k = qkv[s, :, 256 + h * HD : 256 + h * HD + HD]
            v = qkv[s, :, 512 + h * HD : 512 + h * HD + HD]
            gmh = gm[:, h * HD : h * HD + HD]
            p = p_ref[s, h].astype(F32)
            gp = dot(gmh, v, 1, 1)
            gs = (p * (gp - jnp.sum(gp * p, -1, keepdims=True))).astype(BF16)
            gqs.append(dot(gs, k, 1, 0) * (HD**-0.5))
            gks.append(dot(gs, q, 0, 0) * (HD**-0.5))
            gvs.append(dot(p_ref[s, h], gmh, 0, 0))
        g_ref[s, :, :256] = rotated(jnp.concatenate(gqs, 1), cos, sin).astype(BF16)
        g_ref[s, :, 256:512] = rotated(jnp.concatenate(gks, 1), cos, sin).astype(BF16)
        g_ref[s, :, 512:] = jnp.concatenate(gvs, 1).astype(BF16)
        part = dot(g_ref[s], w_ref[...], 1, 1).astype(BF16)
        for half in range(2):
            x = 2 * s + half
            outs[x][...] = part[half * 256 : half * 256 + 256]
            outs[4 + x][...] = (z_near[x].astype(F32) + z_far[x].astype(F32)).astype(BF16)


def attend_grad_body(n1, g, w_qkv, gain, grad_ref, dgain_ref):
    qkv = dot(n1[0], g[0], 0, 0) + dot(n1[1], g[1], 0, 0)
    grad_ref[...] = qkv.astype(BF16)
    weighted = qkv * w_qkv[...].astype(F32)
    ones = jnp.ones((8, QKV), F32)
    sums = lax.dot_general(
        ones,
        weighted,
        (((1,), (1,)), ((), ())),
        precision=lax.Precision.HIGHEST,
        preferred_element_type=F32,
    )
    dgain_ref[...] = sums[:1] / gain[...]


def arrange_body(ids, qkv, dgain, dgain_moe, *refs):
    ghb, mixed = refs[:4], refs[4:8]
    near_ref, far_ref, out = refs[8:]
    out[...] = sum(dot(ghb[x][...], mixed[x][...], 0, 0) for x in range(4)).astype(BF16)
    rows = [v[:, i * 128 : i * 128 + 128] for v in (dgain[...], dgain_moe[...]) for i in range(8)]
    gains = jnp.concatenate(rows + [jnp.zeros((16, 128), F32)], 0).astype(BF16)
    for y in range(4):
        for z in range(4):
            near_ref[z, y, :, OWN:] = gains
            far_ref[z, y, :, OWN:] = gains
            for xh in range(2):
                row = d_block(y ^ ids[0], xh, z ^ ids[1]) * 32
                for dst, c in ((near_ref, ids[2]), (far_ref, 1 - ids[2])):
                    rows = pl.ds(pl.multiple_of(row + c * 16, 16), 16)
                    dst[z, y, xh * 16 : xh * 16 + 16, :256] = out[rows, :]
                    dst[z, y, xh * 16 : xh * 16 + 16, 256:OWN] = qkv[rows, :]


def tokens_back_body(gn1, z, p1, p3, tokens, gain, gh, hidden, out_ref, grad_ref):
    total = p1[...].astype(F32) + p3[...].astype(F32)
    out_ref[...] = (hidden[...] + z[...].astype(F32) + total[256:]).astype(BF16)
    x = tokens[...].astype(F32)
    r1 = lax.rsqrt(jnp.mean(x * x, -1, keepdims=True) + EPSILON)
    w1 = (gn1[...].astype(F32) + total[:256]) * gain[...]
    grad_ref[...] = (
        gh[...] + r1 * w1 - x * (r1 * r1 * r1) * jnp.mean(w1 * x, -1, keepdims=True)
    ).astype(BF16)


def rotary_tables(xl):
    frequency = THETA ** (-2.0 * jnp.arange(HD // 2, dtype=F32) / HD)
    place = jnp.arange(512)
    place = ((place // 256) ^ xl) * 256 + place % 256
    angles = place.astype(F32)[:, None] * frequency[None, :]
    cos, sin = jnp.cos(angles), jnp.sin(angles)
    return jnp.concatenate([cos] * 8, 1), jnp.concatenate([-sin, sin] * 4, 1)


def last_send_body(ids, s0, s1, s2, s3, near, far, own_ref, gain_ref, p1, p2, p3, total):
    total[...] = s0[...].astype(F32) + s1[...].astype(F32) + s2[...].astype(F32) + s3[...].astype(F32)
    own = pl.ds(pl.multiple_of(ids[3] * 16, 16), 16)
    other = pl.ds(pl.multiple_of((1 - ids[3]) * 16, 16), 16)
    gains = total[:16, OWN:]
    gain_ref[...] = gains
    own_ref[...] = total[own, :OWN]
    base = 2 * 3 * LOCAL_E * 16
    for x, p in ((1, p1), (2, p2), (3, p3)):
        for m in range(3):
            for e in range(LOCAL_E):
                row = (m * LOCAL_E + e) * 16
                p[row : row + 16, :] = near[0, x, m, e]
                p[base // 2 + row : base // 2 + row + 16, :] = far[1, x, m, e]
        p[base : base + 16, :] = jnp.concatenate([gains, gains], 1).astype(BF16)
    for j in range(4):
        part = total[other, j * 256 : j * 256 + 256]
        p2[base + 16 + j * 16 : base + 32 + j * 16, :] = part.astype(BF16)


def last_body(ids, own, own_gains, g1, g2, g3, near, far, do, dq, dk, dv, gain_ref, *experts):
    c, xh, xl = ids[2], ids[3], ids[4]
    base = 2 * 3 * LOCAL_E * 16
    mine = pl.ds(pl.multiple_of(xh * 256, 256), 256)
    theirs = pl.ds(pl.multiple_of((1 - xh) * 256, 256), 256)
    for j, d in enumerate((do, dq, dk, dv)):
        d[:, mine] = own[:, j * 256 : j * 256 + 256]
        d[:, theirs] = g2[base + 16 + j * 16 : base + 32 + j * 16, :].astype(F32)
    gain_ref[...] = own_gains[...] + sum(g[base : base + 16, :128].astype(F32) for g in (g1, g2, g3))
    for x in range(4):
        for b in range(2):
            owner = (c ^ b) * 4 + (xh ^ (x // 2)) * 2 + (xl ^ (x % 2))
            for m, d in enumerate(experts):
                for e in range(LOCAL_E):
                    row = ((b * 3 + m) * LOCAL_E + e) * 16
                    if x == 0:
                        block = near[0, 0, m, e] if b == 0 else far[1, 0, m, e]
                    else:
                        block = (g1, g2, g3)[x - 1][row : row + 16, :]
                    d[owner * LOCAL_E + e] = block.astype(F32)


def route_rows(routes, route_weights, xl):
    high = lax.reduce_precision(route_weights, 8, 7)
    low = lax.reduce_precision(route_weights - high, 8, 7)
    table = jnp.concatenate([routes.T.astype(F32), high.T, low.T], 0).reshape(24, 2, 256)
    table = jnp.where(xl == 1, table[:, 1], table[:, 0])
    return jnp.pad(table.astype(BF16), ((0, 40), (0, 0))).reshape(16, 1024)


def route_tables(near, far, c, xh, xl):
    tables = jnp.concatenate([near, far], 0).reshape(8, 64, 256)[:, :24].astype(F32)
    tables = tables.reshape(4, 2, 24, 256).transpose(0, 2, 1, 3).reshape(4, 24, 512)
    first = ((c * 4 + xh * 2 + xl) * LOCAL_E).astype(F32)
    names = first + jnp.arange(LOCAL_E, dtype=F32)
    match = tables[None, :, :8, :] == names[:, None, None, None]
    shares = tables[:, 8:16] + tables[:, 16:]
    share = jnp.sum(jnp.where(match, shares[None], 0.0), 2)
    named = jnp.any(match, 2)
    before = (jnp.arange(512)[:, None] <= jnp.arange(512)[None, :]).astype(BF16)
    count = jnp.dot(named.astype(BF16), before, preferred_element_type=F32)
    rank = jnp.where(named, count.astype(jnp.int32) - 1, -1)
    return rank, share


def on_device(
    tokens,
    gain_attn,
    w_query,
    w_key,
    w_value,
    w_out,
    gain_moe,
    w_gate,
    w_up,
    w_down,
    routes,
    route_weights,
    cotangent,
):
    y, xh, z, c, xl = (lax.axis_index(a) for a in ("y", "xh", "z", "c", "xl"))
    ids = jnp.stack([y, z, c, xh, xl]).astype(jnp.int32)
    gain_attn = gain_attn.reshape(1, 1024)
    gain_moe = gain_moe.reshape(1, 1024)

    heads = jnp.stack([w_query, w_key, w_value], 1).reshape(16, 3, 2, 256)
    heads = flip(heads, 2, xh)
    w_o = w_out.T.reshape(16, 2, 256)
    for_same, for_other = flip(w_o, 1, xh).reshape(16, 512), flip(w_o, 1, 1 - xh).reshape(16, 512)
    for_2 = jnp.concatenate([for_other, heads[:, :, 1].reshape(16, 768)], 1)
    local = jnp.stack([w_gate, w_up, jnp.swapaxes(w_down, 1, 2)])
    local = local.reshape(3, 2, 2, 2, LOCAL_E, 16, 256)
    local = flip(flip(flip(local, 1, c), 2, xh), 3, xl).transpose(1, 2, 3, 0, 4, 5, 6)
    local = local.reshape(2, 4, 3, LOCAL_E, 16, 256)
    near, far = local[0], local[1]

    got_2, got_1, got_3 = together(swap_x(for_2, 2), swap_x(for_same, 1), swap_x(for_other, 3))
    far = swap_c(far)
    here = jnp.concatenate([for_same, got_1, heads[:, :, 0].reshape(16, 768)], 1)
    there = jnp.concatenate([got_2[:, :512], got_3, got_2[:, 512:]], 1)
    rows = flip(jnp.stack([here, there]), 0, xh).reshape(32, PACKED)
    both = [flip(jnp.stack([near[x], far[x]], 2), 2, c) for x in range(4)]
    sent = jnp.concatenate([tokens, route_rows(routes, route_weights, xl)], 0)
    rows, sent = together(rows, sent)

    moved = together(
        *[swap_4(rows, "z", k) for k in (1, 2, 3)], *[swap_x(both[x], x) for x in (1, 2, 3)]
    )
    owned = [both[0], *moved[3:]]
    owned = jnp.stack([jnp.concatenate(owned[:2], -1), jnp.concatenate(owned[2:], -1)])
    owned = flip(owned, 0, xh).reshape(2, 3, LOCAL_E, 32, 512)
    experts = lax.all_gather(owned, ("y", "z"), axis=0)
    zs_o = jnp.stack([rows[:, :OUT], *[m[:, :OUT] for m in moved[:3]]])
    zs = jnp.stack([rows[:, OUT:], *[m[:, OUT:] for m in moved[:3]]])
    zs, zs_o, sent, owned = together(zs, zs_o, sent, owned)

    *moved, t1, t3, cos, sin = together(
        *[swap_4(zs, "y", k) for k in (1, 2, 3)],
        swap_x(sent, 1),
        swap_x(sent, 3),
        *rotary_tables(xl),
    )
    half = kernel_call(assemble_body, [ids, zs, *moved], (shape(512, QKV),), "assemble", smem=1)
    half, zs_o, sent, t1, t3 = together(half[0], zs_o, sent, t1, t3)
    moved_o = [swap_4(zs_o, "y", k) for k in (1, 2, 3)]
    other_half, t2a, t2b = together(swap_c(half), swap_x(t3[:144], 1), swap_x(t1[144:], 3))
    blocks = [sent, t1, t2a, t2b, t3]
    near = jnp.stack([t[-16:] for t in (sent, t1, t2b, t3)])
    other_half, near, cot = together(other_half, near, cotangent)
    ct_1, ct_3 = swap_x(cot, 1), swap_x(cot, 3)

    n1, qkv, w_qkv, probs, *mixed = kernel_call(
        attend_body,
        [ids, *blocks, gain_attn, half, other_half, cos, sin],
        (shape(2, 512, 1024), shape(2, 512, QKV), shape(1024, QKV), shape(2, 4, 512, 512))
        + (shape(256, 256),) * 4,
        "attend",
        smem=1,
        flops=8e9,
    )
    *mixed, ct_1, ct_3, near, cot, moved_o[0], moved_o[1], moved_o[2] = together(
        *mixed, ct_1, ct_3, near, cot, *moved_o
    )
    half = kernel_call(assemble_body, [ids, zs_o, *moved_o], (shape(512, OUT),), "assemble", smem=1)
    other_half, *moved = together(
        swap_c(half[0]), *[swap_x(mixed[x], x) for x in (1, 2, 3)]
    )
    ct_2 = [swap_x(ct_3[:128], 1), swap_x(ct_1[128:], 3)]
    hidden, n2, w_o_full = kernel_call(
        project_body,
        [ids, tokens, gain_moe, mixed[0], *moved, half[0], other_half],
        (shape(256, 1024, dtype=F32), shape(256, 1024), shape(1024, OUT)),
        "project",
        scratch=[pltpu.VMEM((256, OUT), BF16)],
        smem=1,
    )
    n2, *ct_2 = together(n2, *ct_2)
    ct_near = jnp.stack([cot, ct_1, jnp.concatenate(ct_2, 0), ct_3])
    n2_1, n2_3, n2_far, far = together(swap_x(n2, 1), swap_x(n2, 3), swap_c(n2), swap_c(near))
    n2_1, n2_3, ct_near = together(n2_1, n2_3, ct_near)
    rank, share = route_tables(near, far, c, xh, xl)
    n2_2a, n2_2b, n2_far_1, n2_far_3, ct_far, rank, share = together(
        swap_x(n2_3[:128], 1),
        swap_x(n2_1[128:], 3),
        swap_c(n2_1),
        swap_c(n2_3),
        swap_c(ct_near),
        rank,
        share,
    )
    n2_2 = jnp.concatenate([n2_2a, n2_2b], 0)
    n2_all = [n2, n2_1, n2_2, n2_3, n2_far, n2_far_1, swap_c(n2_2), n2_far_3]
    ct_all = [ct_near, ct_far]
    z_near, z_far, g_near, g_far, grads = run_experts(ids, n2_all, ct_all, rank, share, experts)
    reduced = lax.psum_scatter(grads, ("y", "z"), scatter_dimension=0)
    g_far, z_far = together(swap_c(g_far), z_far)
    g_sums = [add(g_near[x], g_far[x]).astype(BF16) for x in range(4)]
    *g_sums, z_far = together(*g_sums, z_far)
    z_far = swap_c(z_far)
    gn2_1, gn2_3, z_far = together(swap_x(g_sums[1], 1), swap_x(g_sums[3], 3), z_far)
    gn2_2 = swap_x(g_sums[2], 2)
    gn2 = [g_sums[0], gn2_1, gn2_2, gn2_3]
    gh, ghb, *gm, dgain_moe = kernel_call(
        hidden_back_body,
        [*gn2, hidden, cotangent, gain_moe, w_o_full],
        (shape(256, 1024, dtype=F32), shape(256, 1024))
        + (shape(256, 256),) * 4
        + (shape(1, 1024, dtype=F32),),
        "hidden_back",
    )
    moved = together(*[swap_x(gm[x], x) for x in (1, 2, 3)])
    gm = [gm[0], *moved]
    ghb, *gm = together(ghb, *gm)
    ghb = [ghb, swap_x(ghb, 1), swap_x(ghb, 2), swap_x(ghb, 3)]
    g, *parts = kernel_call(
        attend_back_body,
        [qkv, probs, *gm, cos, sin, w_qkv, z_near, z_far],
        (shape(2, 512, QKV),) + (shape(256, 1024),) * 8,
        "attend_back",
        flops=10e9,
    )
    g, *parts = together(g, *parts)
    gn1, z_sums = parts[:4], parts[4:]
    via_1, via_3 = swap_x(gn1[2], 1), swap_x(z_sums[2], 3)
    qkv_grad, dgain_attn = kernel_call(
        attend_grad_body,
        [n1, g, w_qkv, gain_attn],
        (shape(1024, QKV), shape(1, 1024, dtype=F32)),
        "attend_grad",
        flops=4e9,
    )
    qkv_grad, *ghb[1:] = together(qkv_grad, *ghb[1:])
    near, far = kernel_call(
        arrange_body,
        [ids, qkv_grad, dgain_attn, dgain_moe, *ghb, *mixed],
        (shape(4, 4, 32, OWN + SPARE),) * 2,
        "arrange",
        scratch=[pltpu.VMEM((1024, 256), BF16)],
        smem=1,
    )
    sums = add(near, swap_c(far)).astype(BF16)
    moved = [swap_4(sums[k], "z", k) for k in (1, 2, 3)]
    moved[0], via_1, via_3 = together(moved[0], via_1, via_3)
    part_1 = jnp.concatenate([gn1[1], add(z_sums[1], via_3).astype(BF16)], 0)
    part_3 = jnp.concatenate([add(gn1[3], via_1).astype(BF16), z_sums[3]], 0)
    part_1, part_3 = swap_x(part_1, 1), swap_x(part_3, 3)
    sums = add(sums[0], *moved).astype(BF16)
    sums, reduced = together(sums, reduced)
    *moved, back_far = together(*[swap_4(sums[k], "y", k) for k in (1, 2, 3)], swap_c(reduced))
    sent_rows = 2 * 3 * LOCAL_E * 16
    own, own_gains, *sent = kernel_call(
        last_send_body,
        [ids, sums[0], *moved, reduced, back_far],
        (
            shape(16, OWN, dtype=F32),
            shape(16, 128, dtype=F32),
            shape(sent_rows + 16, 256),
            shape(sent_rows + 80, 256),
            shape(sent_rows + 16, 256),
        ),
        "last_send",
        scratch=[pltpu.VMEM((32, OWN + SPARE), F32)],
        smem=1,
    )
    *sent, part_1, part_3 = together(*sent, part_1, part_3)
    output, grad_tokens = kernel_call(
        tokens_back_body,
        [gn1[0], z_sums[0], part_1, part_3, tokens, gain_attn, gh, hidden],
        (shape(256, 1024),) * 2,
        "tokens_back",
    )
    *got, output, grad_tokens = together(
        *[swap_x(sent[x - 1], x) for x in (1, 2, 3)], output, grad_tokens
    )
    d_out, d_query, d_key, d_value, gains, d_gate, d_up, d_down = kernel_call(
        last_body,
        [ids, own, own_gains, *got, reduced, back_far],
        (shape(16, 512, dtype=F32),) * 4
        + (shape(16, 128, dtype=F32),)
        + (shape(8 * LOCAL_E, 16, 256, dtype=F32),) * 3,
        "last",
        smem=1,
    )
    gains = gains.reshape(2, 1024)
    return (
        output,
        grad_tokens,
        gains[0],
        d_query,
        d_key,
        d_value,
        d_out.T,
        gains[1],
        d_gate,
        d_up,
        jnp.swapaxes(d_down, 1, 2),
    )


def solution(mesh):
    split = Mesh(mesh.devices.reshape(4, 2, 4, 2, 2), ("y", "xh", "z", "c", "xl"))
    dp = ("y", "xh", "z", "c")
    rows = P((*dp, "xl"), None)
    outs = (
        rows,
        rows,
        P(),
        P(dp, "xl"),
        P(dp, "xl"),
        P(dp, "xl"),
        P("xl", dp),
        P(),
        P(None, dp, "xl"),
        P(None, dp, "xl"),
        P(None, "xl", dp),
    )
    ins = (
        rows,
        P(),
        P(dp, "xl"),
        P(dp, "xl"),
        P(dp, "xl"),
        P("xl", dp),
        P(),
        P(None, dp, "xl"),
        P(None, dp, "xl"),
        P(None, "xl", dp),
        P(dp, None),
        P(dp, None),
        rows,
    )
    return jax.shard_map(on_device, mesh=split, in_specs=ins, out_specs=outs, check_vma=False)
```

```python
import jax
import jax.numpy as jnp
from jax import lax
from jax.experimental import pallas as pl
from jax.experimental.pallas import tpu as pltpu
from jax.sharding import Mesh
from jax.sharding import PartitionSpec as P

HD = 64
CAP = 160
EPSILON = 1e-06
THETA = 10000.0
LOCAL_E = 4
F32 = jnp.float32
BF16 = jnp.bfloat16
VMEM_BYTES = 60 * 1024 * 1024
SMALL_VMEM_BYTES = 32 * 1024 * 1024


def swap_x(value, bits):
    return lax.ppermute(value, ("xh", "xl"), [(i, i ^ bits) for i in range(4)])


def swap_c(value):
    return lax.ppermute(value, "c", [(0, 1), (1, 0)])


def swap_4(value, axis, bits):
    return lax.ppermute(value, axis, [(i, i ^ bits) for i in range(4)])


def after(value, *others):
    return lax.optimization_barrier((value, others))[0]


def together(*values):
    return lax.optimization_barrier(values)


def flip(value, axis, bit):
    return jnp.where(bit == 1, jnp.flip(value, axis), value)


def add(*terms):
    return sum(t.astype(F32) for t in terms)


def dot(a, b, ca, cb):
    return lax.dot_general(a, b, (((ca,), (cb,)), ((), ())), preferred_element_type=F32)


def whole(n):
    return [pl.BlockSpec(memory_space=pltpu.VMEM)] * n


def cost(flops, nbytes):
    return pl.CostEstimate(flops=int(flops), bytes_accessed=int(nbytes), transcendentals=0)


def kernel_call(body, ins, outs, name, scratch=(), smem=0, flops=1e9):
    specs = [pl.BlockSpec(memory_space=pltpu.SMEM)] * smem + whole(len(ins) - smem)
    nbytes = sum(v.size * v.dtype.itemsize for v in (*ins, *outs))
    return pl.pallas_call(
        body,
        out_shape=outs,
        in_specs=specs,
        out_specs=whole(len(outs)),
        scratch_shapes=list(scratch),
        compiler_params=pltpu.CompilerParams(vmem_limit_bytes=SMALL_VMEM_BYTES),
        cost_estimate=cost(flops, nbytes),
        name=name,
    )(*ins)


def shape(*dims, dtype=BF16):
    return jax.ShapeDtypeStruct(dims, dtype)


OUT, QKV, SPARE = 1024, 768, 128
PACKED = OUT + QKV
OWN = 256 + QKV


def d_block(y, xh, z):
    return (y * 2 + xh) * 4 + z


def assemble_body(ids, p0, p1, p2, p3, half_ref):
    for y, piece in enumerate((p0, p1, p2, p3)):
        for z in range(4):
            for xh in range(2):
                row = d_block(y ^ ids[0], xh, z ^ ids[1]) * 16
                rows = pl.ds(pl.multiple_of(row, 16), 16)
                half_ref[rows, :] = piece[z, xh * 16 : xh * 16 + 16, :]


def interleave(ids, own, other, dst):
    for half, c in ((own, ids[2]), (other, 1 - ids[2])):
        for n in range(32):
            rows = pl.ds(pl.multiple_of(n * 32 + c * 16, 16), 16)
            dst[rows, :] = half[n * 16 : n * 16 + 16, :]


def rotated(v, cos, sin):
    lane = lax.broadcasted_iota(jnp.int32, v.shape, 1)
    width = v.shape[1]
    other = jnp.where(lane % HD < HD // 2, pltpu.roll(v, width - 32, 1), pltpu.roll(v, 32, 1))
    return v * cos + other * sin


def attend_body(ids, t0, t1, t2a, t2b, t3, gain, own, other, cos_ref, sin_ref, *outs):
    n1_ref, qkv_ref, w_ref, p_ref = outs[:4]
    outs = outs[4:]
    tokens = [(t0.at[:256],), (t1.at[:256],), (t2a, t2b.at[:112]), (t3.at[:256],)]
    cos, sin = cos_ref[...], sin_ref[...]
    interleave(ids, own, other, w_ref)
    for s in range(2):
        for half in range(2):
            x = jnp.concatenate([t[...] for t in tokens[2 * s + half]], 0).astype(F32)
            r1 = lax.rsqrt(jnp.mean(x * x, -1, keepdims=True) + EPSILON)
            n1_ref[s, half * 256 : half * 256 + 256, :] = (x * r1 * gain[...]).astype(BF16)
        proj = jnp.dot(n1_ref[s], w_ref[...], preferred_element_type=F32)
        q = rotated(proj[:, :256], cos, sin).astype(BF16)
        k = rotated(proj[:, 256:512], cos, sin).astype(BF16)
        v = proj[:, 512:].astype(BF16)
        qkv_ref[s, :, :256] = q
        qkv_ref[s, :, 256:512] = k
        qkv_ref[s, :, 512:] = v
        mixed = []
        for h in range(4):
            cols = slice(h * HD, h * HD + HD)
            scores = dot(q[:, cols], k[:, cols], 1, 1) * (HD**-0.5)
            e = jnp.exp(scores - jnp.max(scores, -1, keepdims=True))
            p = (e / jnp.sum(e, -1, keepdims=True)).astype(BF16)
            p_ref[s, h] = p
            mixed.append(dot(p, v[:, cols], 1, 0).astype(BF16))
        out = jnp.concatenate(mixed, 1)
        outs[2 * s][...] = out[:256]
        outs[2 * s + 1][...] = out[256:]


def out_columns(x):
    block = (x % 2) * 2 + x // 2
    return slice(block * 256, block * 256 + 256)


def project_body(ids, tokens, gain, m0, m1, m2, m3, own, other, hidden_ref, n2_ref, wo_ref, mixed_ref):
    interleave(ids, own, other, wo_ref)
    for x, m in enumerate((m0, m1, m2, m3)):
        mixed_ref[:, out_columns(x)] = m[...]
    hidden = tokens[...].astype(F32) + dot(mixed_ref[...], wo_ref[...], 1, 1)
    hidden_ref[...] = hidden
    r2 = lax.rsqrt(jnp.mean(hidden * hidden, -1, keepdims=True) + EPSILON)
    n2_ref[...] = (hidden * r2 * gain[...]).astype(BF16)


def expert_pieces():
    for y in range(4):
        for z in range(4):
            for xh in range(2):
                row = d_block(y, xh, z) * 32
                yield (y * 4 + z, xh), slice(row, row + 32)


def relative_pieces(ids):
    for y in range(4):
        for z in range(4):
            for c in range(2):
                for x in range(4):
                    row = d_block(y, (x // 2) ^ ids[3], z) * 32 + (c ^ ids[2]) * 16
                    rows = pl.ds(pl.multiple_of(row, 16), 16)
                    yield (y * 4 + z, c, x), rows, slice((x % 2) * 256, (x % 2) * 256 + 256)


def expert_body(*refs):
    ids, n2 = refs[0], refs[1:9]
    ct = [r.at[x] for r in refs[9:11] for x in range(4)]
    rank_ref, share_ref, w_ref = refs[11:14]
    z_ref, g_near, g_far, dw_ref = refs[14:18]
    wg, wu, wd, x_s, gz_s, p_s, gx_s = refs[18:]
    e = pl.program_id(0)
    there = pl.ds(pl.multiple_of(e * CAP, 32), CAP)
    for piece, d in expert_pieces():
        wg[d, :] = w_ref[*piece, 0, 0]
        wu[d, :] = w_ref[*piece, 1, 0]
        wd[d, :] = w_ref[*piece, 2, 0]
    shares = []
    slot = lax.broadcasted_iota(jnp.int32, (CAP, 512), 0)
    for s in range(4):
        hit = slot == rank_ref[0, s : s + 1, :]
        share = jnp.sum(jnp.where(hit, share_ref[0, s : s + 1, :], 0.0), 1, keepdims=True)
        shares.append(share)
        p = hit.astype(F32).astype(BF16)
        p_s[s, there, :] = p
        here = slice(s * CAP, s * CAP + CAP)
        x_s[here, :] = (
            dot(p[:, :256], n2[2 * s][...], 1, 0) + dot(p[:, 256:], n2[2 * s + 1][...], 1, 0)
        ).astype(BF16)
        gz_s[here, :] = (
            (dot(p[:, :256], ct[2 * s][...], 1, 0) + dot(p[:, 256:], ct[2 * s + 1][...], 1, 0))
            * share
        ).astype(BF16)
    share = jnp.concatenate(shares, 0)
    a = dot(x_s[...], wg[...], 1, 0)
    b = dot(x_s[...], wu[...], 1, 0)
    sig = 1.0 / (1.0 + jnp.exp(-a))
    sa = a * sig
    u = (sa * b).astype(BF16)
    gu = dot(gz_s[...], wd[...], 1, 0)
    ga = (gu * b * sig * (1.0 + a * (1.0 - sig))).astype(BF16)
    gb = (gu * sa).astype(BF16)
    z = (dot(u, wd[...], 1, 1) * share).astype(BF16)
    z_ref[0] = z
    gx = (dot(ga, wg[...], 1, 1) + dot(gb, wu[...], 1, 1)).astype(BF16)
    for s in range(4):
        here = slice(s * CAP, s * CAP + CAP)
        gx_s[s, there, :] = gx[here]
    for m, (left, right) in enumerate(((x_s, ga), (x_s, gb), (gz_s, u))):
        wg[...] = dot(left[...], right, 0, 0).astype(BF16)
        for piece, rows, cols in relative_pieces(ids):
            dw_ref[*piece, m, 0] = wg[rows, cols]

    @pl.when(e == LOCAL_E - 1)
    def _():
        for s in range(4):
            total = dot(p_s[s], gx_s[s], 0, 0).astype(BF16)
            dst = g_near if s < 2 else g_far
            dst[2 * (s % 2)] = total[:256]
            dst[2 * (s % 2) + 1] = total[256:]


def combine_body(rank_ref, z_ref, z_near, z_far):
    slot = lax.broadcasted_iota(jnp.int32, (CAP, 512), 0)
    for s in range(4):
        hits = [slot == rank_ref[i, s : s + 1, :] for i in range(LOCAL_E)]
        p = jnp.concatenate([h.astype(F32).astype(BF16) for h in hits], 0)
        here = slice(s * CAP, s * CAP + CAP)
        terms = jnp.concatenate([z_ref[i, here, :] for i in range(LOCAL_E)], 0)
        total = dot(p, terms, 0, 0).astype(BF16)
        dst = z_near if s < 2 else z_far
        dst[2 * (s % 2)] = total[:256]
        dst[2 * (s % 2) + 1] = total[256:]


W_BLOCK = (16, 2, 3, 1, 32, 512)


def run_experts(ids, n2, ct, rank, share, weights):
    table = pl.BlockSpec((1, 4, 512), lambda e: (e, 0, 0))
    w_spec = pl.BlockSpec(W_BLOCK, lambda e: (0, 0, 0, e, 0, 0))
    slots = pl.BlockSpec((1, 4 * CAP, 1024), lambda e: (e, 0, 0))
    dw_spec = pl.BlockSpec((16, 2, 4, 3, 1, 16, 256), lambda e: (0, 0, 0, 0, e, 0, 0))
    blocks = shape(4, 256, 1024)
    return pl.pallas_call(
        expert_body,
        grid=(LOCAL_E,),
        out_shape=(shape(LOCAL_E, 4 * CAP, 1024),) + (blocks,) * 2 + (shape(16, 2, 4, 3, LOCAL_E, 16, 256),),
        in_specs=[pl.BlockSpec(memory_space=pltpu.SMEM)] + whole(10) + [table, table, w_spec],
        out_specs=[slots] + whole(2) + [dw_spec],
        scratch_shapes=[
            pltpu.VMEM((1024, 512), BF16),
            pltpu.VMEM((1024, 512), BF16),
            pltpu.VMEM((1024, 512), BF16),
            pltpu.VMEM((4 * CAP, 1024), BF16),
            pltpu.VMEM((4 * CAP, 1024), BF16),
            pltpu.VMEM((4, LOCAL_E * CAP, 512), BF16),
            pltpu.VMEM((4, LOCAL_E * CAP, 1024), BF16),
        ],
        compiler_params=pltpu.CompilerParams(vmem_limit_bytes=VMEM_BYTES),
        cost_estimate=cost(36e9, 60e6),
        name="experts",
    )(ids, *n2, *ct, rank, share, weights)


def hidden_back_body(g0, g1, g2, g3, hidden_ref, ct, gain, wo, gh_ref, ghb_ref, m0, m1, m2, m3, dgain_ref):
    gn2 = g0[...].astype(F32) + g1[...].astype(F32) + g2[...].astype(F32) + g3[...].astype(F32)
    hidden = hidden_ref[...]
    r2 = lax.rsqrt(jnp.mean(hidden * hidden, -1, keepdims=True) + EPSILON)
    w2 = gn2 * gain[...]
    gh = ct[...].astype(F32) + r2 * w2 - hidden * (r2 * r2 * r2) * jnp.mean(w2 * hidden, -1, keepdims=True)
    gh_ref[...] = gh
    ghb = gh.astype(BF16)
    ghb_ref[...] = ghb
    gm = dot(ghb, wo[...], 1, 0).astype(BF16)
    for x, m in enumerate((m0, m1, m2, m3)):
        m[...] = gm[:, out_columns(x)]
    dgain_ref[...] = jnp.sum(gn2 * hidden * r2, 0, keepdims=True)


def attend_back_body(qkv, p_ref, m0, m1, m2, m3, cos_ref, sin_ref, w_ref, z_near, z_far, g_ref, *outs):
    gm_refs = (m0, m1, m2, m3)
    cos, sin = cos_ref[...], -sin_ref[...]
    for s in range(2):
        gm = jnp.concatenate([gm_refs[2 * s][...], gm_refs[2 * s + 1][...]], 0)
        gqs, gks, gvs = [], [], []
        for h in range(4):
            q = qkv[s, :, h * HD : h * HD + HD]
            k = qkv[s, :, 256 + h * HD : 256 + h * HD + HD]
            v = qkv[s, :, 512 + h * HD : 512 + h * HD + HD]
            gmh = gm[:, h * HD : h * HD + HD]
            p = p_ref[s, h].astype(F32)
            gp = dot(gmh, v, 1, 1)
            gs = (p * (gp - jnp.sum(gp * p, -1, keepdims=True))).astype(BF16)
            gqs.append(dot(gs, k, 1, 0) * (HD**-0.5))
            gks.append(dot(gs, q, 0, 0) * (HD**-0.5))
            gvs.append(dot(p_ref[s, h], gmh, 0, 0))
        g_ref[s, :, :256] = rotated(jnp.concatenate(gqs, 1), cos, sin).astype(BF16)
        g_ref[s, :, 256:512] = rotated(jnp.concatenate(gks, 1), cos, sin).astype(BF16)
        g_ref[s, :, 512:] = jnp.concatenate(gvs, 1).astype(BF16)
        part = dot(g_ref[s], w_ref[...], 1, 1).astype(BF16)
        for half in range(2):
            x = 2 * s + half
            outs[x][...] = part[half * 256 : half * 256 + 256]
            outs[4 + x][...] = (z_near[x].astype(F32) + z_far[x].astype(F32)).astype(BF16)


def attend_grad_body(n1, g, w_qkv, gain, grad_ref, dgain_ref):
    qkv = dot(n1[0], g[0], 0, 0) + dot(n1[1], g[1], 0, 0)
    grad_ref[...] = qkv.astype(BF16)
    weighted = qkv * w_qkv[...].astype(F32)
    ones = jnp.ones((8, QKV), F32)
    sums = lax.dot_general(
        ones,
        weighted,
        (((1,), (1,)), ((), ())),
        precision=lax.Precision.HIGHEST,
        preferred_element_type=F32,
    )
    dgain_ref[...] = sums[:1] / gain[...]


def arrange_body(ids, qkv, dgain, dgain_moe, *refs):
    ghb, mixed = refs[:4], refs[4:8]
    near_ref, far_ref, out = refs[8:]
    out[...] = sum(dot(ghb[x][...], mixed[x][...], 0, 0) for x in range(4)).astype(BF16)
    rows = [v[:, i * 128 : i * 128 + 128] for v in (dgain[...], dgain_moe[...]) for i in range(8)]
    gains = jnp.concatenate(rows + [jnp.zeros((16, 128), F32)], 0).astype(BF16)
    for y in range(4):
        for z in range(4):
            near_ref[z, y, :, OWN:] = gains
            far_ref[z, y, :, OWN:] = gains
            for xh in range(2):
                row = d_block(y ^ ids[0], xh, z ^ ids[1]) * 32
                for dst, c in ((near_ref, ids[2]), (far_ref, 1 - ids[2])):
                    rows = pl.ds(pl.multiple_of(row + c * 16, 16), 16)
                    dst[z, y, xh * 16 : xh * 16 + 16, :256] = out[rows, :]
                    dst[z, y, xh * 16 : xh * 16 + 16, 256:OWN] = qkv[rows, :]


def tokens_back_body(gn1, z, p1, p3, tokens, gain, gh, hidden, out_ref, grad_ref):
    total = p1[...].astype(F32) + p3[...].astype(F32)
    out_ref[...] = (hidden[...] + z[...].astype(F32) + total[256:]).astype(BF16)
    x = tokens[...].astype(F32)
    r1 = lax.rsqrt(jnp.mean(x * x, -1, keepdims=True) + EPSILON)
    w1 = (gn1[...].astype(F32) + total[:256]) * gain[...]
    grad_ref[...] = (
        gh[...] + r1 * w1 - x * (r1 * r1 * r1) * jnp.mean(w1 * x, -1, keepdims=True)
    ).astype(BF16)


def rotary_tables(xl):
    frequency = THETA ** (-2.0 * jnp.arange(HD // 2, dtype=F32) / HD)
    place = jnp.arange(512)
    place = ((place // 256) ^ xl) * 256 + place % 256
    angles = place.astype(F32)[:, None] * frequency[None, :]
    cos, sin = jnp.cos(angles), jnp.sin(angles)
    return jnp.concatenate([cos] * 8, 1), jnp.concatenate([-sin, sin] * 4, 1)


def last_send_body(ids, s0, s1, s2, s3, near, far, own_ref, gain_ref, p1, p2, p3, total):
    total[...] = s0[...].astype(F32) + s1[...].astype(F32) + s2[...].astype(F32) + s3[...].astype(F32)
    own = pl.ds(pl.multiple_of(ids[3] * 16, 16), 16)
    other = pl.ds(pl.multiple_of((1 - ids[3]) * 16, 16), 16)
    gains = total[:16, OWN:]
    gain_ref[...] = gains
    own_ref[...] = total[own, :OWN]
    base = 2 * 3 * LOCAL_E * 16
    for x, p in ((1, p1), (2, p2), (3, p3)):
        for m in range(3):
            for e in range(LOCAL_E):
                row = (m * LOCAL_E + e) * 16
                p[row : row + 16, :] = near[0, x, m, e]
                p[base // 2 + row : base // 2 + row + 16, :] = far[1, x, m, e]
        p[base : base + 16, :] = jnp.concatenate([gains, gains], 1).astype(BF16)
    for j in range(4):
        part = total[other, j * 256 : j * 256 + 256]
        p2[base + 16 + j * 16 : base + 32 + j * 16, :] = part.astype(BF16)


def last_body(ids, own, own_gains, g1, g2, g3, near, far, do, dq, dk, dv, gain_ref, *experts):
    c, xh, xl = ids[2], ids[3], ids[4]
    base = 2 * 3 * LOCAL_E * 16
    mine = pl.ds(pl.multiple_of(xh * 256, 256), 256)
    theirs = pl.ds(pl.multiple_of((1 - xh) * 256, 256), 256)
    for j, d in enumerate((do, dq, dk, dv)):
        d[:, mine] = own[:, j * 256 : j * 256 + 256]
        d[:, theirs] = g2[base + 16 + j * 16 : base + 32 + j * 16, :].astype(F32)
    gain_ref[...] = own_gains[...] + sum(g[base : base + 16, :128].astype(F32) for g in (g1, g2, g3))
    for x in range(4):
        for b in range(2):
            owner = (c ^ b) * 4 + (xh ^ (x // 2)) * 2 + (xl ^ (x % 2))
            for m, d in enumerate(experts):
                for e in range(LOCAL_E):
                    row = ((b * 3 + m) * LOCAL_E + e) * 16
                    if x == 0:
                        block = near[0, 0, m, e] if b == 0 else far[1, 0, m, e]
                    else:
                        block = (g1, g2, g3)[x - 1][row : row + 16, :]
                    d[owner * LOCAL_E + e] = block.astype(F32)


def route_rows(routes, route_weights, xl):
    high = lax.reduce_precision(route_weights, 8, 7)
    low = lax.reduce_precision(route_weights - high, 8, 7)
    table = jnp.concatenate([routes.T.astype(F32), high.T, low.T], 0).reshape(24, 2, 256)
    table = jnp.where(xl == 1, table[:, 1], table[:, 0])
    return jnp.pad(table.astype(BF16), ((0, 40), (0, 0))).reshape(16, 1024)


def route_tables(near, far, c, xh, xl):
    tables = jnp.concatenate([near, far], 0).reshape(8, 64, 256)[:, :24].astype(F32)
    tables = tables.reshape(4, 2, 24, 256).transpose(0, 2, 1, 3).reshape(4, 24, 512)
    first = ((c * 4 + xh * 2 + xl) * LOCAL_E).astype(F32)
    names = first + jnp.arange(LOCAL_E, dtype=F32)
    match = tables[None, :, :8, :] == names[:, None, None, None]
    shares = tables[:, 8:16] + tables[:, 16:]
    share = jnp.sum(jnp.where(match, shares[None], 0.0), 2)
    named = jnp.any(match, 2)
    before = (jnp.arange(512)[:, None] <= jnp.arange(512)[None, :]).astype(BF16)
    count = jnp.dot(named.astype(BF16), before, preferred_element_type=F32)
    rank = jnp.where(named, count.astype(jnp.int32) - 1, -1)
    return rank, share


def on_device(
    tokens,
    gain_attn,
    w_query,
    w_key,
    w_value,
    w_out,
    gain_moe,
    w_gate,
    w_up,
    w_down,
    routes,
    route_weights,
    cotangent,
):
    y, xh, z, c, xl = (lax.axis_index(a) for a in ("y", "xh", "z", "c", "xl"))
    ids = jnp.stack([y, z, c, xh, xl]).astype(jnp.int32)
    gain_attn = gain_attn.reshape(1, 1024)
    gain_moe = gain_moe.reshape(1, 1024)

    heads = jnp.stack([w_query, w_key, w_value], 1).reshape(16, 3, 2, 256)
    heads = flip(heads, 2, xh)
    w_o = w_out.T.reshape(16, 2, 256)
    for_same, for_other = flip(w_o, 1, xh).reshape(16, 512), flip(w_o, 1, 1 - xh).reshape(16, 512)
    for_2 = jnp.concatenate([for_other, heads[:, :, 1].reshape(16, 768)], 1)
    local = jnp.stack([w_gate, w_up, jnp.swapaxes(w_down, 1, 2)])
    local = local.reshape(3, 2, 2, 2, LOCAL_E, 16, 256)
    local = flip(flip(flip(local, 1, c), 2, xh), 3, xl).transpose(1, 2, 3, 0, 4, 5, 6)
    local = local.reshape(2, 4, 3, LOCAL_E, 16, 256)
    near, far = local[0], local[1]

    got_2, got_1, got_3 = together(swap_x(for_2, 2), swap_x(for_same, 1), swap_x(for_other, 3))
    far = swap_c(far)
    here = jnp.concatenate([for_same, got_1, heads[:, :, 0].reshape(16, 768)], 1)
    there = jnp.concatenate([got_2[:, :512], got_3, got_2[:, 512:]], 1)
    rows = flip(jnp.stack([here, there]), 0, xh).reshape(32, PACKED)
    both = [flip(jnp.stack([near[x], far[x]], 2), 2, c) for x in range(4)]
    sent = jnp.concatenate([tokens, route_rows(routes, route_weights, xl)], 0)
    rows, sent = together(rows, sent)

    moved = together(
        *[swap_4(rows, "z", k) for k in (1, 2, 3)], *[swap_x(both[x], x) for x in (1, 2, 3)]
    )
    owned = [both[0], *moved[3:]]
    owned = jnp.stack([jnp.concatenate(owned[:2], -1), jnp.concatenate(owned[2:], -1)])
    owned = flip(owned, 0, xh).reshape(2, 3, LOCAL_E, 32, 512)
    experts = lax.all_gather(owned, ("y", "z"), axis=0)
    zs_o = jnp.stack([rows[:, :OUT], *[m[:, :OUT] for m in moved[:3]]])
    zs = jnp.stack([rows[:, OUT:], *[m[:, OUT:] for m in moved[:3]]])
    zs, zs_o, sent, owned = together(zs, zs_o, sent, owned)

    *moved, t1, t3, cos, sin = together(
        *[swap_4(zs, "y", k) for k in (1, 2, 3)],
        swap_x(sent, 1),
        swap_x(sent, 3),
        *rotary_tables(xl),
    )
    half = kernel_call(assemble_body, [ids, zs, *moved], (shape(512, QKV),), "assemble", smem=1)
    half, zs_o, sent, t1, t3 = together(half[0], zs_o, sent, t1, t3)
    moved_o = [swap_4(zs_o, "y", k) for k in (1, 2, 3)]
    other_half, t2a, t2b = together(swap_c(half), swap_x(t3[:144], 1), swap_x(t1[144:], 3))
    blocks = [sent, t1, t2a, t2b, t3]
    near = jnp.stack([t[-16:] for t in (sent, t1, t2b, t3)])
    other_half, near, cot = together(other_half, near, cotangent)
    ct_1, ct_3 = swap_x(cot, 1), swap_x(cot, 3)

    n1, qkv, w_qkv, probs, *mixed = kernel_call(
        attend_body,
        [ids, *blocks, gain_attn, half, other_half, cos, sin],
        (shape(2, 512, 1024), shape(2, 512, QKV), shape(1024, QKV), shape(2, 4, 512, 512))
        + (shape(256, 256),) * 4,
        "attend",
        smem=1,
        flops=8e9,
    )
    *mixed, ct_1, ct_3, near, cot, moved_o[0], moved_o[1], moved_o[2] = together(
        *mixed, ct_1, ct_3, near, cot, *moved_o
    )
    half = kernel_call(assemble_body, [ids, zs_o, *moved_o], (shape(512, OUT),), "assemble", smem=1)
    other_half, *moved = together(
        swap_c(half[0]), *[swap_x(mixed[x], x) for x in (1, 2, 3)]
    )
    ct_2 = [swap_x(ct_3[:128], 1), swap_x(ct_1[128:], 3)]
    hidden, n2, w_o_full = kernel_call(
        project_body,
        [ids, tokens, gain_moe, mixed[0], *moved, half[0], other_half],
        (shape(256, 1024, dtype=F32), shape(256, 1024), shape(1024, OUT)),
        "project",
        scratch=[pltpu.VMEM((256, OUT), BF16)],
        smem=1,
    )
    n2, *ct_2 = together(n2, *ct_2)
    ct_near = jnp.stack([cot, ct_1, jnp.concatenate(ct_2, 0), ct_3])
    n2_1, n2_3, n2_far, far = together(swap_x(n2, 1), swap_x(n2, 3), swap_c(n2), swap_c(near))
    n2_1, n2_3, ct_near = together(n2_1, n2_3, ct_near)
    rank, share = route_tables(near, far, c, xh, xl)
    n2_2a, n2_2b, n2_far_1, n2_far_3, ct_far, rank, share = together(
        swap_x(n2_3[:128], 1),
        swap_x(n2_1[128:], 3),
        swap_c(n2_1),
        swap_c(n2_3),
        swap_c(ct_near),
        rank,
        share,
    )
    n2_2 = jnp.concatenate([n2_2a, n2_2b], 0)
    n2_all = [n2, n2_1, n2_2, n2_3, n2_far, n2_far_1, swap_c(n2_2), n2_far_3]
    ct_all = [ct_near, ct_far]
    z_slots, g_near, g_far, grads = run_experts(ids, n2_all, ct_all, rank, share, experts)
    reduced = lax.psum_scatter(grads, ("y", "z"), scatter_dimension=0)
    g_far = swap_c(g_far)
    g_sums = [add(g_near[x], g_far[x]).astype(BF16) for x in range(4)]
    *g_sums, z_slots = together(*g_sums, z_slots)
    z_near, z_far = kernel_call(
        combine_body, [rank, z_slots], (shape(4, 256, 1024),) * 2, "combine", flops=4e9
    )
    gn2_1, gn2_3, gn2_2, z_near, z_far = together(
        swap_x(g_sums[1], 1), swap_x(g_sums[3], 3), swap_x(g_sums[2], 2), z_near, z_far
    )
    z_far = swap_c(z_far)
    gn2 = [g_sums[0], gn2_1, gn2_2, gn2_3]
    gh, ghb, *gm, dgain_moe = kernel_call(
        hidden_back_body,
        [*gn2, hidden, cotangent, gain_moe, w_o_full],
        (shape(256, 1024, dtype=F32), shape(256, 1024))
        + (shape(256, 256),) * 4
        + (shape(1, 1024, dtype=F32),),
        "hidden_back",
    )
    moved = together(*[swap_x(gm[x], x) for x in (1, 2, 3)])
    gm = [gm[0], *moved]
    ghb, *gm = together(ghb, *gm)
    ghb = [ghb, swap_x(ghb, 1), swap_x(ghb, 2), swap_x(ghb, 3)]
    g, *parts = kernel_call(
        attend_back_body,
        [qkv, probs, *gm, cos, sin, w_qkv, z_near, z_far],
        (shape(2, 512, QKV),) + (shape(256, 1024),) * 8,
        "attend_back",
        flops=10e9,
    )
    g, *parts = together(g, *parts)
    gn1, z_sums = parts[:4], parts[4:]
    via_1, via_3 = swap_x(gn1[2], 1), swap_x(z_sums[2], 3)
    qkv_grad, dgain_attn = kernel_call(
        attend_grad_body,
        [n1, g, w_qkv, gain_attn],
        (shape(1024, QKV), shape(1, 1024, dtype=F32)),
        "attend_grad",
        flops=4e9,
    )
    qkv_grad, *ghb[1:] = together(qkv_grad, *ghb[1:])
    near, far = kernel_call(
        arrange_body,
        [ids, qkv_grad, dgain_attn, dgain_moe, *ghb, *mixed],
        (shape(4, 4, 32, OWN + SPARE),) * 2,
        "arrange",
        scratch=[pltpu.VMEM((1024, 256), BF16)],
        smem=1,
    )
    sums = add(near, swap_c(far)).astype(BF16)
    moved = [swap_4(sums[k], "z", k) for k in (1, 2, 3)]
    moved[0], via_1, via_3 = together(moved[0], via_1, via_3)
    part_1 = jnp.concatenate([gn1[1], add(z_sums[1], via_3).astype(BF16)], 0)
    part_3 = jnp.concatenate([add(gn1[3], via_1).astype(BF16), z_sums[3]], 0)
    part_1, part_3 = swap_x(part_1, 1), swap_x(part_3, 3)
    sums = add(sums[0], *moved).astype(BF16)
    sums, reduced = together(sums, reduced)
    *moved, back_far = together(*[swap_4(sums[k], "y", k) for k in (1, 2, 3)], swap_c(reduced))
    sent_rows = 2 * 3 * LOCAL_E * 16
    own, own_gains, *sent = kernel_call(
        last_send_body,
        [ids, sums[0], *moved, reduced, back_far],
        (
            shape(16, OWN, dtype=F32),
            shape(16, 128, dtype=F32),
            shape(sent_rows + 16, 256),
            shape(sent_rows + 80, 256),
            shape(sent_rows + 16, 256),
        ),
        "last_send",
        scratch=[pltpu.VMEM((32, OWN + SPARE), F32)],
        smem=1,
    )
    *sent, part_1, part_3 = together(*sent, part_1, part_3)
    output, grad_tokens = kernel_call(
        tokens_back_body,
        [gn1[0], z_sums[0], part_1, part_3, tokens, gain_attn, gh, hidden],
        (shape(256, 1024),) * 2,
        "tokens_back",
    )
    *got, output, grad_tokens = together(
        *[swap_x(sent[x - 1], x) for x in (1, 2, 3)], output, grad_tokens
    )
    d_out, d_query, d_key, d_value, gains, d_gate, d_up, d_down = kernel_call(
        last_body,
        [ids, own, own_gains, *got, reduced, back_far],
        (shape(16, 512, dtype=F32),) * 4
        + (shape(16, 128, dtype=F32),)
        + (shape(8 * LOCAL_E, 16, 256, dtype=F32),) * 3,
        "last",
        smem=1,
    )
    gains = gains.reshape(2, 1024)
    return (
        output,
        grad_tokens,
        gains[0],
        d_query,
        d_key,
        d_value,
        d_out.T,
        gains[1],
        d_gate,
        d_up,
        jnp.swapaxes(d_down, 1, 2),
    )


def solution(mesh):
    split = Mesh(mesh.devices.reshape(4, 2, 4, 2, 2), ("y", "xh", "z", "c", "xl"))
    dp = ("y", "xh", "z", "c")
    rows = P((*dp, "xl"), None)
    outs = (
        rows,
        rows,
        P(),
        P(dp, "xl"),
        P(dp, "xl"),
        P(dp, "xl"),
        P("xl", dp),
        P(),
        P(None, dp, "xl"),
        P(None, dp, "xl"),
        P(None, "xl", dp),
    )
    ins = (
        rows,
        P(),
        P(dp, "xl"),
        P(dp, "xl"),
        P(dp, "xl"),
        P("xl", dp),
        P(),
        P(None, dp, "xl"),
        P(None, dp, "xl"),
        P(None, "xl", dp),
        P(dp, None),
        P(dp, None),
        rows,
    )
    return jax.shard_map(on_device, mesh=split, in_specs=ins, out_specs=outs, check_vma=False)
```

```python
import jax
import jax.numpy as jnp
from jax import lax
from jax.experimental import pallas as pl
from jax.experimental.pallas import tpu as pltpu
from jax.sharding import Mesh
from jax.sharding import PartitionSpec as P

HD = 64
CAP = 160
EPSILON = 1e-06
THETA = 10000.0
LOCAL_E = 4
F32 = jnp.float32
BF16 = jnp.bfloat16
VMEM_BYTES = 60 * 1024 * 1024
SMALL_VMEM_BYTES = 32 * 1024 * 1024


def swap_x(value, bits):
    return lax.ppermute(value, ("xh", "xl"), [(i, i ^ bits) for i in range(4)])


def swap_c(value):
    return lax.ppermute(value, "c", [(0, 1), (1, 0)])


def swap_4(value, axis, bits):
    return lax.ppermute(value, axis, [(i, i ^ bits) for i in range(4)])


def after(value, *others):
    return lax.optimization_barrier((value, others))[0]


def together(*values):
    return lax.optimization_barrier(values)


def flip(value, axis, bit):
    return jnp.where(bit == 1, jnp.flip(value, axis), value)


def add(*terms):
    return sum(t.astype(F32) for t in terms)


def dot(a, b, ca, cb):
    return lax.dot_general(a, b, (((ca,), (cb,)), ((), ())), preferred_element_type=F32)


def whole(n):
    return [pl.BlockSpec(memory_space=pltpu.VMEM)] * n


def cost(flops, nbytes):
    return pl.CostEstimate(flops=int(flops), bytes_accessed=int(nbytes), transcendentals=0)


def kernel_call(body, ins, outs, name, scratch=(), smem=0, flops=1e9):
    specs = [pl.BlockSpec(memory_space=pltpu.SMEM)] * smem + whole(len(ins) - smem)
    nbytes = sum(v.size * v.dtype.itemsize for v in (*ins, *outs))
    return pl.pallas_call(
        body,
        out_shape=outs,
        in_specs=specs,
        out_specs=whole(len(outs)),
        scratch_shapes=list(scratch),
        compiler_params=pltpu.CompilerParams(vmem_limit_bytes=SMALL_VMEM_BYTES),
        cost_estimate=cost(flops, nbytes),
        name=name,
    )(*ins)


def shape(*dims, dtype=BF16):
    return jax.ShapeDtypeStruct(dims, dtype)


OUT, QKV, SPARE = 1024, 768, 128
PACKED = OUT + QKV
OWN = 256 + QKV


def d_block(y, xh, z):
    return (y * 2 + xh) * 4 + z


def assemble_body(ids, p0, p1, p2, p3, half_ref):
    for y, piece in enumerate((p0, p1, p2, p3)):
        for z in range(4):
            for xh in range(2):
                row = d_block(y ^ ids[0], xh, z ^ ids[1]) * 16
                rows = pl.ds(pl.multiple_of(row, 16), 16)
                half_ref[rows, :] = piece[z, xh * 16 : xh * 16 + 16, :]


def interleave(ids, own, other, dst):
    for half, c in ((own, ids[2]), (other, 1 - ids[2])):
        for n in range(32):
            rows = pl.ds(pl.multiple_of(n * 32 + c * 16, 16), 16)
            dst[rows, :] = half[n * 16 : n * 16 + 16, :]


def rotated(v, cos, sin):
    lane = lax.broadcasted_iota(jnp.int32, v.shape, 1)
    width = v.shape[1]
    other = jnp.where(lane % HD < HD // 2, pltpu.roll(v, width - 32, 1), pltpu.roll(v, 32, 1))
    return v * cos + other * sin


def attend_body(ids, t0, t1, t2a, t2b, t3, gain, own, other, cos_ref, sin_ref, *outs):
    n1_ref, qkv_ref, w_ref, p_ref = outs[:4]
    outs = outs[4:]
    tokens = [(t0.at[:256],), (t1.at[:256],), (t2a, t2b.at[:112]), (t3.at[:256],)]
    cos, sin = cos_ref[...], sin_ref[...]
    interleave(ids, own, other, w_ref)
    for s in range(2):
        for half in range(2):
            x = jnp.concatenate([t[...] for t in tokens[2 * s + half]], 0).astype(F32)
            r1 = lax.rsqrt(jnp.mean(x * x, -1, keepdims=True) + EPSILON)
            n1_ref[s, half * 256 : half * 256 + 256, :] = (x * r1 * gain[...]).astype(BF16)
        proj = jnp.dot(n1_ref[s], w_ref[...], preferred_element_type=F32)
        q = rotated(proj[:, :256], cos, sin).astype(BF16)
        k = rotated(proj[:, 256:512], cos, sin).astype(BF16)
        v = proj[:, 512:].astype(BF16)
        qkv_ref[s, :, :256] = q
        qkv_ref[s, :, 256:512] = k
        qkv_ref[s, :, 512:] = v
        mixed = []
        for h in range(4):
            cols = slice(h * HD, h * HD + HD)
            scores = dot(q[:, cols], k[:, cols], 1, 1) * (HD**-0.5)
            e = jnp.exp(scores - jnp.max(scores, -1, keepdims=True))
            p = (e / jnp.sum(e, -1, keepdims=True)).astype(BF16)
            p_ref[s, h] = p
            mixed.append(dot(p, v[:, cols], 1, 0).astype(BF16))
        out = jnp.concatenate(mixed, 1)
        outs[2 * s][...] = out[:256]
        outs[2 * s + 1][...] = out[256:]


def out_columns(x):
    block = (x % 2) * 2 + x // 2
    return slice(block * 256, block * 256 + 256)


def project_body(ids, tokens, gain, m0, m1, m2, m3, own, other, hidden_ref, n2_ref, wo_ref, mixed_ref):
    interleave(ids, own, other, wo_ref)
    for x, m in enumerate((m0, m1, m2, m3)):
        mixed_ref[:, out_columns(x)] = m[...]
    hidden = tokens[...].astype(F32) + dot(mixed_ref[...], wo_ref[...], 1, 1)
    hidden_ref[...] = hidden
    r2 = lax.rsqrt(jnp.mean(hidden * hidden, -1, keepdims=True) + EPSILON)
    n2_ref[...] = (hidden * r2 * gain[...]).astype(BF16)


def expert_pieces():
    for y in range(4):
        for z in range(4):
            for xh in range(2):
                row = d_block(y, xh, z) * 32
                yield (y * 4 + z, xh), slice(row, row + 32)


def relative_pieces(ids):
    for y in range(4):
        for z in range(4):
            for c in range(2):
                for x in range(4):
                    row = d_block(y, (x // 2) ^ ids[3], z) * 32 + (c ^ ids[2]) * 16
                    rows = pl.ds(pl.multiple_of(row, 16), 16)
                    yield (y * 4 + z, c, x), rows, slice((x % 2) * 256, (x % 2) * 256 + 256)


def expert_body(*refs):
    ids, n2 = refs[0], refs[1:9]
    ct = [r.at[x] for r in refs[9:11] for x in range(4)]
    rank_ref, share_ref, w_ref = refs[11:14]
    z_ref, g_near, g_far, dw_ref = refs[14:18]
    wg, wu, wd, x_s, gz_s, p_s, gx_s = refs[18:]
    e = pl.program_id(0)
    there = pl.ds(pl.multiple_of(e * CAP, 32), CAP)
    for piece, d in expert_pieces():
        wg[d, :] = w_ref[*piece, 0, 0]
        wu[d, :] = w_ref[*piece, 1, 0]
        wd[d, :] = w_ref[*piece, 2, 0]
    shares = []
    slot = lax.broadcasted_iota(jnp.int32, (CAP, 512), 0)
    for s in range(4):
        hit = slot == rank_ref[0, s : s + 1, :]
        share = jnp.sum(jnp.where(hit, share_ref[0, s : s + 1, :], 0.0), 1, keepdims=True)
        shares.append(share)
        p = hit.astype(F32).astype(BF16)
        p_s[s, there, :] = p
        here = slice(s * CAP, s * CAP + CAP)
        x_s[here, :] = (
            dot(p[:, :256], n2[2 * s][...], 1, 0) + dot(p[:, 256:], n2[2 * s + 1][...], 1, 0)
        ).astype(BF16)
        gz_s[here, :] = (
            (dot(p[:, :256], ct[2 * s][...], 1, 0) + dot(p[:, 256:], ct[2 * s + 1][...], 1, 0))
            * share
        ).astype(BF16)
    share = jnp.concatenate(shares, 0)
    a = dot(x_s[...], wg[...], 1, 0)
    b = dot(x_s[...], wu[...], 1, 0)
    sig = 1.0 / (1.0 + jnp.exp(-a))
    sa = a * sig
    u = (sa * b).astype(BF16)
    gu = dot(gz_s[...], wd[...], 1, 0)
    ga = (gu * b * sig * (1.0 + a * (1.0 - sig))).astype(BF16)
    gb = (gu * sa).astype(BF16)
    z = (dot(u, wd[...], 1, 1) * share).astype(BF16)
    z_ref[0] = z
    gx = (dot(ga, wg[...], 1, 1) + dot(gb, wu[...], 1, 1)).astype(BF16)
    for s in range(4):
        here = slice(s * CAP, s * CAP + CAP)
        gx_s[s, there, :] = gx[here]
    for m, (left, right) in enumerate(((x_s, ga), (x_s, gb), (gz_s, u))):
        wg[...] = dot(left[...], right, 0, 0).astype(BF16)
        for piece, rows, cols in relative_pieces(ids):
            dw_ref[*piece, m, 0] = wg[rows, cols]

    @pl.when(e == LOCAL_E - 1)
    def _():
        for s in range(4):
            total = dot(p_s[s], gx_s[s], 0, 0).astype(BF16)
            dst = g_near if s < 2 else g_far
            dst[2 * (s % 2)] = total[:256]
            dst[2 * (s % 2) + 1] = total[256:]


def combine_body(rank_ref, z_ref, z_near, z_far):
    slot = lax.broadcasted_iota(jnp.int32, (CAP, 512), 0)
    for s in range(4):
        hits = [slot == rank_ref[i, s : s + 1, :] for i in range(LOCAL_E)]
        p = jnp.concatenate([h.astype(F32).astype(BF16) for h in hits], 0)
        here = slice(s * CAP, s * CAP + CAP)
        terms = jnp.concatenate([z_ref[i, here, :] for i in range(LOCAL_E)], 0)
        total = dot(p, terms, 0, 0).astype(BF16)
        dst = z_near if s < 2 else z_far
        dst[2 * (s % 2)] = total[:256]
        dst[2 * (s % 2) + 1] = total[256:]


W_BLOCK = (16, 2, 3, 1, 32, 512)


def run_experts(ids, n2, ct, rank, share, weights):
    table = pl.BlockSpec((1, 4, 512), lambda e: (e, 0, 0))
    w_spec = pl.BlockSpec(W_BLOCK, lambda e: (0, 0, 0, e, 0, 0))
    slots = pl.BlockSpec((1, 4 * CAP, 1024), lambda e: (e, 0, 0))
    dw_spec = pl.BlockSpec((16, 2, 4, 3, 1, 16, 256), lambda e: (0, 0, 0, 0, e, 0, 0))
    blocks = shape(4, 256, 1024)
    return pl.pallas_call(
        expert_body,
        grid=(LOCAL_E,),
        out_shape=(shape(LOCAL_E, 4 * CAP, 1024),) + (blocks,) * 2 + (shape(16, 2, 4, 3, LOCAL_E, 16, 256),),
        in_specs=[pl.BlockSpec(memory_space=pltpu.SMEM)] + whole(10) + [table, table, w_spec],
        out_specs=[slots] + whole(2) + [dw_spec],
        scratch_shapes=[
            pltpu.VMEM((1024, 512), BF16),
            pltpu.VMEM((1024, 512), BF16),
            pltpu.VMEM((1024, 512), BF16),
            pltpu.VMEM((4 * CAP, 1024), BF16),
            pltpu.VMEM((4 * CAP, 1024), BF16),
            pltpu.VMEM((4, LOCAL_E * CAP, 512), BF16),
            pltpu.VMEM((4, LOCAL_E * CAP, 1024), BF16),
        ],
        compiler_params=pltpu.CompilerParams(vmem_limit_bytes=VMEM_BYTES),
        cost_estimate=cost(36e9, 60e6),
        name="experts",
    )(ids, *n2, *ct, rank, share, weights)


def hidden_back_body(g0, g1, g2, g3, hidden_ref, ct, gain, wo, gh_ref, ghb_ref, m0, m1, m2, m3, dgain_ref):
    gn2 = g0[...].astype(F32) + g1[...].astype(F32) + g2[...].astype(F32) + g3[...].astype(F32)
    hidden = hidden_ref[...]
    r2 = lax.rsqrt(jnp.mean(hidden * hidden, -1, keepdims=True) + EPSILON)
    w2 = gn2 * gain[...]
    gh = ct[...].astype(F32) + r2 * w2 - hidden * (r2 * r2 * r2) * jnp.mean(w2 * hidden, -1, keepdims=True)
    gh_ref[...] = gh
    ghb = gh.astype(BF16)
    ghb_ref[...] = ghb
    gm = dot(ghb, wo[...], 1, 0).astype(BF16)
    for x, m in enumerate((m0, m1, m2, m3)):
        m[...] = gm[:, out_columns(x)]
    dgain_ref[...] = jnp.sum(gn2 * hidden * r2, 0, keepdims=True)


def attend_back_body(qkv, p_ref, m0, m1, m2, m3, cos_ref, sin_ref, w_ref, z_near, z_far, g_ref, *outs):
    gm_refs = (m0, m1, m2, m3)
    cos, sin = cos_ref[...], -sin_ref[...]
    for s in range(2):
        gm = jnp.concatenate([gm_refs[2 * s][...], gm_refs[2 * s + 1][...]], 0)
        gqs, gks, gvs = [], [], []
        for h in range(4):
            q = qkv[s, :, h * HD : h * HD + HD]
            k = qkv[s, :, 256 + h * HD : 256 + h * HD + HD]
            v = qkv[s, :, 512 + h * HD : 512 + h * HD + HD]
            gmh = gm[:, h * HD : h * HD + HD]
            p = p_ref[s, h].astype(F32)
            gp = dot(gmh, v, 1, 1)
            gs = (p * (gp - jnp.sum(gp * p, -1, keepdims=True))).astype(BF16)
            gqs.append(dot(gs, k, 1, 0) * (HD**-0.5))
            gks.append(dot(gs, q, 0, 0) * (HD**-0.5))
            gvs.append(dot(p_ref[s, h], gmh, 0, 0))
        g_ref[s, :, :256] = rotated(jnp.concatenate(gqs, 1), cos, sin).astype(BF16)
        g_ref[s, :, 256:512] = rotated(jnp.concatenate(gks, 1), cos, sin).astype(BF16)
        g_ref[s, :, 512:] = jnp.concatenate(gvs, 1).astype(BF16)
        part = dot(g_ref[s], w_ref[...], 1, 1).astype(BF16)
        for half in range(2):
            x = 2 * s + half
            outs[x][...] = part[half * 256 : half * 256 + 256]
            outs[4 + x][...] = (z_near[x].astype(F32) + z_far[x].astype(F32)).astype(BF16)


def attend_grad_body(n1, g, w_qkv, gain, grad_ref, dgain_ref):
    qkv = dot(n1[0], g[0], 0, 0) + dot(n1[1], g[1], 0, 0)
    grad_ref[...] = qkv.astype(BF16)
    weighted = qkv * w_qkv[...].astype(F32)
    ones = jnp.ones((8, QKV), F32)
    sums = lax.dot_general(
        ones,
        weighted,
        (((1,), (1,)), ((), ())),
        precision=lax.Precision.HIGHEST,
        preferred_element_type=F32,
    )
    dgain_ref[...] = sums[:1] / gain[...]


def arrange_body(ids, qkv, dgain, dgain_moe, *refs):
    ghb, mixed = refs[:4], refs[4:8]
    near_ref, far_ref, out = refs[8:]
    out[...] = sum(dot(ghb[x][...], mixed[x][...], 0, 0) for x in range(4)).astype(BF16)
    rows = [v[:, i * 128 : i * 128 + 128] for v in (dgain[...], dgain_moe[...]) for i in range(8)]
    gains = jnp.concatenate(rows + [jnp.zeros((16, 128), F32)], 0).astype(BF16)
    for y in range(4):
        for z in range(4):
            near_ref[z, y, :, OWN:] = gains
            far_ref[z, y, :, OWN:] = gains
            for xh in range(2):
                row = d_block(y ^ ids[0], xh, z ^ ids[1]) * 32
                for dst, c in ((near_ref, ids[2]), (far_ref, 1 - ids[2])):
                    rows = pl.ds(pl.multiple_of(row + c * 16, 16), 16)
                    dst[z, y, xh * 16 : xh * 16 + 16, :256] = out[rows, :]
                    dst[z, y, xh * 16 : xh * 16 + 16, 256:OWN] = qkv[rows, :]


def tokens_back_body(gn1, z, p1, p3, tokens, gain, gh, hidden, out_ref, grad_ref):
    total = p1[...].astype(F32) + p3[...].astype(F32)
    out_ref[...] = (hidden[...] + z[...].astype(F32) + total[256:]).astype(BF16)
    x = tokens[...].astype(F32)
    r1 = lax.rsqrt(jnp.mean(x * x, -1, keepdims=True) + EPSILON)
    w1 = (gn1[...].astype(F32) + total[:256]) * gain[...]
    grad_ref[...] = (
        gh[...] + r1 * w1 - x * (r1 * r1 * r1) * jnp.mean(w1 * x, -1, keepdims=True)
    ).astype(BF16)


def rotary_tables(xl):
    frequency = THETA ** (-2.0 * jnp.arange(HD // 2, dtype=F32) / HD)
    place = jnp.arange(512)
    place = ((place // 256) ^ xl) * 256 + place % 256
    angles = place.astype(F32)[:, None] * frequency[None, :]
    cos, sin = jnp.cos(angles), jnp.sin(angles)
    return jnp.concatenate([cos] * 8, 1), jnp.concatenate([-sin, sin] * 4, 1)


def last_send_body(ids, s0, s1, s2, s3, near, far, own_ref, gain_ref, p1, p2, p3, total):
    total[...] = s0[...].astype(F32) + s1[...].astype(F32) + s2[...].astype(F32) + s3[...].astype(F32)
    own = pl.ds(pl.multiple_of(ids[3] * 16, 16), 16)
    other = pl.ds(pl.multiple_of((1 - ids[3]) * 16, 16), 16)
    gains = total[:16, OWN:]
    gain_ref[...] = gains
    own_ref[...] = total[own, :OWN]
    base = 2 * 3 * LOCAL_E * 16
    for x, p in ((1, p1), (2, p2), (3, p3)):
        for m in range(3):
            for e in range(LOCAL_E):
                row = (m * LOCAL_E + e) * 16
                p[row : row + 16, :] = near[0, x, m, e]
                p[base // 2 + row : base // 2 + row + 16, :] = far[1, x, m, e]
        p[base : base + 16, :] = jnp.concatenate([gains, gains], 1).astype(BF16)
    for j in range(4):
        part = total[other, j * 256 : j * 256 + 256]
        p2[base + 16 + j * 16 : base + 32 + j * 16, :] = part.astype(BF16)


def last_body(ids, own, own_gains, g1, g2, g3, near, far, do, dq, dk, dv, gain_ref, *experts):
    c, xh, xl = ids[2], ids[3], ids[4]
    base = 2 * 3 * LOCAL_E * 16
    mine = pl.ds(pl.multiple_of(xh * 256, 256), 256)
    theirs = pl.ds(pl.multiple_of((1 - xh) * 256, 256), 256)
    for j, d in enumerate((do, dq, dk, dv)):
        d[:, mine] = own[:, j * 256 : j * 256 + 256]
        d[:, theirs] = g2[base + 16 + j * 16 : base + 32 + j * 16, :].astype(F32)
    gain_ref[...] = own_gains[...] + sum(g[base : base + 16, :128].astype(F32) for g in (g1, g2, g3))
    for x in range(4):
        for b in range(2):
            owner = (c ^ b) * 4 + (xh ^ (x // 2)) * 2 + (xl ^ (x % 2))
            for m, d in enumerate(experts):
                for e in range(LOCAL_E):
                    row = ((b * 3 + m) * LOCAL_E + e) * 16
                    if x == 0:
                        block = near[0, 0, m, e] if b == 0 else far[1, 0, m, e]
                    else:
                        block = (g1, g2, g3)[x - 1][row : row + 16, :]
                    d[owner * LOCAL_E + e] = block.astype(F32)


def route_rows(routes, route_weights, xl):
    high = lax.reduce_precision(route_weights, 8, 7)
    low = lax.reduce_precision(route_weights - high, 8, 7)
    table = jnp.concatenate([routes.T.astype(F32), high.T, low.T], 0).reshape(24, 2, 256)
    table = jnp.where(xl == 1, table[:, 1], table[:, 0])
    return jnp.pad(table.astype(BF16), ((0, 40), (0, 0))).reshape(16, 1024)


def route_tables(near, far, c, xh, xl):
    tables = jnp.concatenate([near, far], 0).reshape(8, 64, 256)[:, :24].astype(F32)
    tables = tables.reshape(4, 2, 24, 256).transpose(0, 2, 1, 3).reshape(4, 24, 512)
    first = ((c * 4 + xh * 2 + xl) * LOCAL_E).astype(F32)
    names = first + jnp.arange(LOCAL_E, dtype=F32)
    match = tables[None, :, :8, :] == names[:, None, None, None]
    shares = tables[:, 8:16] + tables[:, 16:]
    share = jnp.sum(jnp.where(match, shares[None], 0.0), 2)
    named = jnp.any(match, 2)
    before = (jnp.arange(512)[:, None] <= jnp.arange(512)[None, :]).astype(BF16)
    count = jnp.dot(named.astype(BF16), before, preferred_element_type=F32)
    rank = jnp.where(named, count.astype(jnp.int32) - 1, -1)
    return rank, share


def on_device(
    tokens,
    gain_attn,
    w_query,
    w_key,
    w_value,
    w_out,
    gain_moe,
    w_gate,
    w_up,
    w_down,
    routes,
    route_weights,
    cotangent,
):
    y, xh, z, c, xl = (lax.axis_index(a) for a in ("y", "xh", "z", "c", "xl"))
    ids = jnp.stack([y, z, c, xh, xl]).astype(jnp.int32)
    gain_attn = gain_attn.reshape(1, 1024)
    gain_moe = gain_moe.reshape(1, 1024)

    heads = jnp.stack([w_query, w_key, w_value], 1).reshape(16, 3, 2, 256)
    heads = flip(heads, 2, xh)
    w_o = w_out.T.reshape(16, 2, 256)
    for_same, for_other = flip(w_o, 1, xh).reshape(16, 512), flip(w_o, 1, 1 - xh).reshape(16, 512)
    for_2 = jnp.concatenate([for_other, heads[:, :, 1].reshape(16, 768)], 1)
    local = jnp.stack([w_gate, w_up, jnp.swapaxes(w_down, 1, 2)])
    local = local.reshape(3, 2, 2, 2, LOCAL_E, 16, 256)
    local = flip(flip(flip(local, 1, c), 2, xh), 3, xl).transpose(1, 2, 3, 0, 4, 5, 6)
    local = local.reshape(2, 4, 3, LOCAL_E, 16, 256)
    near, far = local[0], local[1]

    got_2, got_1, got_3 = together(swap_x(for_2, 2), swap_x(for_same, 1), swap_x(for_other, 3))
    far = swap_c(far)
    here = jnp.concatenate([for_same, got_1, heads[:, :, 0].reshape(16, 768)], 1)
    there = jnp.concatenate([got_2[:, :512], got_3, got_2[:, 512:]], 1)
    rows = flip(jnp.stack([here, there]), 0, xh).reshape(32, PACKED)
    both = [flip(jnp.stack([near[x], far[x]], 2), 2, c) for x in range(4)]
    sent = jnp.concatenate([tokens, route_rows(routes, route_weights, xl)], 0)
    rows, sent = together(rows, sent)

    moved = together(
        *[swap_4(rows, "z", k) for k in (1, 2, 3)], *[swap_x(both[x], x) for x in (1, 2, 3)]
    )
    owned = [both[0], *moved[3:]]
    owned = jnp.stack([jnp.concatenate(owned[:2], -1), jnp.concatenate(owned[2:], -1)])
    owned = flip(owned, 0, xh).reshape(2, 3, LOCAL_E, 32, 512)
    experts = lax.all_gather(owned, ("y", "z"), axis=0)
    zs_o = jnp.stack([rows[:, :OUT], *[m[:, :OUT] for m in moved[:3]]])
    zs = jnp.stack([rows[:, OUT:], *[m[:, OUT:] for m in moved[:3]]])
    zs, zs_o, sent, owned = together(zs, zs_o, sent, owned)

    *moved, t1, t3, cos, sin = together(
        *[swap_4(zs, "y", k) for k in (1, 2, 3)],
        swap_x(sent, 1),
        swap_x(sent, 3),
        *rotary_tables(xl),
    )
    half = kernel_call(assemble_body, [ids, zs, *moved], (shape(512, QKV),), "assemble", smem=1)
    half, zs_o, sent, t1, t3 = together(half[0], zs_o, sent, t1, t3)
    moved_o = [swap_4(zs_o, "y", k) for k in (1, 2, 3)]
    other_half, t2a, t2b = together(swap_c(half), swap_x(t3[:144], 1), swap_x(t1[144:], 3))
    blocks = [sent, t1, t2a, t2b, t3]
    near = jnp.stack([t[-16:] for t in (sent, t1, t2b, t3)])
    other_half, near, cot = together(other_half, near, cotangent)
    ct_1, ct_3 = swap_x(cot, 1), swap_x(cot, 3)

    n1, qkv, w_qkv, probs, *mixed = kernel_call(
        attend_body,
        [ids, *blocks, gain_attn, half, other_half, cos, sin],
        (shape(2, 512, 1024), shape(2, 512, QKV), shape(1024, QKV), shape(2, 4, 512, 512))
        + (shape(256, 256),) * 4,
        "attend",
        smem=1,
        flops=8e9,
    )
    *mixed, ct_1, ct_3, near, cot, moved_o[0], moved_o[1], moved_o[2] = together(
        *mixed, ct_1, ct_3, near, cot, *moved_o
    )
    half = kernel_call(assemble_body, [ids, zs_o, *moved_o], (shape(512, OUT),), "assemble", smem=1)
    other_half, *moved = together(
        swap_c(half[0]), *[swap_x(mixed[x], x) for x in (1, 2, 3)]
    )
    ct_2 = [swap_x(ct_3[:128], 1), swap_x(ct_1[128:], 3)]
    hidden, n2, w_o_full = kernel_call(
        project_body,
        [ids, tokens, gain_moe, mixed[0], *moved, half[0], other_half],
        (shape(256, 1024, dtype=F32), shape(256, 1024), shape(1024, OUT)),
        "project",
        scratch=[pltpu.VMEM((256, OUT), BF16)],
        smem=1,
    )
    n2, *ct_2 = together(n2, *ct_2)
    ct_near = jnp.stack([cot, ct_1, jnp.concatenate(ct_2, 0), ct_3])
    n2_1, n2_3, n2_far, far = together(swap_x(n2, 1), swap_x(n2, 3), swap_c(n2), swap_c(near))
    n2_1, n2_3, ct_near = together(n2_1, n2_3, ct_near)
    rank, share = route_tables(near, far, c, xh, xl)
    n2_2a, n2_2b, n2_far_1, n2_far_3, ct_far, rank, share = together(
        swap_x(n2_3[:128], 1),
        swap_x(n2_1[128:], 3),
        swap_c(n2_1),
        swap_c(n2_3),
        swap_c(ct_near),
        rank,
        share,
    )
    n2_2 = jnp.concatenate([n2_2a, n2_2b], 0)
    n2_all = [n2, n2_1, n2_2, n2_3, n2_far, n2_far_1, swap_c(n2_2), n2_far_3]
    ct_all = [ct_near, ct_far]
    z_slots, g_near, g_far, grads = run_experts(ids, n2_all, ct_all, rank, share, experts)
    reduced = lax.psum_scatter(grads, ("y", "z"), scatter_dimension=0)
    g_far = swap_c(g_far)
    sum_1, sum_3 = (add(g_near[x], g_far[x]).astype(BF16) for x in (1, 3))
    sum_1, sum_3, g_near, g_far, z_slots = together(sum_1, sum_3, g_near, g_far, z_slots)
    sum_0, sum_2 = (add(g_near[x], g_far[x]).astype(BF16) for x in (0, 2))
    g_sums = [sum_0, sum_1, sum_2, sum_3]
    z_near, z_far = kernel_call(
        combine_body, [rank, z_slots], (shape(4, 256, 1024),) * 2, "combine", flops=4e9
    )
    gn2_1, gn2_3, gn2_2, z_near, z_far = together(
        swap_x(g_sums[1], 1), swap_x(g_sums[3], 3), swap_x(g_sums[2], 2), z_near, z_far
    )
    z_far = swap_c(z_far)
    gn2 = [g_sums[0], gn2_1, gn2_2, gn2_3]
    gh, ghb, *gm, dgain_moe = kernel_call(
        hidden_back_body,
        [*gn2, hidden, cotangent, gain_moe, w_o_full],
        (shape(256, 1024, dtype=F32), shape(256, 1024))
        + (shape(256, 256),) * 4
        + (shape(1, 1024, dtype=F32),),
        "hidden_back",
    )
    moved = together(*[swap_x(gm[x], x) for x in (1, 2, 3)])
    gm = [gm[0], *moved]
    ghb, *gm = together(ghb, *gm)
    ghb = [ghb, swap_x(ghb, 1), swap_x(ghb, 2), swap_x(ghb, 3)]
    g, *parts = kernel_call(
        attend_back_body,
        [qkv, probs, *gm, cos, sin, w_qkv, z_near, z_far],
        (shape(2, 512, QKV),) + (shape(256, 1024),) * 8,
        "attend_back",
        flops=10e9,
    )
    g, *parts = together(g, *parts)
    gn1, z_sums = parts[:4], parts[4:]
    via_1, via_3 = swap_x(gn1[2], 1), swap_x(z_sums[2], 3)
    qkv_grad, dgain_attn = kernel_call(
        attend_grad_body,
        [n1, g, w_qkv, gain_attn],
        (shape(1024, QKV), shape(1, 1024, dtype=F32)),
        "attend_grad",
        flops=4e9,
    )
    qkv_grad, *ghb[1:] = together(qkv_grad, *ghb[1:])
    near, far = kernel_call(
        arrange_body,
        [ids, qkv_grad, dgain_attn, dgain_moe, *ghb, *mixed],
        (shape(4, 4, 32, OWN + SPARE),) * 2,
        "arrange",
        scratch=[pltpu.VMEM((1024, 256), BF16)],
        smem=1,
    )
    sums = add(near, swap_c(far)).astype(BF16)
    moved = [swap_4(sums[k], "z", k) for k in (1, 2, 3)]
    moved[0], via_1, via_3 = together(moved[0], via_1, via_3)
    part_1 = jnp.concatenate([gn1[1], add(z_sums[1], via_3).astype(BF16)], 0)
    part_3 = jnp.concatenate([add(gn1[3], via_1).astype(BF16), z_sums[3]], 0)
    part_1, part_3 = swap_x(part_1, 1), swap_x(part_3, 3)
    sums = add(sums[0], *moved).astype(BF16)
    sums, reduced = together(sums, reduced)
    *moved, back_far = together(*[swap_4(sums[k], "y", k) for k in (1, 2, 3)], swap_c(reduced))
    sent_rows = 2 * 3 * LOCAL_E * 16
    own, own_gains, *sent = kernel_call(
        last_send_body,
        [ids, sums[0], *moved, reduced, back_far],
        (
            shape(16, OWN, dtype=F32),
            shape(16, 128, dtype=F32),
            shape(sent_rows + 16, 256),
            shape(sent_rows + 80, 256),
            shape(sent_rows + 16, 256),
        ),
        "last_send",
        scratch=[pltpu.VMEM((32, OWN + SPARE), F32)],
        smem=1,
    )
    *sent, part_1, part_3 = together(*sent, part_1, part_3)
    output, grad_tokens = kernel_call(
        tokens_back_body,
        [gn1[0], z_sums[0], part_1, part_3, tokens, gain_attn, gh, hidden],
        (shape(256, 1024),) * 2,
        "tokens_back",
    )
    *got, output, grad_tokens = together(
        *[swap_x(sent[x - 1], x) for x in (1, 2, 3)], output, grad_tokens
    )
    d_out, d_query, d_key, d_value, gains, d_gate, d_up, d_down = kernel_call(
        last_body,
        [ids, own, own_gains, *got, reduced, back_far],
        (shape(16, 512, dtype=F32),) * 4
        + (shape(16, 128, dtype=F32),)
        + (shape(8 * LOCAL_E, 16, 256, dtype=F32),) * 3,
        "last",
        smem=1,
    )
    gains = gains.reshape(2, 1024)
    return (
        output,
        grad_tokens,
        gains[0],
        d_query,
        d_key,
        d_value,
        d_out.T,
        gains[1],
        d_gate,
        d_up,
        jnp.swapaxes(d_down, 1, 2),
    )


def solution(mesh):
    split = Mesh(mesh.devices.reshape(4, 2, 4, 2, 2), ("y", "xh", "z", "c", "xl"))
    dp = ("y", "xh", "z", "c")
    rows = P((*dp, "xl"), None)
    outs = (
        rows,
        rows,
        P(),
        P(dp, "xl"),
        P(dp, "xl"),
        P(dp, "xl"),
        P("xl", dp),
        P(),
        P(None, dp, "xl"),
        P(None, dp, "xl"),
        P(None, "xl", dp),
    )
    ins = (
        rows,
        P(),
        P(dp, "xl"),
        P(dp, "xl"),
        P(dp, "xl"),
        P("xl", dp),
        P(),
        P(None, dp, "xl"),
        P(None, dp, "xl"),
        P(None, "xl", dp),
        P(dp, None),
        P(dp, None),
        rows,
    )
    return jax.shard_map(on_device, mesh=split, in_specs=ins, out_specs=outs, check_vma=False)
```
